32 devices in a mesh: wide: 8 (over y, x, core), narrow: 4 (over z).
Axes of the slice: x: 2, y: 2, z: 4, core: 2. Of those that a mesh axis runs over, the one named last changes fastest.
Arguments:
- patches: bfloat16 [16384, 192], P(('wide', 'narrow')), may hold values from -6 to 6
- var_ids: int32 [48], replicated, may hold values from 0 to 47, each once
- segment_ids: int32 [32, 512], P(('wide', 'narrow')), may hold values from 0 to 3, never falling along the last dimension, each value on 1 to 256 neighbouring positions
- pad_mask: int32 [32, 512], P(('wide', 'narrow')), may hold values 0 or 1
- embed_weight: bfloat16 [192, 1024], P(None, 'narrow'), may hold values from -3 to 3
- var_embed: bfloat16 [48, 1024], P(None, 'narrow'), may hold values from -3 to 3
- agg_query: bfloat16 [1024], P('narrow'), may hold values from -6 to 6
- key_weight: bfloat16 [1024, 1024], P('narrow'), may hold values from -0.1875 to 0.1875
- value_weight: bfloat16 [1024, 1024], P('narrow'), may hold values from -0.1875 to 0.1875
- agg_out_weight: bfloat16 [1024, 1024], P('narrow'), may hold values from -0.75 to 0.75
- agg_out_bias: bfloat16 [1024], P('narrow'), may hold values from -3 to 3
- norm_one_gain: bfloat16 [1024], P('narrow'), may hold values from 0.5 to 1.5
- norm_one_bias: bfloat16 [1024], P('narrow'), may hold values from -2 to 2
- qkv_weight: bfloat16 [1024, 3072], P('narrow'), may hold values from -0.1875 to 0.1875
- attn_out_weight: bfloat16 [1024, 1024], P('narrow'), may hold values from -1.5 to 1.5
- attn_out_bias: bfloat16 [1024], P('narrow'), may hold values from -2 to 2
- norm_two_gain: bfloat16 [1024], P('narrow'), may hold values from 0.5 to 1.5
- norm_two_bias: bfloat16 [1024], P('narrow'), may hold values from -2 to 2
- mlp_in_weight: bfloat16 [1024, 4096], P('narrow'), may hold values from -0.1875 to 0.1875
- mlp_in_bias: bfloat16 [4096], P('narrow'), may hold values from -3 to 3
- mlp_out_weight: bfloat16 [4096, 1024], P('narrow'), may hold values from -0.125 to 0.125
- mlp_out_bias: bfloat16 [1024], P('narrow'), may hold values from -2 to 2
- cotangent: bfloat16 [16384, 1024], P(('wide', 'narrow')), may hold values from -16 to 16
Outputs:
- block_out: bfloat16 [16384, 1024], P(('wide', 'narrow'))
- patches_grad: float32 [16384, 192], P(('wide', 'narrow'))
- embed_weight_grad: float32 [192, 1024], P(None, 'narrow')
- var_embed_grad: float32 [48, 1024], P(None, 'narrow')
- agg_query_grad: float32 [1024], P('narrow')
- key_weight_grad: float32 [1024, 1024], P('narrow')
- value_weight_grad: float32 [1024, 1024], P('narrow')
- agg_out_weight_grad: float32 [1024, 1024], P('narrow')
- agg_out_bias_grad: float32 [1024], P('narrow')
- norm_one_gain_grad: float32 [1024], P('narrow')
- norm_one_bias_grad: float32 [1024], P('narrow')
- qkv_weight_grad: float32 [1024, 3072], P('narrow')
- attn_out_weight_grad: float32 [1024, 1024], P('narrow')
- attn_out_bias_grad: float32 [1024], P('narrow')
- norm_two_gain_grad: float32 [1024], P('narrow')
- norm_two_bias_grad: float32 [1024], P('narrow')
- mlp_in_weight_grad: float32 [1024, 4096], P('narrow')
- mlp_in_bias_grad: float32 [4096], P('narrow')
- mlp_out_weight_grad: float32 [4096, 1024], P('narrow')
- mlp_out_bias_grad: float32 [1024], P('narrow')
The draws below stay inside these ranges and needn't reach their ends.
Inputs may be any that keep to these rules, and one draw needn't show every extreme that they name: `var_ids`: each of the 48 variables stands once. `segment_ids`: along each row the segment number never falls; a segment holds at most half of the 512 positions.
All inputs are finite; a program needn't handle non-finite values. No bound on the sum of `pad_mask` on one device may be relied on, other than what follows from the above.
Results may differ from the reference program's by a relative error of at most 0.02.
Values may be sent and summed in bfloat16 or wider, within the bound.
No kernel may reach another device: no remote copies, remote signals or barrier semaphores. Data moves between devices by JAX's collectives and lax.ppermute only.
A program may use at most 256 MiB of HBM per device.

```python
import math
import jax
import jax.numpy as jnp
import numpy as np
from jax import lax

D = 1024
FF = 4096
HEADS = 16
HEAD_DIM = 64
VARS = 48
PIX = 4
TOK_DEV = 512
SEGS = 4
N_BATCH = 32
TOKENS = 16384


def draw_cotangent(key, part):
    key = jax.random.fold_in(key, 17)
    where_row = jnp.arange(TOKENS, dtype=jnp.float32) / (TOKENS - 1)
    noise_base = jnp.clip(jax.random.normal(key, (TOKENS, D), jnp.float32), -4.0, 4.0)
    growth = 3.0 ** where_row
    return (noise_base * growth[:, None]).astype(jnp.bfloat16)


def place_ends(values, key, smallest, high):
    dims = values.shape
    spot = [jax.random.randint(jax.random.fold_in(key, axis), (), 0, dims[axis]) for axis in range(len(dims))]
    values = values.at[tuple(spot)].set(smallest)
    longest = dims.index(max(dims))
    spot[longest] = (spot[longest] + 1) % dims[longest]
    return values.at[tuple(spot)].set(high)


def block_scale(stream_key, shape, pieces, low, largest):
    level = 1.0
    for dim, blocks in pieces:
        draws = jax.random.uniform(jax.random.fold_in(jax.random.fold_in(stream_key, 6), dim), (blocks,), jnp.float32, low / len(pieces), largest / len(pieces))
        level = level * jnp.repeat(jnp.exp(draws), shape[dim] // blocks).reshape((-1,) + (1,) * (len(shape) - 1 - dim))
    return level


def length_profile(number_of, total, limit, skew):
    weights = [(1 << 20) // math.isqrt(rank ** skew) + 1 for rank in range(2, number_of + 1)]
    surplus, holding = total - limit - (number_of - 1), [1] * (number_of - 1)
    while surplus > 0:
        free = [i for i in range(number_of - 1) if holding[i] < limit]
        whole, left = sum([weights[i] for i in free]), surplus
        for i in free:
            addition = min(limit - holding[i], max(1, left * weights[i] // whole), surplus)
            holding[i] = holding[i] + addition
            surplus = surplus - addition
    return np.array([limit] + holding)


def ragged_sizes(key, count, total, limit, skew):
    if count == 2:
        one = jax.random.randint(key, (), max(1, total - limit), min(limit, total - 1) + 1)
        return jnp.stack([one, total - one])
    sizes = jnp.asarray(length_profile(count, total, limit, skew), jnp.int32)
    pairs = (count - 1) // 2
    giver, receiver = sizes[1:1 + 2 * pairs:2], sizes[2:2 + 2 * pairs:2]
    room = jnp.minimum(giver - 1, limit - receiver)
    shifted = jax.random.randint(jax.random.fold_in(key, 1), (pairs,), 0, 1 << 20) % (room + 1)
    sizes = sizes.at[1:1 + 2 * pairs:2].set(giver - shifted).at[2:2 + 2 * pairs:2].set(receiver + shifted)
    return sizes[jax.random.permutation(jax.random.fold_in(key, 2), count)]


def bell_draw(own_key, dims, spread, limit, pieces=(), kind=jnp.bfloat16):
    level = block_scale(own_key, dims, pieces, -0.22, 0.18) if pieces else 1.0
    entries = jax.random.normal(own_key, dims, jnp.float32) * spread * level
    return jnp.minimum(jnp.maximum(entries, -limit), limit).astype(kind)


def setup_inputs(seed: int = 0) -> dict:
    key_of = jax.random.split(jax.random.key(seed), 24)
    patches = bell_draw(key_of[0], (TOKENS, VARS * PIX), 1.0, 6.0, ((0, 32),))
    var_ids = jax.random.permutation(key_of[1], VARS).astype(jnp.int32)
    segment_ids = jax.vmap(lambda own: jnp.searchsorted(jnp.cumsum(ragged_sizes(own, SEGS, TOK_DEV, TOK_DEV // 2, 2)), jnp.arange(TOK_DEV), side="right"))(jax.random.split(key_of[2], N_BATCH)).reshape((N_BATCH, TOK_DEV)).astype(jnp.int32)
    pad_mask = place_ends((jax.random.randint(key_of[3], (N_BATCH, TOK_DEV), 0, 8) < 7).astype(jnp.int32), jax.random.fold_in(key_of[3], 1), 0, 1)
    embed_weight = bell_draw(key_of[4], (VARS * PIX, D), PIX ** -0.5, 3.0, ((1, 4),))
    var_embed = bell_draw(key_of[5], (VARS, D), 0.5, 3.0, ((1, 4),))
    agg_query = bell_draw(key_of[6], (D,), 1.0, 6.0, ((0, 4),))
    key_weight = bell_draw(key_of[7], (D, D), D ** -0.5, 0.1875, ((0, 4),))
    value_weight = bell_draw(key_of[8], (D, D), D ** -0.5, 0.1875, ((0, 4),))
    agg_out_weight = bell_draw(key_of[9], (D, D), (D // 16) ** -0.5, 0.75, ((0, 4),))
    agg_out_bias = bell_draw(key_of[10], (D,), 0.5, 3.0, ((0, 4),))
    norm_one_gain = jnp.clip(1.0 + 0.1 * jax.random.normal(key_of[11], (D,), jnp.float32), 0.5, 1.5).astype(jnp.bfloat16)
    norm_one_bias = bell_draw(key_of[12], (D,), 0.3, 2.0, ((0, 4),))
    qkv_weight = bell_draw(key_of[13], (D, 3 * D), D ** -0.5, 0.1875, ((0, 4),))
    attn_out_weight = bell_draw(key_of[14], (D, D), (D // 64) ** -0.5, 1.5, ((0, 4),))
    attn_out_bias = bell_draw(key_of[15], (D,), 0.3, 2.0, ((0, 4),))
    norm_two_gain = jnp.clip(1.0 + 0.1 * jax.random.normal(key_of[16], (D,), jnp.float32), 0.5, 1.5).astype(jnp.bfloat16)
    norm_two_bias = bell_draw(key_of[17], (D,), 0.3, 2.0, ((0, 4),))
    mlp_in_weight = bell_draw(key_of[18], (D, FF), D ** -0.5, 0.1875, ((0, 4),))
    mlp_in_bias = bell_draw(key_of[19], (FF,), 0.5, 3.0, ((0, 4),))
    mlp_out_weight = bell_draw(key_of[20], (FF, D), (FF // 2) ** -0.5, 0.125, ((0, 4),))
    mlp_out_bias = bell_draw(key_of[21], (D,), 0.3, 2.0, ((0, 4),))
    cotangent = draw_cotangent(jax.random.fold_in(key_of[23], 71), 0)
    return dict(patches=patches, var_ids=var_ids, segment_ids=segment_ids, pad_mask=pad_mask, embed_weight=embed_weight, var_embed=var_embed, agg_query=agg_query, key_weight=key_weight, value_weight=value_weight, agg_out_weight=agg_out_weight, agg_out_bias=agg_out_bias, norm_one_gain=norm_one_gain, norm_one_bias=norm_one_bias, qkv_weight=qkv_weight, attn_out_weight=attn_out_weight, attn_out_bias=attn_out_bias, norm_two_gain=norm_two_gain, norm_two_bias=norm_two_bias, mlp_in_weight=mlp_in_weight, mlp_in_bias=mlp_in_bias, mlp_out_weight=mlp_out_weight, mlp_out_bias=mlp_out_bias, cotangent=cotangent)


@jax.custom_vjp
def low(v):
    return lax.optimization_barrier(v.astype(jnp.bfloat16)).astype(jnp.float32)

@jax.custom_vjp
def low_back(v):
    return v

def low_keep(v):
    return (low(v), None)

def low_pass(kept, grad):
    return (grad,)

def back_keep(v):
    return (v, None)

def back_low(kept, grad):
    return (low(grad),)
low.defvjp(low_keep, low_pass)
low_back.defvjp(back_keep, back_low)
highest = lax.Precision.HIGHEST
norm_eps = 1e-06
masked_out = -1e+30

def layer_norm(values, gain_row, shift_row):
    average = lax.optimization_barrier(jnp.mean(values, axis=-1, keepdims=True))
    centered = values - average
    variance = lax.optimization_barrier(jnp.mean(centered * centered, axis=-1, keepdims=True))
    return centered * lax.rsqrt(variance + norm_eps) * gain_row + shift_row

def soft_max(scores, axis_at):
    biggest = lax.optimization_barrier(jnp.max(scores, axis=axis_at, keepdims=True))
    raised = jnp.exp(scores - biggest)
    return raised / lax.optimization_barrier(jnp.sum(raised, axis=axis_at, keepdims=True))

def forward(params, pixel_rows, chooser, allowed):
    embed_weight, var_embed, agg_query, key_weight, value_weight, agg_out_weight, agg_out_bias, norm_one_gain, norm_one_bias, qkv_weight, attn_out_weight, attn_out_bias, norm_two_gain, norm_two_bias, mlp_in_weight, mlp_in_bias, mlp_out_weight, mlp_out_bias = params
    row_count = pixel_rows.shape[0]
    scale_by = HEAD_DIM ** (-0.5)
    embed_table = jnp.dot(chooser, embed_weight.reshape(VARS, PIX * D), precision=highest).reshape(VARS, PIX, D)
    offsets = jnp.dot(chooser, var_embed, precision=highest)
    pixels = pixel_rows.reshape(row_count, VARS, PIX)
    tokens = jnp.einsum('tcj,cjd->tcd', pixels, embed_table, precision=highest) + offsets[None]
    tokens = low_back(low(tokens))
    key_query = low(lax.optimization_barrier(jnp.sum(key_weight.reshape(D, HEADS, HEAD_DIM) * agg_query.reshape(1, HEADS, HEAD_DIM), axis=-1)))
    var_scores = low_back(jnp.einsum('tcd,dh->tch', tokens, key_query, precision=highest) * scale_by)
    var_probs = low(soft_max(var_scores, 1))
    pooled = low_back(low(jnp.einsum('tch,tcd->thd', var_probs, tokens, precision=highest)))
    merged = jnp.einsum('thd,dhe->the', pooled, value_weight.reshape(D, HEADS, HEAD_DIM), precision=highest)
    merged = low_back(low(merged.reshape(row_count, D)))
    patch_state = low_back(jnp.dot(merged, agg_out_weight, precision=highest) + agg_out_bias)
    normed = low(layer_norm(patch_state, norm_one_gain, norm_one_bias))
    project = low_back(low(jnp.dot(normed, qkv_weight, precision=highest)))
    queries = project[:, :D].reshape(row_count, HEADS, HEAD_DIM)
    keys_all = project[:, D:2 * D].reshape(row_count, HEADS, HEAD_DIM)
    values_all = project[:, 2 * D:].reshape(row_count, HEADS, HEAD_DIM)
    scores = low_back(jnp.einsum('qhe,khe->hqk', queries, keys_all, precision=highest) * scale_by)
    prob_table = low(soft_max(jnp.where(allowed[None], scores, masked_out), 2))
    attended = jnp.einsum('hqk,khe->qhe', prob_table, values_all, precision=highest).reshape(row_count, D)
    attended = low_back(low(attended))
    residual = patch_state + low_back(jnp.dot(attended, attn_out_weight, precision=highest) + attn_out_bias)
    normed_two = low(layer_norm(residual, norm_two_gain, norm_two_bias))
    hidden_pre = low_back(jnp.dot(normed_two, mlp_in_weight, precision=highest) + mlp_in_bias)
    hidden = low(jax.nn.gelu(hidden_pre, approximate=False))
    return residual + low_back(jnp.dot(hidden, mlp_out_weight, precision=highest) + mlp_out_bias)

def reference(patches, var_ids, segment_ids, pad_mask, embed_weight, var_embed, agg_query, key_weight, value_weight, agg_out_weight, agg_out_bias, norm_one_gain, norm_one_bias, qkv_weight, attn_out_weight, attn_out_bias, norm_two_gain, norm_two_bias, mlp_in_weight, mlp_in_bias, mlp_out_weight, mlp_out_bias, cotangent):
    weights = tuple((array_in.astype(jnp.float32) for array_in in (embed_weight, var_embed, agg_query, key_weight, value_weight, agg_out_weight, agg_out_bias, norm_one_gain, norm_one_bias, qkv_weight, attn_out_weight, attn_out_bias, norm_two_gain, norm_two_bias, mlp_in_weight, mlp_in_bias, mlp_out_weight, mlp_out_bias)))
    chooser = (var_ids[:, None] == jnp.arange(VARS, dtype=jnp.int32)[None, :]).astype(jnp.float32)
    pixel_blocks = patches.astype(jnp.float32).reshape(N_BATCH, TOK_DEV, VARS * PIX)
    cot_blocks = cotangent.astype(jnp.float32).reshape(N_BATCH, TOK_DEV, D)
    positions = jnp.arange(TOK_DEV, dtype=jnp.int32)
    diagonal = positions[:, None] == positions[None, :]

    def one_block(totals, block_in):
        pixel_rows, segments, padding, cot_rows = block_in
        allowed = (segments[:, None] == segments[None, :]) & ((padding[None, :] == 1) | diagonal)

        def apply_layer(params, inputs):
            return forward(params, inputs, chooser, allowed)
        result, pullback = jax.vjp(apply_layer, weights, pixel_rows)
        grad_params, grad_pixels = pullback(cot_rows)
        totals = jax.tree.map(jnp.add, totals, grad_params)
        return (totals, (result.astype(jnp.bfloat16), grad_pixels))
    zeros_init = jax.tree.map(jnp.zeros_like, weights)
    totals, (outputs, grad_pixels) = lax.scan(one_block, zeros_init, (pixel_blocks, segment_ids, pad_mask, cot_blocks))
    return (outputs.reshape(TOKENS, D), grad_pixels.reshape(TOKENS, VARS * PIX), totals[0], totals[1], totals[2], totals[3], totals[4], totals[5], totals[6], totals[7], totals[8], totals[9], totals[10], totals[11], totals[12], totals[13], totals[14], totals[15], totals[16], totals[17])
```

```python
import functools

import jax
import jax.numpy as jnp
import numpy as np
from jax import lax
from jax.experimental import pallas as pl
from jax.experimental.pallas import tpu as pltpu
from jax.sharding import PartitionSpec as P

D = 1024
HEADS = 16
HEAD_DIM = 64
VARS = 48
PIX = 4
PATCH_COLS = VARS * PIX
COLS = 256
PAIRS = HEADS // 2
SUB = 8

norm_eps = 1e-06
masked_out = -1e30
scale_by = HEAD_DIM ** (-0.5)
f32 = jnp.float32
bf16 = jnp.bfloat16
MB = 1 << 20


def dot(a, b):
    return jnp.dot(a, b, preferred_element_type=f32)


def dot_nt(a, b):
    return lax.dot_general(a, b, (((1,), (1,)), ((), ())), preferred_element_type=f32)


def dot_tn(a, b):
    return lax.dot_general(a, b, (((0,), (0,)), ((), ())), preferred_element_type=f32)


def split_two(a):
    high = a.astype(bf16)
    return high, (a - high.astype(f32)).astype(bf16)


def swap_wide(a, bits):
    size = lax.axis_size("wide")
    return lax.ppermute(a, "wide", [(i, i ^ bits) for i in range(size)])


def turn_narrow(a, by):
    size = lax.axis_size("narrow")
    return lax.ppermute(a, "narrow", [(i, (i + by) % size) for i in range(size)])


def take(a, at, axis):
    return lax.dynamic_index_in_dim(a, at, axis, keepdims=False)


def spread_plane(piece):
    half = piece.shape[-2] // 2
    from_x = swap_wide(piece, 2)
    from_y = swap_wide(piece, 4)
    low = swap_wide(from_x[..., :half, :], 4)
    high = swap_wide(from_y[..., half:, :], 2)
    here = [(0, 0, piece), (2, 0, from_x), (4, 0, from_y), (6, 0, low), (6, half, high)]
    there = [(bits | 1, start, swap_wide(part, 1)) for bits, start, part in here]
    return here + there


def assemble_kernel(layout, n_shards, n_parts, spot, *refs):
    shards = refs[:n_shards]
    parts = refs[n_shards : n_shards + n_parts]
    fulls = refs[n_shards + n_parts : 2 * n_shards + n_parts]
    sems = refs[-1]
    z, p = spot[0], spot[1]
    copies = []

    def start(src, dst):
        copy = pltpu.make_async_copy(src, dst, sems.at[len(copies)])
        copy.start()
        copies.append(copy)

    for shard, full in zip(shards, fulls):
        rows = shard.shape[0]
        start(shard, full.at[pl.ds(pl.multiple_of(z * rows, rows), rows), :])
    for (bits, first), part in zip(layout, parts):
        count = part.shape[1]
        for turn in range(1, 4):
            origin = lax.rem(z - turn + 4, 4)
            left = 0
            for full in fulls:
                rows, width = full.shape[0] // 4, full.shape[1]
                at = origin * rows + (p ^ bits) * (rows // SUB) + first
                start(
                    part.at[turn - 1, :, left : left + width],
                    full.at[pl.ds(pl.multiple_of(at, 16), count), :],
                )
                left += width
    for copy in copies:
        copy.wait()


def assemble(shards, parts, spot):
    layout = tuple((bits, first) for bits, first, _ in parts)
    arrays = [part for _, _, part in parts]
    n_copies = len(shards) * (1 + 3 * len(parts))
    return pl.pallas_call(
        functools.partial(assemble_kernel, layout, len(shards), len(parts)),
        out_shape=[jax.ShapeDtypeStruct((4 * s.shape[0], s.shape[1]), s.dtype) for s in shards],
        in_specs=[pl.BlockSpec(memory_space=pltpu.SMEM)]
        + [pl.BlockSpec(memory_space=pl.ANY)] * (len(shards) + len(arrays)),
        out_specs=[pl.BlockSpec(memory_space=pltpu.VMEM)] * len(shards),
        scratch_shapes=[pltpu.SemaphoreType.DMA((n_copies,))],
        compiler_params=pltpu.CompilerParams(vmem_limit_bytes=40 * MB),
        cost_estimate=pl.CostEstimate(
            flops=0, transcendentals=0, bytes_accessed=sum(16 * s.size for s in shards)
        ),
        name="assemble",
    )(spot, *shards, *arrays)


def pieces_of(shards, p):
    return jnp.concatenate(
        [
            lax.dynamic_slice_in_dim(s, p * (s.shape[0] // SUB), s.shape[0] // SUB, 0)
            for s in shards
        ],
        axis=1,
    )


def gather(shards, p, spot):
    piece = pieces_of(shards, p)
    bundle = jnp.stack([turn_narrow(piece, turn) for turn in (1, 2, 3)])
    return assemble(shards, spread_plane(bundle), spot)


def add_two(a, b):
    return (a.astype(f32) + b.astype(f32)).astype(bf16)


def reduce_plane(grad, x, y, z):
    sent_x = take(grad[:, :, :, 0], 1 - x, 2)
    sent_y = take(grad[:, :, :, 1], 1 - y, 1)
    got_x = swap_wide(sent_x, 2)
    got_y = swap_wide(sent_y, 4)
    first = add_two(take(grad[:, :, :, 0], x, 2), got_x)
    second = add_two(take(grad[:, :, :, 1], y, 1), got_y)
    got_first = swap_wide(take(first, 1 - y, 1), 4)
    got_second = swap_wide(take(second, 1 - x, 1), 2)
    both = jnp.stack(
        [add_two(take(first, y, 1), got_first), add_two(take(second, x, 1), got_second)], axis=1
    )
    total = take(both, z, 0).astype(f32)
    for turn in (1, 2, 3):
        total = total + turn_narrow(take(both, (z + turn) % 4, 0), turn).astype(f32)
    return across_groups(total.astype(bf16))


def across_groups(a):
    groups = lax.axis_size("wide") // SUB
    if groups == 1:
        return a
    members = [[g * SUB + i for g in range(groups)] for i in range(SUB)]
    return lax.psum(a.astype(f32), "wide", axis_index_groups=members).astype(bf16)


def place_kernel(layout, spans, row_split, n_parts, spot, *refs):
    parts, outs = refs[:n_parts], refs[n_parts:]
    p = spot[1]
    for (bits, first), part in zip(layout, parts):
        at = p ^ bits
        core, quarter = at & 1, at >> 1
        count = part.shape[0]
        left = 0
        for out, span in zip(outs, spans):
            rows = out.shape[0] // (SUB if row_split else 4)
            row = quarter * rows + first
            column = 0
            if row_split:
                row = row + core * (out.shape[0] // 2)
            else:
                column = pl.multiple_of(core * span, 128)
            out[pl.ds(pl.multiple_of(row, 16), count), pl.ds(column, span)] = part[
                :, left : left + span
            ].astype(f32)
            left += span


def place(parts, shapes, row_split, spot):
    layout = tuple((bits, first) for bits, first, _ in parts)
    arrays = [part for _, _, part in parts]
    spans = tuple(s[1] if row_split else s[1] // 2 for s in shapes)
    return pl.pallas_call(
        functools.partial(place_kernel, layout, spans, row_split, len(arrays)),
        out_shape=[jax.ShapeDtypeStruct(s, f32) for s in shapes],
        grid_spec=pltpu.PrefetchScalarGridSpec(
            num_scalar_prefetch=1,
            grid=(1,),
            in_specs=[pl.BlockSpec(a.shape, lambda i, s: (0, 0)) for a in arrays],
            out_specs=[pl.BlockSpec(s, lambda i, s: (0, 0)) for s in shapes],
        ),
        compiler_params=pltpu.CompilerParams(vmem_limit_bytes=40 * MB),
        cost_estimate=pl.CostEstimate(
            flops=0, transcendentals=0, bytes_accessed=sum(6 * s[0] * s[1] for s in shapes)
        ),
        name="place",
    )(spot, *arrays)


def reduce_grad(half, shapes, row_split, x, y, z, spot):
    rows, width = half.shape
    view = half.reshape(4, 2, 2, 2, rows // 32, width)
    piece = reduce_plane(view, x, y, z).reshape(rows // 16, width)
    return place(spread_plane(piece), shapes, row_split, spot)


def sum_all(a, p, z):
    rows = a.shape[0] // SUB
    view = a.reshape(SUB, rows, a.shape[1])
    total = take(view, p, 0).astype(f32)
    for bits in range(1, SUB):
        total = total + swap_wide(take(view, p ^ bits, 0), bits).astype(f32)
    mine = total.astype(bf16)
    total = mine.astype(f32)
    for turn in (1, 2, 3):
        total = total + turn_narrow(mine, turn).astype(f32)
    return share_plane(across_groups(total.astype(bf16)), p)


def share_plane(piece, p):
    found = jnp.stack([piece] + [swap_wide(piece, bits) for bits in range(1, SUB)])
    return jnp.take(found, jnp.arange(SUB) ^ p, axis=0)


def pair_probs(pixels, same, keys_row):
    high, low = split_two(same * keys_row)
    scores = dot(high, pixels) + dot(low, pixels)
    biggest = jnp.max(scores[PATCH_COLS : PATCH_COLS + VARS], axis=0, keepdims=True)
    raised = jnp.exp(scores - biggest)
    total = jnp.sum(raised[PATCH_COLS : PATCH_COLS + VARS], axis=0, keepdims=True)
    return raised * (1.0 / total)


def variable_kernel(pixels_ref, same_ref, keys_ref, table_ref, merged_ref):
    pixels = pixels_ref[...]
    pixels_wide = pixels.astype(f32)
    same = same_ref[...]
    parts = []
    for i in range(2):
        probs = pair_probs(pixels, same, keys_ref[0, i : i + 1, :])
        weighted = (probs * pixels_wide).astype(bf16)
        parts.append(dot(table_ref[i * HEAD_DIM : (i + 1) * HEAD_DIM, :], weighted))
    merged_ref[...] = jnp.concatenate(parts, axis=0).T.astype(bf16)


def variable_forward(pixels, same, keys_rows, table_t):
    rows = pixels.shape[1]
    return pl.pallas_call(
        variable_kernel,
        out_shape=jax.ShapeDtypeStruct((rows, D), bf16),
        grid=(PAIRS,),
        in_specs=[
            pl.BlockSpec((COLS, rows), lambda h: (0, 0)),
            pl.BlockSpec((COLS, COLS), lambda h: (0, 0)),
            pl.BlockSpec((1, 2, COLS), lambda h: (h, 0, 0)),
            pl.BlockSpec((128, COLS), lambda h: (h, 0)),
        ],
        out_specs=pl.BlockSpec((rows, 128), lambda h: (0, h)),
        compiler_params=pltpu.CompilerParams(vmem_limit_bytes=40 * MB),
        cost_estimate=pl.CostEstimate(
            flops=6 * HEADS * rows * COLS * COLS,
            transcendentals=HEADS * rows * COLS,
            bytes_accessed=4 * rows * D,
        ),
        name="variable_forward",
    )(pixels, same, keys_rows, table_t)


def variable_back_kernel(
    pixels_ref, same_ref, keys_ref, keys_col_ref, table_ref, grad_ref, x_ref, zed_ref, pixel_ref
):
    step = pl.program_id(0)
    pixels = pixels_ref[...]
    pixels_wide = pixels.astype(f32)
    same = same_ref[...]
    same_low = same.astype(bf16)
    grad_t = grad_ref[...].astype(f32).T.astype(bf16)
    sums = []
    pixel_grad = None
    for i in range(2):
        probs = pair_probs(pixels, same, keys_ref[0, i : i + 1, :])
        weighted = (probs * pixels_wide).astype(bf16)
        grad_i = grad_t[i * HEAD_DIM : (i + 1) * HEAD_DIM, :]
        spread = dot(table_ref[:, i * HEAD_DIM : (i + 1) * HEAD_DIM], grad_i)
        high, low = split_two(spread * pixels_wide)
        prob_grad = dot(same_low, high) + dot(same_low, low)
        lifted = probs * prob_grad
        centre = jnp.sum(lifted[PATCH_COLS : PATCH_COLS + VARS], axis=0, keepdims=True)
        score_grad = lifted - probs * centre
        x_ref[i * HEAD_DIM : (i + 1) * HEAD_DIM, :] = dot_nt(grad_i, weighted).astype(bf16)
        sums.append(jnp.sum(score_grad * pixels_wide, axis=1, keepdims=True))
        term = probs * spread + score_grad * keys_col_ref[0, :, i : i + 1]
        pixel_grad = term if pixel_grad is None else pixel_grad + term
    zed_ref[0] = jnp.concatenate(sums, axis=1)

    @pl.when(step == 0)
    def _():
        pixel_ref[...] = pixel_grad

    @pl.when(step > 0)
    def _():
        pixel_ref[...] += pixel_grad


def variable_back(pixels, same, keys_rows, keys_cols, table, grad):
    rows = pixels.shape[1]
    return pl.pallas_call(
        variable_back_kernel,
        out_shape=[
            jax.ShapeDtypeStruct((D, COLS), bf16),
            jax.ShapeDtypeStruct((PAIRS, COLS, 2), f32),
            jax.ShapeDtypeStruct((COLS, rows), f32),
        ],
        grid=(PAIRS,),
        in_specs=[
            pl.BlockSpec((COLS, rows), lambda h: (0, 0)),
            pl.BlockSpec((COLS, COLS), lambda h: (0, 0)),
            pl.BlockSpec((1, 2, COLS), lambda h: (h, 0, 0)),
            pl.BlockSpec((1, COLS, 2), lambda h: (h, 0, 0)),
            pl.BlockSpec((COLS, 128), lambda h: (0, h)),
            pl.BlockSpec((rows, 128), lambda h: (0, h)),
        ],
        out_specs=[
            pl.BlockSpec((128, COLS), lambda h: (h, 0)),
            pl.BlockSpec((1, COLS, 2), lambda h: (h, 0, 0)),
            pl.BlockSpec((COLS, rows), lambda h: (0, 0)),
        ],
        compiler_params=pltpu.CompilerParams(vmem_limit_bytes=40 * MB),
        cost_estimate=pl.CostEstimate(
            flops=10 * HEADS * rows * COLS * COLS,
            transcendentals=HEADS * rows * COLS,
            bytes_accessed=4 * rows * D,
        ),
        name="variable_back",
    )(pixels, same, keys_rows, keys_cols, table, grad)


def mask_rows(segment_col, segment_row, padding_col, rows):
    key_at = lax.broadcasted_iota(jnp.int32, (rows, rows), 0)
    query_at = lax.broadcasted_iota(jnp.int32, (rows, rows), 1)
    allowed = (segment_col == segment_row) & ((padding_col == 1) | (key_at == query_at))
    return jnp.where(allowed, 0.0, masked_out).astype(f32)


def attention_kernel(q_ref, k_ref, v_ref, seg_row, seg_col, pad_col, out_ref, log_ref, mask_ref):
    rows = q_ref.shape[0]

    @pl.when(pl.program_id(0) == 0)
    def _():
        mask_ref[...] = mask_rows(seg_col[...], seg_row[...], pad_col[...], rows)

    q_t = (q_ref[...].astype(f32) * scale_by).T.astype(bf16)
    v_t = v_ref[...].astype(f32).T.astype(bf16)
    outs, logs = [], []
    for i in range(2):
        span = slice(i * HEAD_DIM, (i + 1) * HEAD_DIM)
        scores = dot(k_ref[:, span], q_t[span, :]) + mask_ref[...]
        biggest = jnp.max(scores, axis=0, keepdims=True)
        raised = jnp.exp(scores - biggest)
        total = jnp.sum(raised, axis=0, keepdims=True)
        outs.append(dot(v_t[span, :], raised.astype(bf16)) * (1.0 / total))
        logs.append(biggest + jnp.log(total))
    out_ref[...] = jnp.concatenate(outs, axis=0).T.astype(bf16)
    log_ref[0] = jnp.concatenate(logs, axis=0)


def attention(project, seg_row, seg_col, pad_col):
    rows = project.shape[0]
    column = lambda first: pl.BlockSpec((rows, 128), lambda h: (0, first * PAIRS + h))
    return pl.pallas_call(
        attention_kernel,
        out_shape=[
            jax.ShapeDtypeStruct((rows, D), bf16),
            jax.ShapeDtypeStruct((PAIRS, 2, rows), f32),
        ],
        grid=(PAIRS,),
        in_specs=[
            column(0),
            column(1),
            column(2),
            pl.BlockSpec((1, rows), lambda h: (0, 0)),
            pl.BlockSpec((rows, 1), lambda h: (0, 0)),
            pl.BlockSpec((rows, 1), lambda h: (0, 0)),
        ],
        out_specs=[column(0), pl.BlockSpec((1, 2, rows), lambda h: (h, 0, 0))],
        scratch_shapes=[pltpu.VMEM((rows, rows), f32)],
        compiler_params=pltpu.CompilerParams(vmem_limit_bytes=40 * MB),
        cost_estimate=pl.CostEstimate(
            flops=8 * rows * rows * D, transcendentals=HEADS * rows * rows, bytes_accessed=8 * rows * D
        ),
        name="attention",
    )(project, project, project, seg_row, seg_col, pad_col)


def attention_back_kernel(
    q_ref, k_ref, v_ref, grad_ref, log_ref, seg_row, seg_col, pad_col, out_ref, mask_ref
):
    rows = q_ref.shape[0]
    step = pl.program_id(0)

    @pl.when(step == 0)
    def _():
        mask_ref[...] = mask_rows(seg_col[...], seg_row[...], pad_col[...], rows)

    q_scaled = q_ref[...].astype(f32) * scale_by
    q_low = q_scaled.astype(bf16)
    q_t = q_scaled.T.astype(bf16)
    k_t = (k_ref[...].astype(f32) * scale_by).T.astype(bf16)
    grad_t = grad_ref[...].astype(f32).T.astype(bf16)
    q_grads, k_grads, v_grads = [], [], []
    for i in range(2):
        span = slice(i * HEAD_DIM, (i + 1) * HEAD_DIM)
        scores = dot(k_ref[:, span], q_t[span, :]) + mask_ref[...]
        probs = jnp.exp(scores - log_ref[0, i : i + 1, :])
        prob_grad = dot(v_ref[:, span], grad_t[span, :])
        lifted = probs * prob_grad
        centre = jnp.sum(lifted, axis=0, keepdims=True)
        score_grad = (lifted - probs * centre).astype(bf16)
        v_grads.append(dot(probs.astype(bf16), grad_ref[:, span]))
        k_grads.append(dot(score_grad, q_low[:, span]))
        q_grads.append(dot(k_t[span, :], score_grad))
    at = lambda first: pl.ds(pl.multiple_of(first * D + step * 128, 128), 128)
    out_ref[:, at(0)] = jnp.concatenate(q_grads, axis=0).T.astype(bf16)
    out_ref[:, at(1)] = jnp.concatenate(k_grads, axis=1).astype(bf16)
    out_ref[:, at(2)] = jnp.concatenate(v_grads, axis=1).astype(bf16)


def attention_back(project, grad, logs, seg_row, seg_col, pad_col):
    rows = project.shape[0]
    column = lambda first: pl.BlockSpec((rows, 128), lambda h: (0, first * PAIRS + h))
    return pl.pallas_call(
        attention_back_kernel,
        out_shape=jax.ShapeDtypeStruct((rows, 3 * D), bf16),
        grid=(PAIRS,),
        in_specs=[
            column(0),
            column(1),
            column(2),
            column(0),
            pl.BlockSpec((1, 2, rows), lambda h: (h, 0, 0)),
            pl.BlockSpec((1, rows), lambda h: (0, 0)),
            pl.BlockSpec((rows, 1), lambda h: (0, 0)),
            pl.BlockSpec((rows, 1), lambda h: (0, 0)),
        ],
        out_specs=pl.BlockSpec((rows, 3 * D), lambda h: (0, 0)),
        scratch_shapes=[pltpu.VMEM((rows, rows), f32)],
        compiler_params=pltpu.CompilerParams(vmem_limit_bytes=40 * MB),
        cost_estimate=pl.CostEstimate(
            flops=20 * rows * rows * D,
            transcendentals=HEADS * rows * rows,
            bytes_accessed=16 * rows * D,
        ),
        name="attention_back",
    )(project, project, project, grad, logs, seg_row, seg_col, pad_col)


def normalise(values):
    average = jnp.mean(values, axis=-1, keepdims=True)
    centered = values - average
    variance = jnp.mean(centered * centered, axis=-1, keepdims=True)
    inverse = lax.rsqrt(variance + norm_eps)
    return centered * inverse, inverse


def normalise_back(grad, gain, unit, inverse):
    scaled = grad * gain
    first = jnp.mean(scaled, axis=-1, keepdims=True)
    second = jnp.mean(scaled * unit, axis=-1, keepdims=True)
    return inverse * (scaled - first - unit * second)


def gelu_pair(values):
    below = 0.5 * (1.0 + lax.erf(values * (0.5**0.5)))
    density = jnp.exp(-0.5 * values * values) * ((0.5 / np.pi) ** 0.5)
    return values * below, below + values * density


def columns_half(a, core):
    span = a.shape[1] // 2
    return lax.dynamic_slice_in_dim(a, core * span, span, 1)


def per_device(
    patches,
    var_ids,
    segment_ids,
    pad_mask,
    embed_weight,
    var_embed,
    agg_query,
    key_weight,
    value_weight,
    agg_out_weight,
    agg_out_bias,
    norm_one_gain,
    norm_one_bias,
    qkv_weight,
    attn_out_weight,
    attn_out_bias,
    norm_two_gain,
    norm_two_bias,
    mlp_in_weight,
    mlp_in_bias,
    mlp_out_weight,
    mlp_out_bias,
    cotangent,
):
    rows = patches.shape[0]
    wide, z = lax.axis_index("wide"), lax.axis_index("narrow")
    p = wide % SUB
    core, x, y = p & 1, (p >> 1) & 1, p >> 2
    spot = jnp.stack([z, p]).astype(jnp.int32)
    shard = D // 4

    vectors = jnp.concatenate(
        [
            agg_query,
            agg_out_bias,
            norm_one_gain,
            norm_one_bias,
            attn_out_bias,
            norm_two_gain,
            norm_two_bias,
            mlp_out_bias,
            mlp_in_bias,
        ]
    ).reshape(-1, 128)
    around = jnp.stack([vectors] + [turn_narrow(vectors, turn) for turn in (1, 2, 3)])
    around = jnp.take(around, (z - jnp.arange(4)) % 4, axis=0).reshape(4, -1)
    whole = [around[:, i * shard : (i + 1) * shard].reshape(D) for i in range(8)]
    query_full = whole[0]
    agg_out_b, gain_one, bias_one, attn_out_b, gain_two, bias_two, mlp_out_b = [
        v.astype(f32) for v in whole[1:]
    ]
    mlp_in_b = around[:, 8 * shard :].reshape(4 * D).astype(f32)
    cot_there = swap_wide(cotangent, 1)

    line = jnp.arange(COLS, dtype=jnp.int32)
    variable = jnp.where(line < PATCH_COLS, line // PIX, (line - PATCH_COLS) % VARS)
    same = (variable[:, None] == variable[None, :]) & (line[None, :] < PATCH_COLS + VARS)
    same = same.astype(f32)
    chosen = jnp.take(var_ids, variable)
    source = jnp.where(line < PATCH_COLS, chosen * PIX + line % PIX, chosen + PATCH_COLS)
    source = jnp.where(line < PATCH_COLS + VARS, source, -1)
    chooser = (source[:, None] == line[None, :]).astype(bf16)
    embed_rows = jnp.concatenate(
        [embed_weight, var_embed, jnp.zeros((COLS - PATCH_COLS - VARS, shard), bf16)]
    )
    embed_rows = dot(chooser, embed_rows).astype(bf16)
    key_query = jnp.sum(
        key_weight.reshape(shard, HEADS, HEAD_DIM).astype(f32)
        * query_full.reshape(1, HEADS, HEAD_DIM).astype(f32),
        axis=-1,
    ).astype(bf16)
    keys_part = dot_nt(key_query.T, embed_rows) * scale_by
    value_part = lax.dynamic_slice_in_dim(value_weight, p * 128, 128, 1)
    table_part = dot(embed_rows, value_part).astype(bf16)
    keys_t = keys_part
    table_own = table_part.astype(f32)
    for turn in (1, 2, 3):
        keys_t = keys_t + turn_narrow(keys_part, turn)
        table_own = table_own + turn_narrow(table_part, turn).astype(f32)
    table_all = share_plane(table_own.astype(bf16), p)
    table = table_all.transpose(1, 0, 2).reshape(COLS, D)
    table_t = table_all.transpose(0, 2, 1).reshape(D, COLS)
    keys_rows = keys_t.reshape(PAIRS, 2, COLS)
    keys_cols = keys_rows.transpose(0, 2, 1)

    (agg_out_w,) = gather([agg_out_weight], p, spot)
    qkv_w, attn_out_w = gather([qkv_weight, attn_out_weight], p, spot)
    (mlp_in_w,) = gather([mlp_in_weight], p, spot)
    (mlp_out_w,) = gather([mlp_out_weight], p, spot)

    pixels = jnp.concatenate(
        [
            patches.T,
            jnp.ones((VARS, rows), bf16),
            jnp.zeros((COLS - PATCH_COLS - VARS, rows), bf16),
        ]
    )
    merged = variable_forward(pixels, same, keys_rows, table_t)
    merged_there = swap_wide(merged, 1)
    patch_state = dot(merged, agg_out_w) + agg_out_b
    unit_one, inverse_one = normalise(patch_state)
    normed = (unit_one * gain_one + bias_one).astype(bf16)
    normed_there = swap_wide(normed, 1)
    project = dot(normed, qkv_w).astype(bf16)
    seg_row, seg_col, pad_col = segment_ids, segment_ids.T, pad_mask.T
    attended, logs = attention(project, seg_row, seg_col, pad_col)
    attended_there = swap_wide(attended, 1)
    residual = patch_state + dot(attended, attn_out_w) + attn_out_b
    unit_two, inverse_two = normalise(residual)
    normed_two = (unit_two * gain_two + bias_two).astype(bf16)
    normed_two_there = swap_wide(normed_two, 1)
    hidden_pre = dot(normed_two, mlp_in_w) + mlp_in_b
    hidden, slope = gelu_pair(hidden_pre)
    hidden, slope = hidden.astype(bf16), slope.astype(bf16)
    result = (residual + dot(hidden, mlp_out_w) + mlp_out_b).astype(bf16)

    cot_float = cotangent.astype(f32)
    cot_both = jnp.concatenate([cotangent, cot_there])
    hidden_view = hidden.reshape(rows, 4, 2, D // 2)
    hidden_got = swap_wide(take(hidden_view, 1 - core, 2), 1)
    hidden_both = jnp.concatenate([take(hidden_view, core, 2), hidden_got]).reshape(2 * rows, -1)
    grad_mlp_out = dot_tn(hidden_both, cot_both).astype(bf16)
    (grad_mlp_out_w,) = reduce_grad(grad_mlp_out, [(D, D)], True, x, y, z, spot)

    hidden_pre_grad = (dot_nt(cotangent, mlp_out_w) * slope.astype(f32)).astype(bf16)
    pre_got = swap_wide(columns_half(hidden_pre_grad, 1 - core), 1)
    pre_both = jnp.concatenate([columns_half(hidden_pre_grad, core), pre_got])
    normed_two_both = jnp.concatenate([normed_two, normed_two_there])
    grad_mlp_in = dot_tn(normed_two_both, pre_both).astype(bf16)
    (grad_mlp_in_w,) = reduce_grad(grad_mlp_in, [(shard, 4 * D)], False, x, y, z, spot)

    normed_two_grad = dot_nt(hidden_pre_grad, mlp_in_w)
    residual_grad = cot_float + normalise_back(normed_two_grad, gain_two, unit_two, inverse_two)
    branch_grad = residual_grad.astype(bf16)
    branch_got = swap_wide(columns_half(branch_grad, 1 - core), 1)
    branch_both = jnp.concatenate([columns_half(branch_grad, core), branch_got])
    attended_both = jnp.concatenate([attended, attended_there])
    grad_attn_out = dot_tn(attended_both, branch_both).astype(bf16)
    attended_grad = dot_nt(branch_grad, attn_out_w).astype(bf16)
    project_grad = attention_back(project, attended_grad, logs, seg_row, seg_col, pad_col)
    project_got = swap_wide(columns_half(project_grad, 1 - core), 1)
    project_both = jnp.concatenate([columns_half(project_grad, core), project_got])
    normed_both = jnp.concatenate([normed, normed_there])
    grad_qkv = dot_tn(normed_both, project_both).astype(bf16)
    grad_qkv_w, grad_attn_out_w = reduce_grad(
        jnp.concatenate([grad_qkv, grad_attn_out], axis=1),
        [(shard, 3 * D), (shard, D)],
        False,
        x,
        y,
        z,
        spot,
    )

    normed_grad = dot_nt(project_grad, qkv_w)
    state_grad = residual_grad + normalise_back(normed_grad, gain_one, unit_one, inverse_one)
    state_grad = state_grad.astype(bf16)
    state_got = swap_wide(columns_half(state_grad, 1 - core), 1)
    state_both = jnp.concatenate([columns_half(state_grad, core), state_got])
    merged_both = jnp.concatenate([merged, merged_there])
    grad_agg_out = dot_tn(merged_both, state_both).astype(bf16)
    (grad_agg_out_w,) = reduce_grad(grad_agg_out, [(shard, D)], False, x, y, z, spot)
    merged_grad = dot_nt(state_grad, agg_out_w).astype(bf16)

    cross, zed, pixel_grad = variable_back(pixels, same, keys_rows, keys_cols, table, merged_grad)
    patches_grad = pixel_grad[:PATCH_COLS].T
    zed_high, zed_low = split_two(zed.transpose(0, 2, 1).reshape(HEADS, COLS))
    column_sums = [
        jnp.sum(state_grad.astype(f32), axis=0),
        jnp.sum(normed_grad * unit_one, axis=0),
        jnp.sum(normed_grad, axis=0),
        jnp.sum(branch_grad.astype(f32), axis=0),
        jnp.sum(normed_two_grad * unit_two, axis=0),
        jnp.sum(normed_two_grad, axis=0),
        jnp.sum(cot_float, axis=0),
        jnp.sum(hidden_pre_grad.astype(f32), axis=0),
    ]
    small = jnp.concatenate(column_sums).astype(bf16).reshape(-1, COLS)
    used = D + 2 * HEADS + small.shape[0]
    padded = -(-used // 128) * 128
    small = jnp.concatenate(
        [cross, zed_high, zed_low, small, jnp.zeros((padded - used, COLS), bf16)]
    )
    small = sum_all(small, p, z).reshape(padded, COLS)
    cross = small[:D]
    zed = small[D : D + HEADS].astype(f32) + small[D + HEADS : D + 2 * HEADS].astype(f32)
    sums = small[D + 2 * HEADS : used].astype(f32)
    own = lambda i: take(sums[4 * i : 4 * i + 4], z, 0)
    grad_mlp_in_b = lax.dynamic_slice_in_dim(sums[28:44], 4 * z, 4, 0).reshape(D)

    zed_both = split_two(zed)
    grad_embed = dot(value_weight, cross).T + sum(
        dot_nt(part.T, key_query) for part in zed_both
    ) * scale_by
    grad_embed = lax.dot_general(
        chooser.astype(f32),
        grad_embed,
        (((0,), (0,)), ((), ())),
        precision=lax.Precision.HIGHEST,
        preferred_element_type=f32,
    )
    grad_value_w = dot_nt(embed_rows.T, cross)
    query_grad = sum(dot_nt(embed_rows.T, part) for part in zed_both) * scale_by
    grad_key_w = jnp.repeat(query_grad, HEAD_DIM, axis=1) * query_full.astype(f32)[None, :]
    grad_query = jnp.sum(
        jnp.repeat(query_grad, HEAD_DIM, axis=1) * key_weight.astype(f32), axis=0
    )
    grad_query = grad_query.astype(bf16).reshape(4, shard)
    grad_agg_query = take(grad_query, z, 0).astype(f32)
    for turn in (1, 2, 3):
        grad_agg_query = grad_agg_query + turn_narrow(
            take(grad_query, (z + turn) % 4, 0), turn
        ).astype(f32)

    return (
        result,
        patches_grad,
        grad_embed[:PATCH_COLS],
        grad_embed[PATCH_COLS : PATCH_COLS + VARS],
        grad_agg_query,
        grad_key_w,
        grad_value_w,
        grad_agg_out_w,
        own(0),
        own(1),
        own(2),
        grad_qkv_w,
        grad_attn_out_w,
        own(3),
        own(4),
        own(5),
        grad_mlp_in_w,
        grad_mlp_in_b,
        grad_mlp_out_w,
        own(6),
    )


def solution(mesh):
    rows, shard = P(("wide", "narrow"), None), P("narrow", None)
    wide_shard, vector = P(None, "narrow"), P("narrow")
    return jax.shard_map(
        per_device,
        mesh=mesh,
        in_specs=(
            rows,
            P(),
            rows,
            rows,
            wide_shard,
            wide_shard,
            vector,
            shard,
            shard,
            shard,
            vector,
            vector,
            vector,
            shard,
            shard,
            vector,
            vector,
            vector,
            shard,
            vector,
            shard,
            vector,
            rows,
        ),
        out_specs=(
            rows,
            rows,
            wide_shard,
            wide_shard,
            vector,
            shard,
            shard,
            shard,
            vector,
            vector,
            vector,
            shard,
            shard,
            vector,
            vector,
            vector,
            shard,
            vector,
            shard,
            vector,
        ),
        check_vma=False,
    )
```

```python
import functools

import jax
import jax.numpy as jnp
import numpy as np
from jax import lax
from jax.experimental import pallas as pl
from jax.experimental.pallas import tpu as pltpu
from jax.sharding import PartitionSpec as P

D = 1024
HEADS = 16
HEAD_DIM = 64
VARS = 48
PIX = 4
PATCH_COLS = VARS * PIX
COLS = 256
PAIRS = HEADS // 2
SUB = 8

norm_eps = 1e-06
masked_out = -1e30
scale_by = HEAD_DIM ** (-0.5)
f32 = jnp.float32
bf16 = jnp.bfloat16
MB = 1 << 20


def dot(a, b):
    return jnp.dot(a, b, preferred_element_type=f32)


def dot_nt(a, b):
    return lax.dot_general(a, b, (((1,), (1,)), ((), ())), preferred_element_type=f32)


def dot_tn(a, b):
    return lax.dot_general(a, b, (((0,), (0,)), ((), ())), preferred_element_type=f32)


def split_two(a):
    high = a.astype(bf16)
    return high, (a - high.astype(f32)).astype(bf16)


def wide_pairs(bits_of):
    return [(i, i ^ bits_of(i)) for i in range(lax.axis_size("wide"))]


def over_core(a):
    return lax.ppermute(a, "wide", wide_pairs(lambda i: 1))


def over_first(a):
    return lax.ppermute(a, "wide", wide_pairs(lambda i: 4 if i & 1 else 2))


def over_second(a):
    return lax.ppermute(a, "wide", wide_pairs(lambda i: 2 if i & 1 else 4))


def turn_narrow(a, by):
    size = lax.axis_size("narrow")
    return lax.ppermute(a, "narrow", [(i, (i + by) % size) for i in range(size)])


def take(a, at, axis):
    return lax.dynamic_index_in_dim(a, at, axis, keepdims=False)


class Order:
    def __init__(self):
        self.last = None

    def hold(self, *arrays):
        if self.last is not None:
            arrays = lax.optimization_barrier((*arrays, self.last))[:-1]
        return arrays[0] if len(arrays) == 1 else arrays

    def mark(self, array):
        self.last = array


class Spread:
    def __init__(self, own, order):
        self.order = order
        self.own = own
        self.other = over_core(own)

    def near_step(self):
        other = self.order.hold(self.other)
        self.other = other
        both = jnp.stack([self.own, other])
        self.order.mark(both)
        self.near = over_first(both)

    def corner_step(self):
        self.near = self.order.hold(self.near)
        corner = self.near[0]
        self.order.mark(corner)
        self.corner = over_second(corner)
        self.far = over_core(self.near)

    def last_step(self):
        self.corner = self.order.hold(self.corner)
        self.order.mark(self.corner)
        self.corner_other = over_core(self.corner)

    def parts(self):
        parts = [self.own, self.other, self.near, self.far, self.corner, self.corner_other]
        return list(self.order.hold(*parts))


def origins(p, parts):
    own, other, near, far, corner, corner_other = parts
    first = 2 + 2 * (p & 1)
    second = 6 - first
    return [
        (p, own),
        (p ^ 1, other),
        (p ^ first, near.at[0]),
        (p ^ first ^ 1, near.at[1]),
        (p ^ second ^ 1, far.at[0]),
        (p ^ second, far.at[1]),
        (p ^ 6, corner),
        (p ^ 7, corner_other),
    ]


def core_and_quarter(place):
    core, x, y = place & 1, (place >> 1) & 1, place >> 2
    return core, jnp.where(core == 0, 2 * x + y, 2 * y + x)


def assemble_kernel(n_shards, spot, *refs):
    shards, parts = refs[:n_shards], refs[n_shards : n_shards + 6]
    fulls, sems = refs[n_shards + 6 : -1], refs[-1]
    z, p = spot[0], spot[1]
    copies = []

    def start(src, dst):
        copy = pltpu.make_async_copy(src, dst, sems.at[len(copies)])
        copy.start()
        copies.append(copy)

    for shard, full in zip(shards, fulls):
        rows = shard.shape[0]
        start(shard, full.at[pl.ds(pl.multiple_of(z * rows, rows), rows), :])
    for place, part in origins(p, parts):
        for turn in range(1, 4):
            origin = lax.rem(z - turn + 4, 4)
            left = 0
            for full in fulls:
                rows, width = full.shape[0] // 4, full.shape[1]
                count = rows // SUB
                at = pl.multiple_of(origin * rows + place * count, count)
                start(part.at[turn - 1, :, left : left + width], full.at[pl.ds(at, count), :])
                left += width
    for copy in copies:
        copy.wait()


def assemble(shards, parts, spot):
    n_copies = len(shards) * 25
    return pl.pallas_call(
        functools.partial(assemble_kernel, len(shards)),
        out_shape=[jax.ShapeDtypeStruct((4 * s.shape[0], s.shape[1]), s.dtype) for s in shards],
        in_specs=[pl.BlockSpec(memory_space=pltpu.SMEM)]
        + [pl.BlockSpec(memory_space=pl.ANY)] * (len(shards) + 6),
        out_specs=[pl.BlockSpec(memory_space=pltpu.VMEM)] * len(shards),
        scratch_shapes=[pltpu.SemaphoreType.DMA((n_copies,))],
        compiler_params=pltpu.CompilerParams(vmem_limit_bytes=40 * MB),
        cost_estimate=pl.CostEstimate(
            flops=0, transcendentals=0, bytes_accessed=sum(16 * s.size for s in shards)
        ),
        name="assemble",
    )(spot, *shards, *parts)


def pieces_of(shards, p):
    return jnp.concatenate(
        [
            lax.dynamic_slice_in_dim(s, p * (s.shape[0] // SUB), s.shape[0] // SUB, 0)
            for s in shards
        ],
        axis=1,
    )


def around_narrow(piece):
    return jnp.stack([turn_narrow(piece, turn) for turn in (1, 2, 3)])


def add_two(a, b):
    return (a.astype(f32) + b.astype(f32)).astype(bf16)


def first_and_second(p):
    core, x, y = p & 1, (p >> 1) & 1, p >> 2
    return jnp.where(core == 0, x, y), jnp.where(core == 0, y, x)


def reduce_first(grad, p):
    first, _ = first_and_second(p)
    axis = grad.ndim - 4
    return take(grad, first, axis), over_first(take(grad, 1 - first, axis))


def reduce_second(grad, p):
    _, second = first_and_second(p)
    axis = grad.ndim - 3
    return take(grad, second, axis), over_second(take(grad, 1 - second, axis))


def send_narrow(pick, z):
    return [pick(z)] + [turn_narrow(pick((z + turn) % 4), turn) for turn in (1, 2, 3)]


def add_four(parts):
    total = parts[0].astype(f32)
    for part in parts[1:]:
        total = total + part.astype(f32)
    return across_groups(total.astype(bf16))


def across_groups(a):
    groups = lax.axis_size("wide") // SUB
    if groups == 1:
        return a
    members = [[g * SUB + i for g in range(groups)] for i in range(SUB)]
    return lax.psum(a.astype(f32), "wide", axis_index_groups=members).astype(bf16)


def place_kernel(spans, shared, spot, *refs):
    parts, outs = refs[:6], refs[6:]
    for place, part in origins(spot[1], parts):
        core, quarter = core_and_quarter(place)
        left = 0
        for out, span in zip(outs, spans):
            count = out.shape[0] // 4
            row = pl.multiple_of(quarter * count, 16)
            column = pl.multiple_of(core * span, 128)
            out[pl.ds(row, count), pl.ds(column, span)] = part[
                :count, left : left + span
            ].astype(f32)
            left += span
        if shared:
            pair = core * 4 + quarter
            cross, rest = outs[-2:]
            row = pl.multiple_of(pair * 128, 128)
            cross[pl.ds(row, HEAD_DIM), :] = part[64:128, :COLS]
            cross[pl.ds(row + HEAD_DIM, HEAD_DIM), :] = part[64:128, COLS:]
            rest[pair] = part[128:, :].astype(f32)


def place(parts, shapes, spot, shared=False):
    spans = tuple(s[1] // 2 for s in shapes)
    out_shape = [jax.ShapeDtypeStruct(s, f32) for s in shapes]
    if shared:
        out_shape.append(jax.ShapeDtypeStruct((D, COLS), bf16))
        out_shape.append(jax.ShapeDtypeStruct((SUB, 16, 2 * COLS), f32))
    return pl.pallas_call(
        functools.partial(place_kernel, spans, shared),
        out_shape=out_shape,
        in_specs=[pl.BlockSpec(memory_space=pltpu.SMEM)]
        + [pl.BlockSpec(memory_space=pltpu.VMEM)] * 6,
        out_specs=[pl.BlockSpec(memory_space=pltpu.VMEM)] * len(out_shape),
        compiler_params=pltpu.CompilerParams(vmem_limit_bytes=40 * MB),
        cost_estimate=pl.CostEstimate(
            flops=0, transcendentals=0, bytes_accessed=sum(6 * s[0] * s[1] for s in shapes)
        ),
        name="place",
    )(spot, *parts)


def arrange_kernel(spot, *refs):
    parts, table, table_t = refs[:6], refs[6], refs[7]
    for place, part in origins(spot[1], parts):
        at = pl.ds(pl.multiple_of(place * 128, 128), 128)
        table[:, at] = part[...]
        table_t[at, :] = part[...].astype(f32).T.astype(bf16)


def arrange(parts, spot):
    return pl.pallas_call(
        arrange_kernel,
        out_shape=[
            jax.ShapeDtypeStruct((COLS, D), bf16),
            jax.ShapeDtypeStruct((D, COLS), bf16),
        ],
        in_specs=[pl.BlockSpec(memory_space=pltpu.SMEM)]
        + [pl.BlockSpec(memory_space=pltpu.VMEM)] * 6,
        out_specs=[pl.BlockSpec(memory_space=pltpu.VMEM)] * 2,
        name="arrange",
    )(spot, *parts)


def order_kernel(spot, *refs):
    out = refs[4]
    for turn in range(4):
        out[lax.rem(spot[0] - turn + 4, 4)] = refs[turn][...]


def order_narrow(own, others, spot):
    return pl.pallas_call(
        order_kernel,
        out_shape=jax.ShapeDtypeStruct((4, *own.shape), own.dtype),
        in_specs=[pl.BlockSpec(memory_space=pltpu.SMEM)]
        + [pl.BlockSpec(memory_space=pltpu.VMEM)] * 4,
        out_specs=pl.BlockSpec(memory_space=pltpu.VMEM),
        name="order",
    )(spot, own, *others)


def pair_probs(pixels, same, keys_row):
    high, low = split_two(same * keys_row)
    scores = dot(high, pixels) + dot(low, pixels)
    biggest = jnp.max(scores[PATCH_COLS : PATCH_COLS + VARS], axis=0, keepdims=True)
    raised = jnp.exp(scores - biggest)
    total = jnp.sum(raised[PATCH_COLS : PATCH_COLS + VARS], axis=0, keepdims=True)
    return raised * (1.0 / total)


def variable_kernel(pixels_ref, same_ref, keys_ref, table_ref, merged_ref):
    pixels = pixels_ref[...]
    pixels_wide = pixels.astype(f32)
    same = same_ref[...]
    parts = []
    for i in range(2):
        probs = pair_probs(pixels, same, keys_ref[0, i : i + 1, :])
        weighted = (probs * pixels_wide).astype(bf16)
        parts.append(dot(table_ref[i * HEAD_DIM : (i + 1) * HEAD_DIM, :], weighted))
    merged_ref[...] = jnp.concatenate(parts, axis=0).T.astype(bf16)


def variable_forward(pixels, same, keys_rows, table_t):
    rows = pixels.shape[1]
    return pl.pallas_call(
        variable_kernel,
        out_shape=jax.ShapeDtypeStruct((rows, D), bf16),
        grid=(PAIRS,),
        in_specs=[
            pl.BlockSpec((COLS, rows), lambda h: (0, 0)),
            pl.BlockSpec((COLS, COLS), lambda h: (0, 0)),
            pl.BlockSpec((1, 2, COLS), lambda h: (h, 0, 0)),
            pl.BlockSpec((128, COLS), lambda h: (h, 0)),
        ],
        out_specs=pl.BlockSpec((rows, 128), lambda h: (0, h)),
        compiler_params=pltpu.CompilerParams(vmem_limit_bytes=40 * MB),
        cost_estimate=pl.CostEstimate(
            flops=6 * HEADS * rows * COLS * COLS,
            transcendentals=HEADS * rows * COLS,
            bytes_accessed=4 * rows * D,
        ),
        name="variable_forward",
    )(pixels, same, keys_rows, table_t)


def variable_back_kernel(
    pixels_ref, same_ref, keys_ref, keys_col_ref, table_ref, grad_ref, x_ref, zed_ref, pixel_ref
):
    step = pl.program_id(0)
    pixels = pixels_ref[...]
    pixels_wide = pixels.astype(f32)
    same = same_ref[...]
    same_low = same.astype(bf16)
    grad_t = grad_ref[...].astype(f32).T.astype(bf16)
    sums = []
    pixel_grad = None
    for i in range(2):
        probs = pair_probs(pixels, same, keys_ref[0, i : i + 1, :])
        weighted = (probs * pixels_wide).astype(bf16)
        grad_i = grad_t[i * HEAD_DIM : (i + 1) * HEAD_DIM, :]
        spread = dot(table_ref[:, i * HEAD_DIM : (i + 1) * HEAD_DIM], grad_i)
        high, low = split_two(spread * pixels_wide)
        prob_grad = dot(same_low, high) + dot(same_low, low)
        lifted = probs * prob_grad
        centre = jnp.sum(lifted[PATCH_COLS : PATCH_COLS + VARS], axis=0, keepdims=True)
        score_grad = lifted - probs * centre
        x_ref[:, i * COLS : (i + 1) * COLS] = dot_nt(grad_i, weighted).astype(bf16)
        sums.append(jnp.sum(score_grad * pixels_wide, axis=1, keepdims=True))
        term = probs * spread + score_grad * keys_col_ref[0, :, i : i + 1]
        pixel_grad = term if pixel_grad is None else pixel_grad + term
    zed_ref[0] = jnp.concatenate(sums, axis=1)

    @pl.when(step == 0)
    def _():
        pixel_ref[...] = pixel_grad

    @pl.when(step > 0)
    def _():
        pixel_ref[...] += pixel_grad


def variable_back(pixels, same, keys_rows, keys_cols, table, grad):
    rows = pixels.shape[1]
    return pl.pallas_call(
        variable_back_kernel,
        out_shape=[
            jax.ShapeDtypeStruct((D // 2, 2 * COLS), bf16),
            jax.ShapeDtypeStruct((PAIRS, COLS, 2), f32),
            jax.ShapeDtypeStruct((COLS, rows), f32),
        ],
        grid=(PAIRS,),
        in_specs=[
            pl.BlockSpec((COLS, rows), lambda h: (0, 0)),
            pl.BlockSpec((COLS, COLS), lambda h: (0, 0)),
            pl.BlockSpec((1, 2, COLS), lambda h: (h, 0, 0)),
            pl.BlockSpec((1, COLS, 2), lambda h: (h, 0, 0)),
            pl.BlockSpec((COLS, 128), lambda h: (0, h)),
            pl.BlockSpec((rows, 128), lambda h: (0, h)),
        ],
        out_specs=[
            pl.BlockSpec((HEAD_DIM, 2 * COLS), lambda h: (h, 0)),
            pl.BlockSpec((1, COLS, 2), lambda h: (h, 0, 0)),
            pl.BlockSpec((COLS, rows), lambda h: (0, 0)),
        ],
        compiler_params=pltpu.CompilerParams(vmem_limit_bytes=40 * MB),
        cost_estimate=pl.CostEstimate(
            flops=10 * HEADS * rows * COLS * COLS,
            transcendentals=HEADS * rows * COLS,
            bytes_accessed=4 * rows * D,
        ),
        name="variable_back",
    )(pixels, same, keys_rows, keys_cols, table, grad)


def mask_rows(segment_col, segment_row, padding_col, rows):
    key_at = lax.broadcasted_iota(jnp.int32, (rows, rows), 0)
    query_at = lax.broadcasted_iota(jnp.int32, (rows, rows), 1)
    allowed = (segment_col == segment_row) & ((padding_col == 1) | (key_at == query_at))
    return jnp.where(allowed, 0.0, masked_out).astype(f32)


def attention_kernel(q_ref, k_ref, v_ref, seg_row, seg_col, pad_col, out_ref, log_ref, mask_ref):
    rows = q_ref.shape[0]

    @pl.when(pl.program_id(0) == 0)
    def _():
        mask_ref[...] = mask_rows(seg_col[...], seg_row[...], pad_col[...], rows)

    q_t = (q_ref[...].astype(f32) * scale_by).T.astype(bf16)
    v_t = v_ref[...].astype(f32).T.astype(bf16)
    outs, logs = [], []
    for i in range(2):
        span = slice(i * HEAD_DIM, (i + 1) * HEAD_DIM)
        scores = dot(k_ref[:, span], q_t[span, :]) + mask_ref[...]
        biggest = jnp.max(scores, axis=0, keepdims=True)
        raised = jnp.exp(scores - biggest)
        total = jnp.sum(raised, axis=0, keepdims=True)
        outs.append(dot(v_t[span, :], raised.astype(bf16)) * (1.0 / total))
        logs.append(biggest + jnp.log(total))
    out_ref[...] = jnp.concatenate(outs, axis=0).T.astype(bf16)
    log_ref[0] = jnp.concatenate(logs, axis=0)


def attention(project, seg_row, seg_col, pad_col):
    rows = project.shape[0]
    column = lambda first: pl.BlockSpec((rows, 128), lambda h: (0, first * PAIRS + h))
    return pl.pallas_call(
        attention_kernel,
        out_shape=[
            jax.ShapeDtypeStruct((rows, D), bf16),
            jax.ShapeDtypeStruct((PAIRS, 2, rows), f32),
        ],
        grid=(PAIRS,),
        in_specs=[
            column(0),
            column(1),
            column(2),
            pl.BlockSpec((1, rows), lambda h: (0, 0)),
            pl.BlockSpec((rows, 1), lambda h: (0, 0)),
            pl.BlockSpec((rows, 1), lambda h: (0, 0)),
        ],
        out_specs=[column(0), pl.BlockSpec((1, 2, rows), lambda h: (h, 0, 0))],
        scratch_shapes=[pltpu.VMEM((rows, rows), f32)],
        compiler_params=pltpu.CompilerParams(vmem_limit_bytes=40 * MB),
        cost_estimate=pl.CostEstimate(
            flops=8 * rows * rows * D, transcendentals=HEADS * rows * rows, bytes_accessed=8 * rows * D
        ),
        name="attention",
    )(project, project, project, seg_row, seg_col, pad_col)


def attention_back_kernel(
    q_ref, k_ref, v_ref, grad_ref, log_ref, seg_row, seg_col, pad_col, out_ref, mask_ref
):
    rows = q_ref.shape[0]
    step = pl.program_id(0)

    @pl.when(step == 0)
    def _():
        mask_ref[...] = mask_rows(seg_col[...], seg_row[...], pad_col[...], rows)

    q_scaled = q_ref[...].astype(f32) * scale_by
    q_low = q_scaled.astype(bf16)
    q_t = q_scaled.T.astype(bf16)
    k_t = (k_ref[...].astype(f32) * scale_by).T.astype(bf16)
    grad_t = grad_ref[...].astype(f32).T.astype(bf16)
    q_grads, k_grads, v_grads = [], [], []
    for i in range(2):
        span = slice(i * HEAD_DIM, (i + 1) * HEAD_DIM)
        scores = dot(k_ref[:, span], q_t[span, :]) + mask_ref[...]
        probs = jnp.exp(scores - log_ref[0, i : i + 1, :])
        prob_grad = dot(v_ref[:, span], grad_t[span, :])
        lifted = probs * prob_grad
        centre = jnp.sum(lifted, axis=0, keepdims=True)
        score_grad = (lifted - probs * centre).astype(bf16)
        v_grads.append(dot(probs.astype(bf16), grad_ref[:, span]))
        k_grads.append(dot(score_grad, q_low[:, span]))
        q_grads.append(dot(k_t[span, :], score_grad))
    at = lambda first: pl.ds(pl.multiple_of(first * D + step * 128, 128), 128)
    out_ref[:, at(0)] = jnp.concatenate(q_grads, axis=0).T.astype(bf16)
    out_ref[:, at(1)] = jnp.concatenate(k_grads, axis=1).astype(bf16)
    out_ref[:, at(2)] = jnp.concatenate(v_grads, axis=1).astype(bf16)


def attention_back(project, grad, logs, seg_row, seg_col, pad_col):
    rows = project.shape[0]
    column = lambda first: pl.BlockSpec((rows, 128), lambda h: (0, first * PAIRS + h))
    return pl.pallas_call(
        attention_back_kernel,
        out_shape=jax.ShapeDtypeStruct((rows, 3 * D), bf16),
        grid=(PAIRS,),
        in_specs=[
            column(0),
            column(1),
            column(2),
            column(0),
            pl.BlockSpec((1, 2, rows), lambda h: (h, 0, 0)),
            pl.BlockSpec((1, rows), lambda h: (0, 0)),
            pl.BlockSpec((rows, 1), lambda h: (0, 0)),
            pl.BlockSpec((rows, 1), lambda h: (0, 0)),
        ],
        out_specs=pl.BlockSpec((rows, 3 * D), lambda h: (0, 0)),
        scratch_shapes=[pltpu.VMEM((rows, rows), f32)],
        compiler_params=pltpu.CompilerParams(vmem_limit_bytes=40 * MB),
        cost_estimate=pl.CostEstimate(
            flops=20 * rows * rows * D,
            transcendentals=HEADS * rows * rows,
            bytes_accessed=16 * rows * D,
        ),
        name="attention_back",
    )(project, project, project, grad, logs, seg_row, seg_col, pad_col)


def normalise(values):
    average = jnp.mean(values, axis=-1, keepdims=True)
    centered = values - average
    variance = jnp.mean(centered * centered, axis=-1, keepdims=True)
    inverse = lax.rsqrt(variance + norm_eps)
    return centered * inverse, inverse


def normalise_back(grad, gain, unit, inverse):
    scaled = grad * gain
    first = jnp.mean(scaled, axis=-1, keepdims=True)
    second = jnp.mean(scaled * unit, axis=-1, keepdims=True)
    return inverse * (scaled - first - unit * second)


def gelu_pair(values):
    below = 0.5 * (1.0 + lax.erf(values * (0.5**0.5)))
    density = jnp.exp(-0.5 * values * values) * ((0.5 / np.pi) ** 0.5)
    return values * below, below + values * density


def columns_half(a, core):
    span = a.shape[1] // 2
    return lax.dynamic_slice_in_dim(a, core * span, span, 1)


def per_device(
    patches,
    var_ids,
    segment_ids,
    pad_mask,
    embed_weight,
    var_embed,
    agg_query,
    key_weight,
    value_weight,
    agg_out_weight,
    agg_out_bias,
    norm_one_gain,
    norm_one_bias,
    qkv_weight,
    attn_out_weight,
    attn_out_bias,
    norm_two_gain,
    norm_two_bias,
    mlp_in_weight,
    mlp_in_bias,
    mlp_out_weight,
    mlp_out_bias,
    cotangent,
):
    rows = patches.shape[0]
    z, p = lax.axis_index("narrow"), lax.axis_index("wide") % SUB
    core = p & 1
    spot = jnp.stack([z, p]).astype(jnp.int32)
    shard = D // 4
    order = Order()
    half = lambda a: columns_half(a, core)
    other_half = lambda a: columns_half(a, 1 - core)

    singles = (
        agg_query,
        agg_out_bias,
        norm_one_gain,
        norm_one_bias,
        attn_out_bias,
        norm_two_gain,
        norm_two_bias,
        mlp_out_bias,
    )
    at_row = lax.broadcasted_iota(jnp.int32, (8, shard), 0)
    vectors = jnp.zeros((8, shard), bf16)
    for i, single in enumerate(singles):
        vectors = jnp.where(at_row == i, single[None, :], vectors)
    vectors = jnp.concatenate([vectors, mlp_in_bias.reshape(4, shard)])
    around = [turn_narrow(vectors, turn) for turn in (1, 2, 3)]
    piece_a = pieces_of([agg_out_weight], p)
    got_a = [turn_narrow(piece_a, turn) for turn in (1, 2, 3)]
    piece_b = pieces_of([qkv_weight, attn_out_weight], p)
    got_b = [turn_narrow(piece_b, turn) for turn in (1, 2, 3)]

    line = jnp.arange(COLS, dtype=jnp.int32)
    variable = jnp.where(line < PATCH_COLS, line // PIX, (line - PATCH_COLS) % VARS)
    used = line < PATCH_COLS + VARS
    same = ((variable[:, None] == variable[None, :]) & used[None, :]).astype(f32)
    picks = variable[:, None] == jnp.arange(VARS, dtype=jnp.int32)[None, :]
    chosen = jnp.sum(jnp.where(picks, var_ids[None, :], 0), axis=1)
    source = jnp.where(line < PATCH_COLS, chosen * PIX + line % PIX, chosen + PATCH_COLS)
    source = jnp.where(used, source, -1)
    chooser = (source[:, None] == line[None, :]).astype(bf16)
    embed_rows = jnp.concatenate(
        [embed_weight, var_embed, jnp.zeros((COLS - PATCH_COLS - VARS, shard), bf16)]
    )
    value_part = lax.dynamic_slice_in_dim(value_weight, p * 128, 128, 1)
    table_part = dot(embed_rows, value_part).astype(bf16)

    around = order_narrow(vectors, order.hold(*around), spot)
    whole = [around[:, i].reshape(D) for i in range(8)]
    query_full = whole[0].astype(f32)
    agg_out_b, gain_one, bias_one, attn_out_b, gain_two, bias_two, mlp_out_b = [
        v.astype(f32) for v in whole[1:]
    ]
    mlp_in_b = around[:, 8:].reshape(4 * D).astype(f32)
    head_of = jnp.arange(D, dtype=jnp.int32) // HEAD_DIM
    heads_eye = (jnp.arange(HEADS, dtype=jnp.int32)[:, None] == head_of[None, :]).astype(f32)
    query_rows = (heads_eye * query_full[None, :]).astype(bf16)
    key_query_t = dot_nt(query_rows, key_weight).astype(bf16)
    keys_part = dot_nt(key_query_t, embed_rows) * scale_by
    keys_packed = jnp.concatenate(split_two(keys_part)).reshape(-1, 128)
    packed = jnp.concatenate([table_part, keys_packed])
    order.mark(packed)
    got_packed = [turn_narrow(packed, turn) for turn in (1, 2, 3)]

    full_patches = jnp.concatenate(
        [
            patches,
            jnp.ones((rows, VARS), bf16),
            jnp.zeros((rows, COLS - PATCH_COLS - VARS), bf16),
        ],
        axis=1,
    )
    pixels = lax.dot_general(
        chooser, full_patches, (((0,), (1,)), ((), ())), preferred_element_type=f32
    ).astype(bf16)
    seg_row, seg_col, pad_col = segment_ids, segment_ids.T, pad_mask.T
    cot_half, cot_got = half(cotangent), over_core(other_half(cotangent))

    bundle_a = jnp.stack(order.hold(*got_a))
    order.mark(bundle_a)
    spread_a = Spread(bundle_a, order)
    piece_c = order.hold(pieces_of([mlp_in_weight], p))
    got_c = [turn_narrow(piece_c, turn) for turn in (1, 2, 3)]
    spread_a.near_step()

    got_packed = order.hold(*got_packed)
    total = packed.astype(f32)
    for part in got_packed:
        total = total + part.astype(f32)
    table_own = total[:COLS].astype(bf16)
    order.mark(table_own)
    keys_two = total[COLS:].reshape(2, HEADS, COLS)
    keys_rows = (keys_two[0] + keys_two[1]).reshape(PAIRS, 2, COLS)
    keys_cols = keys_rows.transpose(0, 2, 1)
    spread_t = Spread(table_own, order)
    spread_t.near_step()
    spread_a.corner_step()
    spread_t.corner_step()

    bundle_b = jnp.stack(order.hold(*got_b))
    order.mark(bundle_b)
    spread_b = Spread(bundle_b, order)
    piece_d = order.hold(pieces_of([mlp_out_weight], p))
    got_d = [turn_narrow(piece_d, turn) for turn in (1, 2, 3)]
    spread_b.near_step()
    spread_t.last_step()
    spread_a.last_step()
    table, table_t = arrange(spread_t.parts(), spot)
    merged = variable_forward(pixels, same, keys_rows, table_t)
    order.mark(merged)
    merged_there = over_core(merged)
    (agg_out_w,) = assemble([agg_out_weight], spread_a.parts(), spot)
    patch_state = dot(merged, agg_out_w) + agg_out_b
    unit_one, inverse_one = normalise(patch_state)
    normed = (unit_one * gain_one + bias_one).astype(bf16)
    order.mark(normed)
    normed_there = over_core(normed)

    ke_part = dot(embed_rows, key_weight).astype(bf16)
    got_ke = send_narrow(lambda at: lax.dynamic_slice_in_dim(ke_part, at * shard, shard, 1), z)

    spread_b.corner_step()
    bundle_c = jnp.stack(order.hold(*got_c))
    order.mark(bundle_c)
    spread_c = Spread(bundle_c, order)
    spread_b.last_step()
    spread_c.near_step()
    qkv_w, attn_out_w = assemble([qkv_weight, attn_out_weight], spread_b.parts(), spot)
    project = dot(normed, qkv_w).astype(bf16)
    order.mark(project)
    spread_c.corner_step()
    attended, logs = attention(order.hold(project), seg_row, seg_col, pad_col)
    order.mark(attended)
    attended_there = over_core(attended)
    bundle_d = jnp.stack(order.hold(*got_d))
    order.mark(bundle_d)
    spread_d = Spread(bundle_d, order)
    spread_c.last_step()
    spread_d.near_step()
    residual = patch_state + dot(attended, attn_out_w) + attn_out_b
    unit_two, inverse_two = normalise(residual)
    normed_two = (unit_two * gain_two + bias_two).astype(bf16)
    order.mark(normed_two)
    normed_two_there = over_core(normed_two)
    (mlp_in_w,) = assemble([mlp_in_weight], spread_c.parts(), spot)
    hidden_pre = dot(normed_two, mlp_in_w) + mlp_in_b
    hidden, slope = gelu_pair(hidden_pre)
    hidden, slope = hidden.astype(bf16), slope.astype(bf16)
    order.mark(hidden)
    hidden_there = over_core(hidden)
    spread_d.corner_step()

    def grad_of(own, there, own_half, got):
        return (dot_tn(own, own_half) + dot_tn(there, got)).astype(bf16)

    def blocks(a):
        return a.reshape(4, 2, 2, a.shape[0] // 16, a.shape[1])

    def add_held(pair):
        total = add_two(*order.hold(*pair))
        order.mark(total)
        return total

    def send_block(grad):
        return send_narrow(lambda at: take(grad, at, 0), z)

    def add_narrow(parts):
        total = add_four(order.hold(*parts))
        order.mark(total)
        return total

    cot_float = cotangent.astype(f32)
    grad_d = blocks(grad_of(order.hold(hidden), hidden_there, cot_half, cot_got))
    order.mark(grad_d)
    grad_d = reduce_first(grad_d, p)
    spread_d.last_step()
    (mlp_out_w,) = assemble([mlp_out_weight], spread_d.parts(), spot)
    hidden_pre_grad = (dot_nt(cotangent, mlp_out_w) * slope.astype(f32)).astype(bf16)
    order.mark(hidden_pre_grad)
    pre_got = over_core(other_half(hidden_pre_grad))

    normed_two_grad = dot_nt(order.hold(hidden_pre_grad), mlp_in_w)
    residual_grad = cot_float + normalise_back(normed_two_grad, gain_two, unit_two, inverse_two)
    branch_grad = residual_grad.astype(bf16)
    order.mark(branch_grad)
    branch_got = over_core(other_half(branch_grad))
    grad_c = blocks(
        grad_of(normed_two, normed_two_there, order.hold(half(hidden_pre_grad)), pre_got)
    )
    order.mark(grad_c)
    grad_c = reduce_first(grad_c, p)
    attended_grad = dot_nt(order.hold(branch_grad), attn_out_w).astype(bf16)
    order.mark(attended_grad)
    grad_d = reduce_second(add_held(grad_d), p)
    project_grad = attention_back(
        project, order.hold(attended_grad), logs, seg_row, seg_col, pad_col
    )
    order.mark(project_grad)
    project_got = over_core(other_half(project_grad))
    normed_grad = dot_nt(order.hold(project_grad), qkv_w)
    state_grad = residual_grad + normalise_back(normed_grad, gain_one, unit_one, inverse_one)
    state_grad = state_grad.astype(bf16)
    order.mark(state_grad)
    state_got = over_core(other_half(state_grad))
    grad_c = reduce_second(add_held(grad_c), p)
    grad_b = jnp.concatenate(
        [
            grad_of(normed, normed_there, order.hold(half(project_grad)), project_got),
            grad_of(attended, attended_there, half(branch_grad), branch_got),
        ],
        axis=1,
    )
    order.mark(grad_b)
    grad_b = reduce_first(blocks(grad_b), p)
    grad_d = send_block(add_held(grad_d))
    merged_grad = dot_nt(order.hold(state_grad), agg_out_w).astype(bf16)

    cross, zed, pixel_grad = variable_back(pixels, same, keys_rows, keys_cols, table, merged_grad)
    order.mark(cross)
    zed_parts = split_two(zed.transpose(0, 2, 1).reshape(HEADS, COLS))
    column_sums = [
        jnp.sum(state_grad.astype(f32), axis=0),
        jnp.sum(normed_grad * unit_one, axis=0),
        jnp.sum(normed_grad, axis=0),
        jnp.sum(branch_grad.astype(f32), axis=0),
        jnp.sum(normed_two_grad * unit_two, axis=0),
        jnp.sum(normed_two_grad, axis=0),
        jnp.sum(cot_float, axis=0),
        jnp.sum(hidden_pre_grad.astype(f32), axis=0),
    ]
    small = jnp.concatenate(
        [part.reshape(-1) for part in zed_parts] + [v.astype(bf16) for v in column_sums]
    ).reshape(-1, 2 * COLS)
    n_small = small.shape[0]
    small = jnp.concatenate([small, jnp.zeros((16 * SUB - n_small, 2 * COLS), bf16)])
    shared = jnp.concatenate(
        [cross.reshape(SUB, HEAD_DIM, 2 * COLS), small.reshape(SUB, 16, 2 * COLS)], axis=1
    )
    shared = shared.reshape(2, 2, 2, 80, 2 * COLS)
    shared_got = over_core(take(shared, 1 - core, 0))
    grad_c = send_block(add_held(grad_c))
    grad_a = grad_of(merged, merged_there, order.hold(half(state_grad)), state_got)
    grad_a = grad_a.reshape(4, 2, 2, shard // 4, D // 2).transpose(1, 2, 0, 3, 4)
    grad_a = grad_a.reshape(2, 2, shard, D // 2)
    shared = add_two(take(shared, core, 0), shared_got)
    grad_a = jnp.concatenate([grad_a, shared], axis=2)
    order.mark(grad_a)
    grad_a = reduce_first(grad_a, p)
    grad_b = reduce_second(add_held(grad_b), p)
    spread_d = Spread(add_narrow(grad_d), order)
    result = (residual + dot(order.hold(hidden), mlp_out_w) + mlp_out_b).astype(bf16)
    order.mark(result)
    grad_a = reduce_second(add_held(grad_a), p)
    spread_d.near_step()
    spread_c = Spread(add_narrow(grad_c), order)
    patches_grad = lax.dot_general(
        order.hold(pixel_grad),
        chooser.astype(f32),
        (((0,), (1,)), ((), ())),
        precision=lax.Precision.HIGHEST,
        preferred_element_type=f32,
    )[:, :PATCH_COLS]
    order.mark(patches_grad)
    grad_a = add_held(grad_a)
    grad_a = send_narrow(
        lambda at: jnp.concatenate(
            [lax.dynamic_slice_in_dim(grad_a, at * 64, 64, 0), grad_a[shard:]]
        ),
        z,
    )
    grad_b = send_block(add_held(grad_b))
    spread_c.near_step()
    spread_d.corner_step()
    spread_a = Spread(add_narrow(grad_a), order)
    spread_c.corner_step()
    spread_a.near_step()
    spread_b = Spread(add_narrow(grad_b), order)
    spread_d.last_step()
    spread_a.corner_step()
    spread_b.near_step()
    spread_c.last_step()
    (grad_mlp_out_w,) = place(spread_d.parts(), [(D, D)], spot)
    order.mark(grad_mlp_out_w)
    spread_a.last_step()
    spread_b.corner_step()
    (grad_mlp_in_w,) = place(spread_c.parts(), [(shard, 4 * D)], spot)
    order.mark(grad_mlp_in_w)
    grad_agg_out_w, cross, rest = place(spread_a.parts(), [(shard, D)], spot, shared=True)
    order.mark(cross)

    rest = rest.reshape(16 * SUB, 2 * COLS)
    zed = rest[:16].reshape(2, HEADS, COLS)
    zed = zed[0] + zed[1]
    sums = rest[16:n_small].reshape(-1, COLS)
    own = lambda i: take(sums[4 * i : 4 * i + 4], z, 0)
    grad_mlp_in_b = lax.dynamic_slice_in_dim(sums[28:44], 4 * z, 4, 0).reshape(D)
    zed_both = split_two(zed)
    grad_embed = lax.dot_general(
        cross, value_weight, (((0,), (1,)), ((), ())), preferred_element_type=f32
    ) + (dot_tn(zed_both[0], key_query_t) + dot_tn(zed_both[1], key_query_t)) * scale_by
    grad_value_w = lax.dot_general(
        embed_rows, cross, (((0,), (1,)), ((), ())), preferred_element_type=f32
    )
    query_grad = sum(
        lax.dot_general(embed_rows, part, (((0,), (1,)), ((), ())), preferred_element_type=f32)
        for part in zed_both
    ) * scale_by
    grad_key_w = jnp.repeat(query_grad, HEAD_DIM, axis=1) * query_full[None, :]
    ke_own = split_two(sum(part.astype(f32) for part in got_ke))
    per_head = sum(dot(part, ke) for part in zed_both for ke in ke_own)
    own_head = z * 4 + jnp.arange(shard, dtype=jnp.int32) // HEAD_DIM
    mine = jnp.arange(HEADS, dtype=jnp.int32)[:, None] == own_head[None, :]
    grad_agg_query = jnp.sum(jnp.where(mine, per_head, 0.0), axis=0) * scale_by

    spread_b.last_step()
    grad_qkv_w, grad_attn_out_w = place(spread_b.parts(), [(shard, 3 * D), (shard, D)], spot)

    return (
        result,
        patches_grad,
        grad_embed[:PATCH_COLS],
        grad_embed[PATCH_COLS : PATCH_COLS + VARS],
        grad_agg_query,
        grad_key_w,
        grad_value_w,
        grad_agg_out_w,
        own(0),
        own(1),
        own(2),
        grad_qkv_w,
        grad_attn_out_w,
        own(3),
        own(4),
        own(5),
        grad_mlp_in_w,
        grad_mlp_in_b,
        grad_mlp_out_w,
        own(6),
    )


def solution(mesh):
    rows, shard = P(("wide", "narrow"), None), P("narrow", None)
    wide_shard, vector = P(None, "narrow"), P("narrow")
    return jax.shard_map(
        per_device,
        mesh=mesh,
        in_specs=(
            rows,
            P(),
            rows,
            rows,
            wide_shard,
            wide_shard,
            vector,
            shard,
            shard,
            shard,
            vector,
            vector,
            vector,
            shard,
            shard,
            vector,
            vector,
            vector,
            shard,
            vector,
            shard,
            vector,
            rows,
        ),
        out_specs=(
            rows,
            rows,
            wide_shard,
            wide_shard,
            vector,
            shard,
            shard,
            shard,
            vector,
            vector,
            vector,
            shard,
            shard,
            vector,
            vector,
            vector,
            shard,
            vector,
            shard,
            vector,
        ),
        check_vma=False,
    )
```

```python
import functools

import jax
import jax.numpy as jnp
import numpy as np
from jax import lax
from jax.experimental import pallas as pl
from jax.experimental.pallas import tpu as pltpu
from jax.sharding import PartitionSpec as P

D = 1024
HEADS = 16
HEAD_DIM = 64
VARS = 48
PIX = 4
PATCH_COLS = VARS * PIX
COLS = 256
PAIRS = HEADS // 2
SUB = 8

norm_eps = 1e-06
masked_out = -1e30
scale_by = HEAD_DIM ** (-0.5)
f32 = jnp.float32
bf16 = jnp.bfloat16
MB = 1 << 20


def takes(microseconds):
    flops = int(microseconds * 0.6 * 1e9)
    return pl.CostEstimate(flops=flops, transcendentals=0, bytes_accessed=1)


def dot(a, b):
    return jnp.dot(a, b, preferred_element_type=f32)


def dot_nt(a, b):
    return lax.dot_general(a, b, (((1,), (1,)), ((), ())), preferred_element_type=f32)


def dot_tn(a, b):
    return lax.dot_general(a, b, (((0,), (0,)), ((), ())), preferred_element_type=f32)


def split_two(a):
    high = a.astype(bf16)
    return high, (a - high.astype(f32)).astype(bf16)


def wide_pairs(bits_of):
    return [(i, i ^ bits_of(i)) for i in range(lax.axis_size("wide"))]


def over_core(a):
    return lax.ppermute(a, "wide", wide_pairs(lambda i: 1))


def over_first(a):
    return lax.ppermute(a, "wide", wide_pairs(lambda i: 4 if i & 1 else 2))


def over_second(a):
    return lax.ppermute(a, "wide", wide_pairs(lambda i: 2 if i & 1 else 4))


def turn_narrow(a, by):
    size = lax.axis_size("narrow")
    return lax.ppermute(a, "narrow", [(i, (i + by) % size) for i in range(size)])


def swap_narrow(a, bits):
    size = lax.axis_size("narrow")
    return lax.ppermute(a, "narrow", [(i, i ^ bits) for i in range(size)])


def take(a, at, axis):
    return lax.dynamic_index_in_dim(a, at, axis, keepdims=False)


class Order:
    def __init__(self):
        self.pending = []

    def hold(self, *arrays):
        arrays = lax.optimization_barrier((*arrays, *self.pending))[: len(arrays)]
        self.pending = [arrays[0]]
        return arrays[0] if len(arrays) == 1 else arrays

    def mark(self, array):
        self.pending.append(array)


class Narrow:
    def __init__(self, own, order):
        self.order = order
        self.own = own
        self.two = swap_narrow(own, 2)

    def second_step(self):
        self.two = self.order.hold(self.two)
        both = jnp.stack([self.own, self.two])
        self.order.mark(both)
        self.others = swap_narrow(both, 1)

    def bundle(self):
        others = self.order.hold(self.others)
        bundle = jnp.concatenate([self.two[None], others])
        self.order.mark(bundle)
        return bundle


class Spread:
    def __init__(self, own, order):
        self.order = order
        self.own = own
        self.other = over_core(own)

    def near_step(self):
        other = self.order.hold(self.other)
        self.other = other
        both = jnp.stack([self.own, other])
        self.order.mark(both)
        self.near = over_first(both)

    def corner_step(self):
        self.near = self.order.hold(self.near)
        corner = self.near[0]
        self.order.mark(corner)
        self.corner = over_second(corner)
        self.far = over_core(self.near)

    def last_step(self):
        self.corner = self.order.hold(self.corner)
        self.order.mark(self.corner)
        self.corner_other = over_core(self.corner)

    def parts(self):
        parts = [self.own, self.other, self.near, self.far, self.corner, self.corner_other]
        return list(self.order.hold(*parts))


def origins(p, parts):
    own, other, near, far, corner, corner_other = parts
    first = 2 + 2 * (p & 1)
    second = 6 - first
    return [
        (p, own),
        (p ^ 1, other),
        (p ^ first, near.at[0]),
        (p ^ first ^ 1, near.at[1]),
        (p ^ second ^ 1, far.at[0]),
        (p ^ second, far.at[1]),
        (p ^ 6, corner),
        (p ^ 7, corner_other),
    ]


def core_and_quarter(place):
    core, x, y = place & 1, (place >> 1) & 1, place >> 2
    return core, jnp.where(core == 0, 2 * x + y, 2 * y + x)


def assemble_kernel(n_shards, spot, *refs):
    shards, parts = refs[:n_shards], refs[n_shards : n_shards + 6]
    fulls, sems = refs[n_shards + 6 : -1], refs[-1]
    z, p = spot[0], spot[1]
    copies = []

    def start(src, dst):
        copy = pltpu.make_async_copy(src, dst, sems.at[len(copies)])
        copy.start()
        copies.append(copy)

    for shard, full in zip(shards, fulls):
        rows = shard.shape[0]
        start(shard, full.at[pl.ds(pl.multiple_of(z * rows, rows), rows), :])
    for place, part in origins(p, parts):
        for i, bits in enumerate((2, 1, 3)):
            origin = z ^ bits
            left = 0
            for full in fulls:
                rows, width = full.shape[0] // 4, full.shape[1]
                count = rows // SUB
                at = pl.multiple_of(origin * rows + place * count, count)
                start(part.at[i, :, left : left + width], full.at[pl.ds(at, count), :])
                left += width
    for copy in copies:
        copy.wait()


def assemble(shards, parts, spot):
    n_copies = 25 * len(shards)
    return pl.pallas_call(
        functools.partial(assemble_kernel, len(shards)),
        out_shape=[jax.ShapeDtypeStruct((4 * s.shape[0], s.shape[1]), s.dtype) for s in shards],
        in_specs=[pl.BlockSpec(memory_space=pltpu.SMEM)]
        + [pl.BlockSpec(memory_space=pl.ANY)] * (len(shards) + 6),
        out_specs=[pl.BlockSpec(memory_space=pltpu.VMEM)] * len(shards),
        scratch_shapes=[pltpu.SemaphoreType.DMA((n_copies,))],
        compiler_params=pltpu.CompilerParams(vmem_limit_bytes=12 * MB),
        cost_estimate=takes(3.5),
        name="assemble",
    )(spot, *shards, *parts)


def pieces_of(shards, p):
    return jnp.concatenate(
        [
            lax.dynamic_slice_in_dim(s, p * (s.shape[0] // SUB), s.shape[0] // SUB, 0)
            for s in shards
        ],
        axis=1,
    )


def add_two(a, b):
    return (a.astype(f32) + b.astype(f32)).astype(bf16)


def pick_kernel(bits, grad, sent):
    sent[...] = grad[...].reshape(sent.shape)


def pick_first(grad, bit):
    n, _, _, rows, width = grad.shape
    return pl.pallas_call(
        pick_kernel,
        out_shape=jax.ShapeDtypeStruct((n, 2, rows, width), bf16),
        grid_spec=pltpu.PrefetchScalarGridSpec(
            num_scalar_prefetch=1,
            grid=(n,),
            in_specs=[pl.BlockSpec((1, 1, 2, rows, width), lambda i, b: (i, b[0], 0, 0, 0))],
            out_specs=pl.BlockSpec((1, 2, rows, width), lambda i, b: (i, 0, 0, 0)),
        ),
        compiler_params=pltpu.CompilerParams(vmem_limit_bytes=5 * MB),
        cost_estimate=takes(2.5),
        name="pick_first",
    )(bit[None], grad)


def add_split_kernel(bits, kept_sent, got_sent, kept_kept, got_kept, sent, kept):
    def total(a, b):
        return (a[...].astype(f32).reshape(sent.shape) + b[...].astype(f32).reshape(sent.shape)).astype(bf16)

    sent[...] = total(kept_sent, got_sent)
    kept[...] = total(kept_kept, got_kept)


def add_split(grad, got, first, bit):
    n, _, _, rows, width = grad.shape
    block = (1, 1, 1, rows, width)
    got_block = (1, 1, rows, width)
    out = jax.ShapeDtypeStruct((n, rows, width), bf16)
    return pl.pallas_call(
        add_split_kernel,
        out_shape=[out, out],
        grid_spec=pltpu.PrefetchScalarGridSpec(
            num_scalar_prefetch=1,
            grid=(n,),
            in_specs=[
                pl.BlockSpec(block, lambda i, b: (i, b[0], 1 - b[1], 0, 0)),
                pl.BlockSpec(got_block, lambda i, b: (i, 1 - b[1], 0, 0)),
                pl.BlockSpec(block, lambda i, b: (i, b[0], b[1], 0, 0)),
                pl.BlockSpec(got_block, lambda i, b: (i, b[1], 0, 0)),
            ],
            out_specs=[pl.BlockSpec((1, rows, width), lambda i, b: (i, 0, 0))] * 2,
        ),
        compiler_params=pltpu.CompilerParams(vmem_limit_bytes=8 * MB),
        cost_estimate=takes(2.5),
        name="add_split",
    )(jnp.stack([first, bit]), grad, got, grad, got)


class Reduce:
    def __init__(self, grad, p, z, order):
        core, x, y = p & 1, (p >> 1) & 1, p >> 2
        self.bits = [jnp.where(core == 0, x, y), jnp.where(core == 0, y, x), z & 1, z >> 1]
        self.order, self.stage, self.kept = order, 0, grad
        sent = pick_first(grad, 1 - self.bits[0])
        order.mark(sent)
        self.got = over_first(sent)

    def step(self):
        kept, got = self.kept, self.order.hold(self.got)
        self.stage += 1
        if self.stage == 4:
            self.total = across_groups(add_two(kept[0], got[0]))
            self.order.mark(self.total)
            return
        bit, first = self.bits[self.stage], jnp.zeros_like(self.bits[0])
        if self.stage == 1:
            first = self.bits[0]
        else:
            rows, width = kept.shape[1:]
            kept = kept.reshape(-1, 1, 2, rows, width)
            got = got.reshape(-1, 2, rows, width)
        sent, self.kept = add_split(kept, got, first, bit)
        self.order.mark(sent)
        self.got = over_second(sent) if self.stage == 1 else swap_narrow(sent, self.stage - 1)


class ReduceShared(Reduce):
    def step(self):
        if self.stage == 0:
            return super().step()
        total = add_two(self.kept, self.order.hold(self.got))
        self.order.mark(total)
        self.stage += 1
        if self.stage == 4:
            self.total = across_groups(total)
            return
        total = total.reshape(-1, total.shape[-1])
        shape, axis = ((2, 2, 64, -1), 1) if self.stage == 2 else ((2, 64, -1), 0)
        blocks, shared = total[:-80].reshape(shape), total[-80:]

        def pick(bit):
            return jnp.concatenate([take(blocks, bit, axis).reshape(-1, total.shape[-1]), shared])

        sent = pick(1 - self.bits[self.stage])
        self.order.mark(sent)
        self.kept = pick(self.bits[self.stage])
        self.got = swap_narrow(sent, self.stage - 1)


def across_groups(a):
    groups = lax.axis_size("wide") // SUB
    if groups == 1:
        return a
    members = [[g * SUB + i for g in range(groups)] for i in range(SUB)]
    return lax.psum(a.astype(f32), "wide", axis_index_groups=members).astype(bf16)


def place_kernel(spans, shared, spot, *refs):
    parts, outs = refs[:6], refs[6:]
    for place, part in origins(spot[1], parts):
        core, quarter = core_and_quarter(place)
        left = 0
        for out, span in zip(outs, spans):
            count = out.shape[0] // 4
            row = pl.multiple_of(quarter * count, 16)
            column = pl.multiple_of(core * span, 128)
            out[pl.ds(row, count), pl.ds(column, span)] = part[
                :count, left : left + span
            ].astype(f32)
            left += span
        if shared:
            pair = core * 4 + quarter
            cross, rest = outs[-2:]
            row = pl.multiple_of(pair * 128, 128)
            cross[pl.ds(row, HEAD_DIM), :] = part[64:128, :COLS]
            cross[pl.ds(row + HEAD_DIM, HEAD_DIM), :] = part[64:128, COLS:]
            rest[pair] = part[128:, :].astype(f32)


def place(parts, shapes, spot, shared=False):
    spans = tuple(s[1] // 2 for s in shapes)
    out_shape = [jax.ShapeDtypeStruct(s, f32) for s in shapes]
    if shared:
        out_shape.append(jax.ShapeDtypeStruct((D, COLS), bf16))
        out_shape.append(jax.ShapeDtypeStruct((SUB, 16, 2 * COLS), f32))
    return pl.pallas_call(
        functools.partial(place_kernel, spans, shared),
        out_shape=out_shape,
        in_specs=[pl.BlockSpec(memory_space=pltpu.SMEM)]
        + [pl.BlockSpec(memory_space=pltpu.VMEM)] * 6,
        out_specs=[pl.BlockSpec(memory_space=pltpu.VMEM)] * len(out_shape),
        compiler_params=pltpu.CompilerParams(vmem_limit_bytes=10 * MB),
        cost_estimate=takes(3),
        name="place",
    )(spot, *parts)


def arrange_kernel(spot, *refs):
    parts, table, table_t = refs[:6], refs[6], refs[7]
    for place, part in origins(spot[1], parts):
        at = pl.ds(pl.multiple_of(place * 128, 128), 128)
        table[:, at] = part[...]
        table_t[at, :] = part[...].astype(f32).T.astype(bf16)


def arrange(parts, spot):
    return pl.pallas_call(
        arrange_kernel,
        out_shape=[
            jax.ShapeDtypeStruct((COLS, D), bf16),
            jax.ShapeDtypeStruct((D, COLS), bf16),
        ],
        in_specs=[pl.BlockSpec(memory_space=pltpu.SMEM)]
        + [pl.BlockSpec(memory_space=pltpu.VMEM)] * 6,
        out_specs=[pl.BlockSpec(memory_space=pltpu.VMEM)] * 2,
        name="arrange",
    )(spot, *parts)


def order_kernel(spot, own, others, out):
    out[spot[0]] = own[...]
    for i, bits in enumerate((2, 1, 3)):
        out[spot[0] ^ bits] = others[i]


def order_narrow(own, others, spot):
    return pl.pallas_call(
        order_kernel,
        out_shape=jax.ShapeDtypeStruct((4, *own.shape), own.dtype),
        in_specs=[pl.BlockSpec(memory_space=pltpu.SMEM)]
        + [pl.BlockSpec(memory_space=pltpu.VMEM)] * 2,
        out_specs=pl.BlockSpec(memory_space=pltpu.VMEM),
        name="order",
    )(spot, own, others)


def pair_probs(pixels, same, keys_row):
    high, low = split_two(same * keys_row)
    scores = dot(high, pixels) + dot(low, pixels)
    biggest = jnp.max(scores[PATCH_COLS : PATCH_COLS + VARS], axis=0, keepdims=True)
    raised = jnp.exp(scores - biggest)
    total = jnp.sum(raised[PATCH_COLS : PATCH_COLS + VARS], axis=0, keepdims=True)
    return raised * (1.0 / total)


def variable_kernel(pixels_ref, same_ref, keys_ref, table_ref, merged_ref):
    pixels = pixels_ref[...]
    pixels_wide = pixels.astype(f32)
    same = same_ref[...]
    parts = []
    for i in range(2):
        probs = pair_probs(pixels, same, keys_ref[0, i : i + 1, :])
        weighted = (probs * pixels_wide).astype(bf16)
        parts.append(dot(table_ref[i * HEAD_DIM : (i + 1) * HEAD_DIM, :], weighted))
    merged_ref[...] = jnp.concatenate(parts, axis=0).T.astype(bf16)


def variable_forward(pixels, same, keys_rows, table_t):
    rows = pixels.shape[1]
    return pl.pallas_call(
        variable_kernel,
        out_shape=jax.ShapeDtypeStruct((rows, D), bf16),
        grid=(PAIRS,),
        in_specs=[
            pl.BlockSpec((COLS, rows), lambda h: (0, 0)),
            pl.BlockSpec((COLS, COLS), lambda h: (0, 0)),
            pl.BlockSpec((1, 2, COLS), lambda h: (h, 0, 0)),
            pl.BlockSpec((128, COLS), lambda h: (h, 0)),
        ],
        out_specs=pl.BlockSpec((rows, 128), lambda h: (0, h)),
        compiler_params=pltpu.CompilerParams(vmem_limit_bytes=8 * MB),
        cost_estimate=takes(9),
        name="variable_forward",
    )(pixels, same, keys_rows, table_t)


def variable_back_kernel(
    pixels_ref, same_ref, keys_ref, keys_col_ref, table_ref, grad_ref, x_ref, zed_ref, pixel_ref
):
    step = pl.program_id(0)
    pixels = pixels_ref[...]
    pixels_wide = pixels.astype(f32)
    same = same_ref[...]
    same_low = same.astype(bf16)
    grad_t = grad_ref[...].astype(f32).T.astype(bf16)
    sums = []
    pixel_grad = None
    for i in range(2):
        probs = pair_probs(pixels, same, keys_ref[0, i : i + 1, :])
        weighted = (probs * pixels_wide).astype(bf16)
        grad_i = grad_t[i * HEAD_DIM : (i + 1) * HEAD_DIM, :]
        spread = dot(table_ref[:, i * HEAD_DIM : (i + 1) * HEAD_DIM], grad_i)
        high, low = split_two(spread * pixels_wide)
        prob_grad = dot(same_low, high) + dot(same_low, low)
        lifted = probs * prob_grad
        centre = jnp.sum(lifted[PATCH_COLS : PATCH_COLS + VARS], axis=0, keepdims=True)
        score_grad = lifted - probs * centre
        x_ref[:, i * COLS : (i + 1) * COLS] = dot_nt(grad_i, weighted).astype(bf16)
        sums.append(jnp.sum(score_grad * pixels_wide, axis=1, keepdims=True))
        term = probs * spread + score_grad * keys_col_ref[0, :, i : i + 1]
        pixel_grad = term if pixel_grad is None else pixel_grad + term
    zed_ref[0] = jnp.concatenate(sums, axis=1)

    @pl.when(step == 0)
    def _():
        pixel_ref[...] = pixel_grad

    @pl.when(step > 0)
    def _():
        pixel_ref[...] += pixel_grad


def variable_back(pixels, same, keys_rows, keys_cols, table, grad):
    rows = pixels.shape[1]
    return pl.pallas_call(
        variable_back_kernel,
        out_shape=[
            jax.ShapeDtypeStruct((D // 2, 2 * COLS), bf16),
            jax.ShapeDtypeStruct((PAIRS, COLS, 2), f32),
            jax.ShapeDtypeStruct((COLS, rows), f32),
        ],
        grid=(PAIRS,),
        in_specs=[
            pl.BlockSpec((COLS, rows), lambda h: (0, 0)),
            pl.BlockSpec((COLS, COLS), lambda h: (0, 0)),
            pl.BlockSpec((1, 2, COLS), lambda h: (h, 0, 0)),
            pl.BlockSpec((1, COLS, 2), lambda h: (h, 0, 0)),
            pl.BlockSpec((COLS, 128), lambda h: (0, h)),
            pl.BlockSpec((rows, 128), lambda h: (0, h)),
        ],
        out_specs=[
            pl.BlockSpec((HEAD_DIM, 2 * COLS), lambda h: (h, 0)),
            pl.BlockSpec((1, COLS, 2), lambda h: (h, 0, 0)),
            pl.BlockSpec((COLS, rows), lambda h: (0, 0)),
        ],
        compiler_params=pltpu.CompilerParams(vmem_limit_bytes=10 * MB),
        cost_estimate=takes(14.5),
        name="variable_back",
    )(pixels, same, keys_rows, keys_cols, table, grad)


def mask_rows(segment_col, segment_row, padding_col, rows):
    key_at = lax.broadcasted_iota(jnp.int32, (rows, rows), 0)
    query_at = lax.broadcasted_iota(jnp.int32, (rows, rows), 1)
    allowed = (segment_col == segment_row) & ((padding_col == 1) | (key_at == query_at))
    return jnp.where(allowed, 0.0, masked_out).astype(f32)


def attention_kernel(q_ref, k_ref, v_ref, seg_row, seg_col, pad_col, out_ref, log_ref, mask_ref):
    rows = q_ref.shape[0]

    @pl.when(pl.program_id(0) == 0)
    def _():
        mask_ref[...] = mask_rows(seg_col[...], seg_row[...], pad_col[...], rows)

    q_t = (q_ref[...].astype(f32) * scale_by).T.astype(bf16)
    v_t = v_ref[...].astype(f32).T.astype(bf16)
    outs, logs = [], []
    for i in range(2):
        span = slice(i * HEAD_DIM, (i + 1) * HEAD_DIM)
        scores = dot(k_ref[:, span], q_t[span, :]) + mask_ref[...]
        biggest = jnp.max(scores, axis=0, keepdims=True)
        raised = jnp.exp(scores - biggest)
        total = jnp.sum(raised, axis=0, keepdims=True)
        outs.append(dot(v_t[span, :], raised.astype(bf16)) * (1.0 / total))
        logs.append(biggest + jnp.log(total))
    out_ref[...] = jnp.concatenate(outs, axis=0).T.astype(bf16)
    log_ref[0] = jnp.concatenate(logs, axis=0)


def attention(project, seg_row, seg_col, pad_col):
    rows = project.shape[0]
    column = lambda first: pl.BlockSpec((rows, 128), lambda h: (0, first * PAIRS + h))
    return pl.pallas_call(
        attention_kernel,
        out_shape=[
            jax.ShapeDtypeStruct((rows, D), bf16),
            jax.ShapeDtypeStruct((PAIRS, 2, rows), f32),
        ],
        grid=(PAIRS,),
        in_specs=[
            column(0),
            column(1),
            column(2),
            pl.BlockSpec((1, rows), lambda h: (0, 0)),
            pl.BlockSpec((rows, 1), lambda h: (0, 0)),
            pl.BlockSpec((rows, 1), lambda h: (0, 0)),
        ],
        out_specs=[column(0), pl.BlockSpec((1, 2, rows), lambda h: (h, 0, 0))],
        scratch_shapes=[pltpu.VMEM((rows, rows), f32)],
        compiler_params=pltpu.CompilerParams(vmem_limit_bytes=8 * MB),
        cost_estimate=takes(12.5),
        name="attention",
    )(project, project, project, seg_row, seg_col, pad_col)


def attention_back_kernel(
    q_ref, k_ref, v_ref, grad_ref, log_ref, seg_row, seg_col, pad_col, out_ref, mask_ref
):
    rows = q_ref.shape[0]
    step = pl.program_id(0)

    @pl.when(step == 0)
    def _():
        mask_ref[...] = mask_rows(seg_col[...], seg_row[...], pad_col[...], rows)

    q_scaled = q_ref[...].astype(f32) * scale_by
    q_low = q_scaled.astype(bf16)
    q_t = q_scaled.T.astype(bf16)
    k_t = (k_ref[...].astype(f32) * scale_by).T.astype(bf16)
    grad_t = grad_ref[...].astype(f32).T.astype(bf16)
    q_grads, k_grads, v_grads = [], [], []
    for i in range(2):
        span = slice(i * HEAD_DIM, (i + 1) * HEAD_DIM)
        scores = dot(k_ref[:, span], q_t[span, :]) + mask_ref[...]
        probs = jnp.exp(scores - log_ref[0, i : i + 1, :])
        prob_grad = dot(v_ref[:, span], grad_t[span, :])
        lifted = probs * prob_grad
        centre = jnp.sum(lifted, axis=0, keepdims=True)
        score_grad = (lifted - probs * centre).astype(bf16)
        v_grads.append(dot(probs.astype(bf16), grad_ref[:, span]))
        k_grads.append(dot(score_grad, q_low[:, span]))
        q_grads.append(dot(k_t[span, :], score_grad))
    at = lambda first: pl.ds(pl.multiple_of(first * D + step * 128, 128), 128)
    out_ref[:, at(0)] = jnp.concatenate(q_grads, axis=0).T.astype(bf16)
    out_ref[:, at(1)] = jnp.concatenate(k_grads, axis=1).astype(bf16)
    out_ref[:, at(2)] = jnp.concatenate(v_grads, axis=1).astype(bf16)


def attention_back(project, grad, logs, seg_row, seg_col, pad_col):
    rows = project.shape[0]
    column = lambda first: pl.BlockSpec((rows, 128), lambda h: (0, first * PAIRS + h))
    return pl.pallas_call(
        attention_back_kernel,
        out_shape=jax.ShapeDtypeStruct((rows, 3 * D), bf16),
        grid=(PAIRS,),
        in_specs=[
            column(0),
            column(1),
            column(2),
            column(0),
            pl.BlockSpec((1, 2, rows), lambda h: (h, 0, 0)),
            pl.BlockSpec((1, rows), lambda h: (0, 0)),
            pl.BlockSpec((rows, 1), lambda h: (0, 0)),
            pl.BlockSpec((rows, 1), lambda h: (0, 0)),
        ],
        out_specs=pl.BlockSpec((rows, 3 * D), lambda h: (0, 0)),
        scratch_shapes=[pltpu.VMEM((rows, rows), f32)],
        compiler_params=pltpu.CompilerParams(vmem_limit_bytes=14 * MB),
        cost_estimate=takes(16.5),
        name="attention_back",
    )(project, project, project, grad, logs, seg_row, seg_col, pad_col)


def mlp_in_kernel(rows_ref, weight, bias, hidden, slope):
    value, change = gelu_pair(dot(rows_ref[...], weight[...]) + bias[...])
    hidden[...] = value.astype(bf16)
    slope[...] = change.astype(bf16)


def mlp_in(rows_in, weight, bias):
    rows, hidden = rows_in.shape[0], weight.shape[1]
    block = 512
    columns = lambda count: pl.BlockSpec((count, block), lambda i: (0, i))
    return pl.pallas_call(
        mlp_in_kernel,
        out_shape=[jax.ShapeDtypeStruct((rows, hidden), bf16)] * 2,
        grid=(hidden // block,),
        in_specs=[pl.BlockSpec((rows, D), lambda i: (0, 0)), columns(D), columns(1)],
        out_specs=[columns(rows)] * 2,
        compiler_params=pltpu.CompilerParams(vmem_limit_bytes=14 * MB),
        cost_estimate=takes(11),
        name="mlp_in",
    )(rows_in, weight, bias[None])


def mlp_back_kernel(core, cot, w_out, w_in, slope, own, other, grad, sums):
    step = pl.program_id(0)
    pre = (dot_nt(cot[...], w_out[...]) * slope[...].astype(f32)).astype(bf16)
    sums[0] = jnp.sum(pre.astype(f32), axis=0, keepdims=True)
    part = dot_nt(pre, w_in[...])

    @pl.when(step < 2)
    def _():
        other[...] = pre

    @pl.when(step >= 2)
    def _():
        own[...] = pre

    @pl.when(step == 0)
    def _():
        grad[...] = part

    @pl.when(step > 0)
    def _():
        grad[...] += part


def mlp_back(core, cot, w_out, w_in, slope):
    rows, hidden = cot.shape[0], w_out.shape[0]
    block = hidden // 4
    at = lambda i, c: lax.rem(i + 2 - 2 * c[0], 4)
    return pl.pallas_call(
        mlp_back_kernel,
        out_shape=[
            jax.ShapeDtypeStruct((rows, hidden // 2), bf16),
            jax.ShapeDtypeStruct((rows, hidden // 2), bf16),
            jax.ShapeDtypeStruct((rows, D), f32),
            jax.ShapeDtypeStruct((4, 1, block), f32),
        ],
        grid_spec=pltpu.PrefetchScalarGridSpec(
            num_scalar_prefetch=1,
            grid=(4,),
            in_specs=[
                pl.BlockSpec((rows, D), lambda i, c: (0, 0)),
                pl.BlockSpec((block, D), lambda i, c: (at(i, c), 0)),
                pl.BlockSpec((D, block), lambda i, c: (0, at(i, c))),
                pl.BlockSpec((rows, block), lambda i, c: (0, at(i, c))),
            ],
            out_specs=[
                pl.BlockSpec((rows, block), lambda i, c: (0, jnp.maximum(i - 2, 0))),
                pl.BlockSpec((rows, block), lambda i, c: (0, jnp.minimum(i, 1))),
                pl.BlockSpec((rows, D), lambda i, c: (0, 0)),
                pl.BlockSpec((1, 1, block), lambda i, c: (at(i, c), 0, 0)),
            ],
        ),
        compiler_params=pltpu.CompilerParams(vmem_limit_bytes=50 * MB),
        cost_estimate=takes(15.5),
        name="mlp_back",
    )(core, cot, w_out, w_in, slope)


def finish_kernel(
    spot, cross, rest, value, embed_t, key_query, query, ke, embed_out, value_out, key_out, query_out, bias_out, *sums_out
):
    z = spot[0]
    summed = cross[...]
    zed = rest[0, :, :COLS] + rest[0, :, COLS:]
    zed_both = split_two(zed)
    embed_grad = dot(value[...], summed)
    query_grad = 0.0
    per_head = 0.0
    for part in zed_both:
        embed_grad += dot(key_query[...], part) * scale_by
        query_grad += dot_nt(embed_t[...], part) * scale_by
        per_head += dot_nt(part, ke[...]) * scale_by
    embed_out[...] = embed_grad.T
    value_out[...] = dot_nt(embed_t[...], summed)
    head = lax.broadcasted_iota(jnp.int32, (HEADS, D), 0)
    line = lax.broadcasted_iota(jnp.int32, (HEADS, D), 1)
    eye = (head == line // HEAD_DIM).astype(bf16)
    high, low = split_two(query_grad)
    key_out[...] = (dot(high, eye) + dot(low, eye)) * query[...]
    head = lax.broadcasted_iota(jnp.int32, per_head.shape, 0)
    line = lax.broadcasted_iota(jnp.int32, per_head.shape, 1)
    mine = head == z * 4 + line // HEAD_DIM
    query_out[...] = jnp.sum(jnp.where(mine, per_head, 0.0), axis=0, keepdims=True)
    column = pl.multiple_of((z & 1) * COLS, COLS)
    for i, out in enumerate(sums_out):
        at = 16 + 2 * i + (z >> 1)
        out[...] = rest[at // 16, pl.ds(lax.rem(at, 16), 1), pl.ds(column, COLS)]
    for i in range(2):
        at = 16 + 14 + 2 * z + i
        bias_out[pl.ds(i, 1), :] = rest[at // 16, pl.ds(lax.rem(at, 16), 1), :]


def finish(spot, cross, rest, value, embed_t, key_query, query, ke):
    shard = value.shape[0]
    row = jax.ShapeDtypeStruct((1, shard), f32)
    out_shape = [
        jax.ShapeDtypeStruct((COLS, shard), f32),
        jax.ShapeDtypeStruct((shard, D), f32),
        jax.ShapeDtypeStruct((shard, D), f32),
        row,
        jax.ShapeDtypeStruct((2, 2 * COLS), f32),
    ] + [row] * 7
    return pl.pallas_call(
        finish_kernel,
        out_shape=out_shape,
        in_specs=[pl.BlockSpec(memory_space=pltpu.SMEM)]
        + [pl.BlockSpec(memory_space=pltpu.VMEM)] * 7,
        out_specs=[pl.BlockSpec(memory_space=pltpu.VMEM)] * len(out_shape),
        compiler_params=pltpu.CompilerParams(vmem_limit_bytes=12 * MB),
        cost_estimate=takes(3),
        name="finish",
    )(spot, cross, rest, value, embed_t, key_query, query[None], ke)


def normalise(values):
    average = jnp.mean(values, axis=-1, keepdims=True)
    centered = values - average
    variance = jnp.mean(centered * centered, axis=-1, keepdims=True)
    inverse = lax.rsqrt(variance + norm_eps)
    return centered * inverse, inverse


def normalise_back(grad, gain, unit, inverse):
    scaled = grad * gain
    first = jnp.mean(scaled, axis=-1, keepdims=True)
    second = jnp.mean(scaled * unit, axis=-1, keepdims=True)
    return inverse * (scaled - first - unit * second)


def gelu_pair(values):
    below = 0.5 * (1.0 + lax.erf(values * (0.5**0.5)))
    density = jnp.exp(-0.5 * values * values) * ((0.5 / np.pi) ** 0.5)
    return values * below, below + values * density


def columns_half(a, core):
    span = a.shape[1] // 2
    return lax.dynamic_slice_in_dim(a, core * span, span, 1)


def per_device(
    patches,
    var_ids,
    segment_ids,
    pad_mask,
    embed_weight,
    var_embed,
    agg_query,
    key_weight,
    value_weight,
    agg_out_weight,
    agg_out_bias,
    norm_one_gain,
    norm_one_bias,
    qkv_weight,
    attn_out_weight,
    attn_out_bias,
    norm_two_gain,
    norm_two_bias,
    mlp_in_weight,
    mlp_in_bias,
    mlp_out_weight,
    mlp_out_bias,
    cotangent,
):
    rows = patches.shape[0]
    z, p = lax.axis_index("narrow"), lax.axis_index("wide") % SUB
    core = p & 1
    spot = jnp.stack([z, p]).astype(jnp.int32)
    shard = D // 4
    order = Order()
    half = lambda a: columns_half(a, core)
    other_half = lambda a: columns_half(a, 1 - core)

    singles = (
        agg_query,
        agg_out_bias,
        norm_one_gain,
        norm_one_bias,
        attn_out_bias,
        norm_two_gain,
        norm_two_bias,
        mlp_out_bias,
    )
    at_row = lax.broadcasted_iota(jnp.int32, (8, shard), 0)
    vectors = jnp.zeros((8, shard), bf16)
    for i, single in enumerate(singles):
        vectors = jnp.where(at_row == i, single[None, :], vectors)
    vectors = jnp.concatenate([vectors, mlp_in_bias.reshape(4, shard)])
    narrow_v = Narrow(vectors, order)
    narrow_a = Narrow(pieces_of([agg_out_weight], p), order)
    narrow_b = Narrow(pieces_of([qkv_weight, attn_out_weight], p), order)
    narrow_v.second_step()
    narrow_a.second_step()

    line = jnp.arange(COLS, dtype=jnp.int32)
    variable = jnp.where(line < PATCH_COLS, line // PIX, (line - PATCH_COLS) % VARS)
    used = line < PATCH_COLS + VARS
    same = ((variable[:, None] == variable[None, :]) & used[None, :]).astype(f32)
    picks = variable[:, None] == jnp.arange(VARS, dtype=jnp.int32)[None, :]
    chosen = jnp.sum(jnp.where(picks, var_ids[None, :], 0), axis=1)
    source = jnp.where(line < PATCH_COLS, chosen * PIX + line % PIX, chosen + PATCH_COLS)
    source = jnp.where(used, source, -1)
    chooser = (source[:, None] == line[None, :]).astype(bf16)
    embed_rows = jnp.concatenate(
        [embed_weight, var_embed, jnp.zeros((COLS - PATCH_COLS - VARS, shard), bf16)]
    )
    value_part = lax.dynamic_slice_in_dim(value_weight, p * 128, 128, 1)
    table_part = dot(embed_rows, value_part).astype(bf16)

    around = order_narrow(vectors, narrow_v.bundle(), spot)
    whole = [around[:, i].reshape(D) for i in range(8)]
    query_full = whole[0].astype(f32)
    agg_out_b, gain_one, bias_one, attn_out_b, gain_two, bias_two, mlp_out_b = [
        v.astype(f32) for v in whole[1:]
    ]
    mlp_in_b = around[:, 8:].reshape(4 * D).astype(f32)
    head_of = jnp.arange(D, dtype=jnp.int32) // HEAD_DIM
    heads_eye = (jnp.arange(HEADS, dtype=jnp.int32)[:, None] == head_of[None, :]).astype(f32)
    query_rows = (heads_eye * query_full[None, :]).astype(bf16)
    key_query_t = dot_nt(query_rows, key_weight).astype(bf16)
    keys_part = dot_nt(key_query_t, embed_rows) * scale_by
    keys_packed = jnp.concatenate(split_two(keys_part)).reshape(-1, 128)
    packed = jnp.concatenate([table_part, keys_packed])
    order.mark(packed)
    got_packed = [turn_narrow(packed, turn) for turn in (1, 2, 3)]

    full_patches = jnp.concatenate(
        [
            patches,
            jnp.ones((rows, VARS), bf16),
            jnp.zeros((rows, COLS - PATCH_COLS - VARS), bf16),
        ],
        axis=1,
    )
    pixels = lax.dot_general(
        chooser, full_patches, (((0,), (1,)), ((), ())), preferred_element_type=f32
    ).astype(bf16)
    seg_row, seg_col, pad_col = segment_ids, segment_ids.T, pad_mask.T
    cot_half, cot_got = half(cotangent), over_core(other_half(cotangent))

    spread_a = Spread(narrow_a.bundle(), order)
    narrow_b.second_step()
    spread_a.near_step()
    got_packed = order.hold(*got_packed)
    total = packed.astype(f32)
    for part in got_packed:
        total = total + part.astype(f32)
    table_own = total[:COLS].astype(bf16)
    order.mark(table_own)
    keys_two = total[COLS:].reshape(2, HEADS, COLS)
    keys_rows = (keys_two[0] + keys_two[1]).reshape(PAIRS, 2, COLS)
    keys_cols = keys_rows.transpose(0, 2, 1)
    spread_t = Spread(table_own, order)
    spread_t.near_step()
    spread_a.corner_step()
    spread_t.corner_step()
    spread_b = Spread(narrow_b.bundle(), order)
    narrow_c = Narrow(order.hold(pieces_of([mlp_in_weight], p)), order)
    spread_b.near_step()
    spread_t.last_step()
    spread_a.last_step()
    table, table_t = arrange(spread_t.parts(), spot)
    merged = variable_forward(pixels, same, keys_rows, table_t)
    order.mark(merged)
    (agg_out_w,) = assemble([agg_out_weight], spread_a.parts(), spot)
    merged_there = over_core(merged)
    patch_state = dot(merged, agg_out_w) + agg_out_b
    unit_one, inverse_one = normalise(patch_state)
    normed = (unit_one * gain_one + bias_one).astype(bf16)
    order.mark(normed)
    narrow_c.second_step()
    spread_b.corner_step()
    merged_there = order.hold(merged_there)
    spread_b.last_step()
    normed_there = over_core(normed)
    spread_c = Spread(narrow_c.bundle(), order)
    narrow_d = Narrow(order.hold(pieces_of([mlp_out_weight], p)), order)
    spread_c.near_step()
    qkv_w, attn_out_w = assemble([qkv_weight, attn_out_weight], spread_b.parts(), spot)
    project = dot(order.hold(normed), qkv_w).astype(bf16)
    order.mark(project)
    narrow_d.second_step()
    normed_there = order.hold(normed_there)
    attended, logs = attention(order.hold(project), seg_row, seg_col, pad_col)
    order.mark(attended)
    spread_c.corner_step()
    attended_there = over_core(attended)
    spread_d = Spread(narrow_d.bundle(), order)
    residual = patch_state + dot(order.hold(attended), attn_out_w) + attn_out_b
    unit_two, inverse_two = normalise(residual)
    normed_two = (unit_two * gain_two + bias_two).astype(bf16)
    order.mark(normed_two)
    spread_c.last_step()
    spread_d.near_step()
    normed_two_there = over_core(normed_two)
    (mlp_in_w,) = assemble([mlp_in_weight], spread_c.parts(), spot)
    attended_there, normed_two_there = order.hold(attended_there, normed_two_there)
    hidden, slope = mlp_in(order.hold(normed_two), mlp_in_w, mlp_in_b)
    order.mark(hidden)
    hidden_there = over_core(hidden)
    spread_d.corner_step()
    spread_d.last_step()
    (mlp_out_w,) = assemble([mlp_out_weight], spread_d.parts(), spot)

    def grad_of(own, there, own_half, got):
        return (dot_tn(own, own_half) + dot_tn(there, got)).astype(bf16)

    def blocks(a):
        return a.reshape(4, 2, 2, a.shape[0] // 16, a.shape[1])

    cot_float = cotangent.astype(f32)
    pre_half, pre_other, normed_two_grad, pre_sums = mlp_back(
        core[None], order.hold(cotangent), mlp_out_w, mlp_in_w, slope
    )
    order.mark(pre_other)
    pre_got = over_core(pre_other)
    grad_d = blocks(grad_of(*order.hold(hidden, hidden_there), cot_half, cot_got))
    order.mark(grad_d)
    reduce_d = Reduce(grad_d, p, z, order)
    ke_part = lax.dot_general(
        key_weight, embed_rows, (((0,), (1,)), ((), ())), preferred_element_type=f32
    ).astype(bf16)
    ke_part = order.hold(ke_part).reshape(2, 2, shard, COLS)
    ke_kept, ke_got = take(ke_part, z & 1, 1), swap_narrow(take(ke_part, 1 - (z & 1), 1), 1)
    residual_grad = cot_float + normalise_back(
        order.hold(normed_two_grad), gain_two, unit_two, inverse_two
    )
    branch_grad = residual_grad.astype(bf16)
    order.mark(branch_grad)
    branch_got = over_core(other_half(branch_grad))
    grad_c = grad_of(normed_two, normed_two_there, *order.hold(pre_half, pre_got))
    order.mark(grad_c)
    grad_c = jnp.concatenate(
        [grad_c, grad_of(attended, attended_there, *order.hold(half(branch_grad), branch_got))],
        axis=1,
    )
    order.mark(grad_c)
    reduce_c = Reduce(blocks(grad_c), p, z, order)
    attended_grad = dot_nt(order.hold(branch_grad), attn_out_w).astype(bf16)
    order.mark(attended_grad)
    reduce_d.step()
    ke_two = add_two(ke_kept, order.hold(ke_got))
    order.mark(ke_two)
    ke_got = swap_narrow(take(ke_two, 1 - (z >> 1), 0), 2)
    attended_grad = order.hold(attended_grad)
    project_grad = attention_back(project, attended_grad, logs, seg_row, seg_col, pad_col)
    project_other = other_half(project_grad)
    order.mark(project_other)
    project_got = over_core(project_other)
    reduce_d.step()
    ke_own = add_two(take(ke_two, z >> 1, 0), order.hold(ke_got))
    order.mark(ke_own)
    normed_grad = dot_nt(order.hold(project_grad), qkv_w)
    state_grad = residual_grad + normalise_back(normed_grad, gain_one, unit_one, inverse_one)
    state_grad = state_grad.astype(bf16)
    order.mark(state_grad)
    grad_b = grad_of(normed, normed_there, *order.hold(half(project_grad), project_got))
    order.mark(grad_b)
    reduce_b = Reduce(blocks(grad_b), p, z, order)
    state_got = over_core(other_half(state_grad))
    merged_grad = dot_nt(order.hold(state_grad), agg_out_w).astype(bf16)
    order.mark(merged_grad)
    reduce_d.step()
    reduce_c.step()
    merged_grad = order.hold(merged_grad)
    cross, zed, pixel_grad = variable_back(pixels, same, keys_rows, keys_cols, table, merged_grad)
    order.mark(cross)
    reduce_d.step()
    spread_d = Spread(reduce_d.total, order)
    reduce_c.step()
    grad_a = grad_of(merged, merged_there, *order.hold(half(state_grad), state_got))
    order.mark(grad_a)
    zed_parts = split_two(zed.transpose(0, 2, 1).reshape(HEADS, COLS))
    column_sums = [
        jnp.sum(state_grad.astype(f32), axis=0),
        jnp.sum(normed_grad * unit_one, axis=0),
        jnp.sum(normed_grad, axis=0),
        jnp.sum(branch_grad.astype(f32), axis=0),
        jnp.sum(normed_two_grad * unit_two, axis=0),
        jnp.sum(normed_two_grad, axis=0),
        jnp.sum(cot_float, axis=0),
        pre_sums.reshape(-1),
    ]
    sums = jnp.concatenate([v.astype(bf16) for v in column_sums]).reshape(-1, 2 * COLS)
    filler = jnp.zeros((16 * (SUB - 1) - sums.shape[0], 2 * COLS), bf16)
    small = jnp.concatenate([jnp.concatenate(zed_parts, axis=1), sums, filler])
    shared = jnp.concatenate(
        [cross.reshape(SUB, HEAD_DIM, 2 * COLS), small.reshape(SUB, 16, 2 * COLS)], axis=1
    )
    shared = shared.reshape(2, 2, 2, 80, 2 * COLS)
    order.mark(shared)
    shared_got = over_core(take(shared, 1 - core, 0))
    grad_a = grad_a.reshape(4, 2, 2, shard // 4, D // 2).transpose(1, 2, 0, 3, 4)
    grad_a = grad_a.reshape(2, 2, shard, D // 2)
    shared = add_two(take(shared, core, 0), order.hold(shared_got))
    grad_a = jnp.concatenate([grad_a, shared], axis=2)
    order.mark(grad_a)
    reduce_a = ReduceShared(grad_a[None], p, z, order)
    reduce_b.step()
    spread_d.near_step()
    reduce_c.step()
    result = (residual + dot(order.hold(hidden), mlp_out_w) + mlp_out_b).astype(bf16)
    order.mark(result)
    reduce_a.step()
    reduce_b.step()
    reduce_c.step()
    spread_c = Spread(reduce_c.total, order)
    spread_d.corner_step()
    reduce_a.step()
    spread_c.near_step()
    reduce_b.step()
    reduce_a.step()
    spread_d.last_step()
    patches_grad = lax.dot_general(
        order.hold(pixel_grad),
        chooser.astype(f32),
        (((0,), (1,)), ((), ())),
        precision=lax.Precision.HIGHEST,
        preferred_element_type=f32,
    )[:, :PATCH_COLS]
    order.mark(patches_grad)
    reduce_a.step()
    spread_a = Spread(reduce_a.total, order)
    reduce_b.step()
    spread_b = Spread(reduce_b.total, order)
    spread_a.near_step()
    spread_b.near_step()
    spread_c.corner_step()
    (grad_mlp_out_w,) = place(spread_d.parts(), [(D, D)], spot)
    order.mark(grad_mlp_out_w)
    spread_a.corner_step()
    spread_b.corner_step()
    spread_c.last_step()
    spread_a.last_step()
    grad_mlp_in_w, grad_attn_out_w = place(spread_c.parts(), [(shard, 4 * D), (shard, D)], spot)
    order.mark(grad_mlp_in_w)
    spread_b.last_step()
    grad_agg_out_w, cross, rest = place(spread_a.parts(), [(shard, D)], spot, shared=True)
    order.mark(cross)
    (grad_qkv_w,) = place(spread_b.parts(), [(shard, 3 * D)], spot)

    finished = finish(
        spot, cross, rest, value_weight, embed_rows.T, key_query_t.T, query_full, ke_own
    )
    grad_embed, grad_value_w, grad_key_w, grad_agg_query, grad_mlp_in_b = finished[:5]
    grad_agg_query, grad_mlp_in_b = grad_agg_query.reshape(shard), grad_mlp_in_b.reshape(D)
    own = lambda i: finished[5 + i].reshape(shard)

    return (
        result,
        patches_grad,
        grad_embed[:PATCH_COLS],
        grad_embed[PATCH_COLS : PATCH_COLS + VARS],
        grad_agg_query,
        grad_key_w,
        grad_value_w,
        grad_agg_out_w,
        own(0),
        own(1),
        own(2),
        grad_qkv_w,
        grad_attn_out_w,
        own(3),
        own(4),
        own(5),
        grad_mlp_in_w,
        grad_mlp_in_b,
        grad_mlp_out_w,
        own(6),
    )


def solution(mesh):
    rows, shard = P(("wide", "narrow"), None), P("narrow", None)
    wide_shard, vector = P(None, "narrow"), P("narrow")
    return jax.shard_map(
        per_device,
        mesh=mesh,
        in_specs=(
            rows,
            P(),
            rows,
            rows,
            wide_shard,
            wide_shard,
            vector,
            shard,
            shard,
            shard,
            vector,
            vector,
            vector,
            shard,
            shard,
            vector,
            vector,
            vector,
            shard,
            vector,
            shard,
            vector,
            rows,
        ),
        out_specs=(
            rows,
            rows,
            wide_shard,
            wide_shard,
            vector,
            shard,
            shard,
            shard,
            vector,
            vector,
            vector,
            shard,
            shard,
            vector,
            vector,
            vector,
            shard,
            vector,
            shard,
            vector,
        ),
        check_vma=False,
    )
```

```python
import functools

import jax
import jax.numpy as jnp
import numpy as np
from jax import lax
from jax.experimental import pallas as pl
from jax.experimental.pallas import tpu as pltpu
from jax.sharding import PartitionSpec as P

D = 1024
HEADS = 16
HEAD_DIM = 64
VARS = 48
PIX = 4
PATCH_COLS = VARS * PIX
COLS = 256
PAIRS = HEADS // 2
SUB = 8

norm_eps = 1e-06
masked_out = -1e30
scale_by = HEAD_DIM ** (-0.5)
f32 = jnp.float32
bf16 = jnp.bfloat16
MB = 1 << 20


def takes(microseconds):
    flops = int(microseconds * 1.3 * 1e9)
    return pl.CostEstimate(flops=flops, transcendentals=0, bytes_accessed=1)


def dot(a, b):
    return jnp.dot(a, b, preferred_element_type=f32)


def dot_nt(a, b):
    return lax.dot_general(a, b, (((1,), (1,)), ((), ())), preferred_element_type=f32)


def dot_tn(a, b):
    return lax.dot_general(a, b, (((0,), (0,)), ((), ())), preferred_element_type=f32)


def split_two(a):
    high = a.astype(bf16)
    return high, (a - high.astype(f32)).astype(bf16)


def wide_pairs(bits_of):
    return [(i, i ^ bits_of(i)) for i in range(lax.axis_size("wide"))]


def over_core(a):
    return lax.ppermute(a, "wide", wide_pairs(lambda i: 1))


def over_first(a):
    return lax.ppermute(a, "wide", wide_pairs(lambda i: 4 if i & 1 else 2))


def over_second(a):
    return lax.ppermute(a, "wide", wide_pairs(lambda i: 2 if i & 1 else 4))


def turn_narrow(a, by):
    size = lax.axis_size("narrow")
    return lax.ppermute(a, "narrow", [(i, (i + by) % size) for i in range(size)])


def swap_narrow(a, bits):
    size = lax.axis_size("narrow")
    return lax.ppermute(a, "narrow", [(i, i ^ bits) for i in range(size)])


def take(a, at, axis):
    return lax.dynamic_index_in_dim(a, at, axis, keepdims=False, allow_negative_indices=False)


def rows_from(a, start, count, axis):
    return lax.dynamic_slice_in_dim(a, start, count, axis, allow_negative_indices=False)


class Order:
    def __init__(self):
        self.pending = []

    def hold(self, *arrays):
        arrays = lax.optimization_barrier((*arrays, *self.pending))[: len(arrays)]
        self.pending = [arrays[0]]
        return arrays[0] if len(arrays) == 1 else arrays

    def mark(self, array):
        self.pending.append(array)


class Where:
    def __init__(self, order):
        z, p = lax.axis_index("narrow"), lax.axis_index("wide") % SUB
        core, x, y = p & 1, (p >> 1) & 1, p >> 2
        first, second = jnp.where(core == 0, x, y), jnp.where(core == 0, y, x)
        low, high = z & 1, z >> 1
        zero = jnp.zeros_like(z)
        plain = {
            "core": core,
            "other_core": 1 - core,
            "low": low,
            "other_low": 1 - low,
            "high": high,
            "other_high": 1 - high,
            "piece_row": p * (D // 4 // SUB),
            "long_piece_row": p * (D // SUB),
            "half_column": core * (D // 2),
            "other_half_column": (1 - core) * (D // 2),
            "wide_half_column": core * (3 * D // 2),
            "other_wide_half_column": (1 - core) * (3 * D // 2),
            "spot": jnp.stack([z, p]),
            "core_alone": core[None],
            "unsent": (1 - first)[None],
            "second_step": jnp.stack([first, second]),
            "third_step": jnp.stack([zero, low]),
            "fourth_step": jnp.stack([zero, high]),
        }
        for name, value in zip(plain, order.hold(*plain.values())):
            setattr(self, name, value)


class Narrow:
    def __init__(self, own, order):
        self.order = order
        self.own = own
        self.two = swap_narrow(own, 2)

    def second_step(self):
        self.two = self.order.hold(self.two)
        both = jnp.stack([self.own, self.two])
        self.order.mark(both)
        self.others = swap_narrow(both, 1)

    def bundle(self, *more):
        others = self.order.hold(self.others)
        bundle = jnp.concatenate([self.two[None], others, *more])
        self.order.mark(bundle)
        return bundle


class Spread:
    def __init__(self, own, order):
        self.order = order
        self.own = own
        self.other = over_core(own)

    def near_step(self):
        other = self.order.hold(self.other)
        self.other = other
        both = jnp.stack([self.own, other])
        self.order.mark(both)
        self.near = over_first(both)

    def corner_step(self):
        self.near = self.order.hold(self.near)
        corner = self.near[0]
        self.order.mark(corner)
        self.corner = over_second(corner)
        self.far = over_core(self.near)

    def last_step(self):
        self.corner = self.order.hold(self.corner)
        self.order.mark(self.corner)
        self.corner_other = over_core(self.corner)

    def parts(self):
        parts = [self.own, self.other, self.near, self.far, self.corner, self.corner_other]
        return list(self.order.hold(*parts))


def origins(p, parts):
    own, other, near, far, corner, corner_other = parts
    first = 2 + 2 * (p & 1)
    second = 6 - first
    return [
        (p, own),
        (p ^ 1, other),
        (p ^ first, near.at[0]),
        (p ^ first ^ 1, near.at[1]),
        (p ^ second ^ 1, far.at[0]),
        (p ^ second, far.at[1]),
        (p ^ 6, corner),
        (p ^ 7, corner_other),
    ]


def core_and_quarter(place):
    core, x, y = place & 1, (place >> 1) & 1, place >> 2
    return core, jnp.where(core == 0, 2 * x + y, 2 * y + x)


def assemble_kernel(n_shards, spot, *refs):
    shards, parts = refs[:n_shards], refs[n_shards : n_shards + 6]
    fulls, sems = refs[n_shards + 6 : -1], refs[-1]
    z, p = spot[0], spot[1]
    copies = []

    def start(src, dst):
        copy = pltpu.make_async_copy(src, dst, sems.at[len(copies)])
        copy.start()
        copies.append(copy)

    for shard, full in zip(shards, fulls):
        rows = shard.shape[0]
        start(shard, full.at[pl.ds(pl.multiple_of(z * rows, rows), rows), :])
    for place, part in origins(p, parts):
        for i, bits in enumerate((2, 1, 3)):
            origin = z ^ bits
            left = 0
            for full in fulls:
                rows, width = full.shape[0] // 4, full.shape[1]
                count = rows // SUB
                at = pl.multiple_of(origin * rows + place * count, count)
                start(part.at[i, :, left : left + width], full.at[pl.ds(at, count), :])
                left += width
    for copy in copies:
        copy.wait()


def assemble(shards, parts, spot):
    n_copies = 25 * len(shards)
    return pl.pallas_call(
        functools.partial(assemble_kernel, len(shards)),
        out_shape=[jax.ShapeDtypeStruct((4 * s.shape[0], s.shape[1]), s.dtype) for s in shards],
        in_specs=[pl.BlockSpec(memory_space=pltpu.SMEM)]
        + [pl.BlockSpec(memory_space=pl.ANY)] * (len(shards) + 6),
        out_specs=[pl.BlockSpec(memory_space=pltpu.VMEM)] * len(shards),
        scratch_shapes=[pltpu.SemaphoreType.DMA((n_copies,))],
        compiler_params=pltpu.CompilerParams(vmem_limit_bytes=12 * MB),
        cost_estimate=takes(3.5),
        name="assemble",
    )(spot, *shards, *parts)


def pieces_of(shards, start):
    rows = shards[0].shape[0] // SUB
    return jnp.concatenate([rows_from(shard, start, rows, 0) for shard in shards], axis=1)


def beside(a):
    rows = a.shape[0] // 4
    return jnp.concatenate([a[i * rows : (i + 1) * rows] for i in range(4)], axis=1)


def add_two(a, b):
    return (a.astype(f32) + b.astype(f32)).astype(bf16)


def pick_kernel(bits, grad, sent):
    sent[...] = grad[...].reshape(sent.shape)


def pick_first(grad, bits):
    n, _, _, rows, width = grad.shape
    return pl.pallas_call(
        pick_kernel,
        out_shape=jax.ShapeDtypeStruct((n, 2, rows, width), bf16),
        grid_spec=pltpu.PrefetchScalarGridSpec(
            num_scalar_prefetch=1,
            grid=(n,),
            in_specs=[pl.BlockSpec((1, 1, 2, rows, width), lambda i, b: (i, b[0], 0, 0, 0))],
            out_specs=pl.BlockSpec((1, 2, rows, width), lambda i, b: (i, 0, 0, 0)),
        ),
        compiler_params=pltpu.CompilerParams(vmem_limit_bytes=5 * MB),
        cost_estimate=takes(2.5),
        name="pick_first",
    )(bits, grad)


def add_split_kernel(bits, kept_sent, got_sent, kept_kept, got_kept, sent, kept):
    def total(a, b):
        return (a[...].astype(f32).reshape(sent.shape) + b[...].astype(f32).reshape(sent.shape)).astype(bf16)

    sent[...] = total(kept_sent, got_sent)
    kept[...] = total(kept_kept, got_kept)


def add_split(grad, got, bits):
    n, _, _, rows, width = grad.shape
    block = (1, 1, 1, rows, width)
    got_block = (1, 1, rows, width)
    out = jax.ShapeDtypeStruct((n, rows, width), bf16)
    return pl.pallas_call(
        add_split_kernel,
        out_shape=[out, out],
        grid_spec=pltpu.PrefetchScalarGridSpec(
            num_scalar_prefetch=1,
            grid=(n,),
            in_specs=[
                pl.BlockSpec(block, lambda i, b: (i, b[0], 1 - b[1], 0, 0)),
                pl.BlockSpec(got_block, lambda i, b: (i, 1 - b[1], 0, 0)),
                pl.BlockSpec(block, lambda i, b: (i, b[0], b[1], 0, 0)),
                pl.BlockSpec(got_block, lambda i, b: (i, b[1], 0, 0)),
            ],
            out_specs=[pl.BlockSpec((1, rows, width), lambda i, b: (i, 0, 0))] * 2,
        ),
        compiler_params=pltpu.CompilerParams(vmem_limit_bytes=8 * MB),
        cost_estimate=takes(2.5),
        name="add_split",
    )(bits, grad, got, grad, got)


class Reduce:
    def __init__(self, grad, where, order):
        self.where, self.order, self.stage, self.kept = where, order, 0, grad
        sent = pick_first(grad, where.unsent)
        order.mark(sent)
        self.got = over_first(sent)

    def step(self):
        kept, got = self.kept, self.order.hold(self.got)
        self.stage += 1
        if self.stage == 4:
            self.total = across_groups(add_two(kept[0], got[0]))
            self.order.mark(self.total)
            return
        if self.stage > 1:
            rows, width = kept.shape[1:]
            kept = kept.reshape(-1, 1, 2, rows, width)
            got = got.reshape(-1, 2, rows, width)
        where = self.where
        bits = (where.second_step, where.third_step, where.fourth_step)[self.stage - 1]
        sent, self.kept = add_split(kept, got, bits)
        self.order.mark(sent)
        self.got = over_second(sent) if self.stage == 1 else swap_narrow(sent, self.stage - 1)


class ReduceShared(Reduce):
    def step(self):
        if self.stage == 0:
            return super().step()
        total = add_two(self.kept, self.order.hold(self.got))
        self.order.mark(total)
        self.stage += 1
        if self.stage == 4:
            self.total = across_groups(total)
            return
        total = total.reshape(-1, total.shape[-1])
        shape, axis = ((2, 2, 64, -1), 1) if self.stage == 2 else ((2, 64, -1), 0)
        blocks, shared = total[:-80].reshape(shape), total[-80:]

        def pick(bit):
            return jnp.concatenate([take(blocks, bit, axis).reshape(-1, total.shape[-1]), shared])

        where = self.where
        own, other = (where.low, where.other_low) if self.stage == 2 else (where.high, where.other_high)
        sent = pick(other)
        self.order.mark(sent)
        self.kept = pick(own)
        self.got = swap_narrow(sent, self.stage - 1)


def across_groups(a):
    groups = lax.axis_size("wide") // SUB
    if groups == 1:
        return a
    members = [[g * SUB + i for g in range(groups)] for i in range(SUB)]
    return lax.psum(a.astype(f32), "wide", axis_index_groups=members).astype(bf16)


def place_kernel(spans, shared, spot, *refs):
    parts, outs = refs[:6], refs[6:]
    for place, part in origins(spot[1], parts):
        core, quarter = core_and_quarter(place)
        left = 0
        for out, span in zip(outs, spans):
            count = out.shape[0] // 4
            row = pl.multiple_of(quarter * count, 16)
            column = pl.multiple_of(core * span, 128)
            out[pl.ds(row, count), pl.ds(column, span)] = part[
                :count, left : left + span
            ].astype(f32)
            left += span
        if shared:
            pair = core * 4 + quarter
            cross, rest = outs[-2:]
            row = pl.multiple_of(pair * 128, 128)
            cross[pl.ds(row, HEAD_DIM), :] = part[64:128, :COLS]
            cross[pl.ds(row + HEAD_DIM, HEAD_DIM), :] = part[64:128, COLS:]
            rest[pair] = part[128:, :].astype(f32)


def place(parts, shapes, spot, shared=False):
    spans = tuple(s[1] // 2 for s in shapes)
    out_shape = [jax.ShapeDtypeStruct(s, f32) for s in shapes]
    if shared:
        out_shape.append(jax.ShapeDtypeStruct((D, COLS), bf16))
        out_shape.append(jax.ShapeDtypeStruct((SUB, 16, 2 * COLS), f32))
    return pl.pallas_call(
        functools.partial(place_kernel, spans, shared),
        out_shape=out_shape,
        in_specs=[pl.BlockSpec(memory_space=pltpu.SMEM)]
        + [pl.BlockSpec(memory_space=pltpu.VMEM)] * 6,
        out_specs=[pl.BlockSpec(memory_space=pltpu.VMEM)] * len(out_shape),
        compiler_params=pltpu.CompilerParams(vmem_limit_bytes=10 * MB),
        cost_estimate=takes(3),
        name="place",
    )(spot, *parts)


def arrange_kernel(spot, *refs):
    parts, table, table_t = refs[:6], refs[6], refs[7]
    for place, part in origins(spot[1], parts):
        at = pl.ds(pl.multiple_of(place * 128, 128), 128)
        rows = jnp.concatenate([part[3, :, i * COLS : (i + 1) * COLS] for i in range(4)], axis=0)
        table_t[at, :] = rows
        table[:, at] = rows.astype(f32).T.astype(bf16)


def arrange(parts, spot):
    return pl.pallas_call(
        arrange_kernel,
        out_shape=[
            jax.ShapeDtypeStruct((COLS, D), bf16),
            jax.ShapeDtypeStruct((D, COLS), bf16),
        ],
        in_specs=[pl.BlockSpec(memory_space=pltpu.SMEM)]
        + [pl.BlockSpec(memory_space=pltpu.VMEM)] * 6,
        out_specs=[pl.BlockSpec(memory_space=pltpu.VMEM)] * 2,
        name="arrange",
    )(spot, *parts)


def order_kernel(spot, own, others, out):
    out[spot[0]] = own[...]
    for i, bits in enumerate((2, 1, 3)):
        out[spot[0] ^ bits] = others[i]


def order_narrow(own, others, spot):
    return pl.pallas_call(
        order_kernel,
        out_shape=jax.ShapeDtypeStruct((4, *own.shape), own.dtype),
        in_specs=[pl.BlockSpec(memory_space=pltpu.SMEM)]
        + [pl.BlockSpec(memory_space=pltpu.VMEM)] * 2,
        out_specs=pl.BlockSpec(memory_space=pltpu.VMEM),
        name="order",
    )(spot, own, others)


def pair_probs(pixels, same, keys_row):
    high, low = split_two(same * keys_row)
    scores = dot(high, pixels) + dot(low, pixels)
    biggest = jnp.max(scores[PATCH_COLS : PATCH_COLS + VARS], axis=0, keepdims=True)
    raised = jnp.exp(scores - biggest)
    total = jnp.sum(raised[PATCH_COLS : PATCH_COLS + VARS], axis=0, keepdims=True)
    return raised * (1.0 / total)


def variable_kernel(pixels_ref, same_ref, keys_ref, table_ref, merged_ref):
    pixels = pixels_ref[...]
    pixels_wide = pixels.astype(f32)
    same = same_ref[...]
    parts = []
    for i in range(2):
        probs = pair_probs(pixels, same, keys_ref[0, i : i + 1, :])
        weighted = (probs * pixels_wide).astype(bf16)
        parts.append(dot(table_ref[i * HEAD_DIM : (i + 1) * HEAD_DIM, :], weighted))
    merged_ref[...] = jnp.concatenate(parts, axis=0).T.astype(bf16)


def variable_forward(pixels, same, keys_rows, table_t):
    rows = pixels.shape[1]
    return pl.pallas_call(
        variable_kernel,
        out_shape=jax.ShapeDtypeStruct((rows, D), bf16),
        grid=(PAIRS,),
        in_specs=[
            pl.BlockSpec((COLS, rows), lambda h: (0, 0)),
            pl.BlockSpec((COLS, COLS), lambda h: (0, 0)),
            pl.BlockSpec((1, 2, COLS), lambda h: (h, 0, 0)),
            pl.BlockSpec((128, COLS), lambda h: (h, 0)),
        ],
        out_specs=pl.BlockSpec((rows, 128), lambda h: (0, h)),
        compiler_params=pltpu.CompilerParams(vmem_limit_bytes=8 * MB),
        cost_estimate=takes(9),
        name="variable_forward",
    )(pixels, same, keys_rows, table_t)


def variable_back_kernel(
    pixels_ref, same_ref, keys_ref, keys_col_ref, table_ref, grad_ref, x_ref, zed_ref, pixel_ref, zed_columns
):
    step = pl.program_id(0)

    @pl.when(step == 0)
    def _():
        zed_columns[...] = jnp.zeros_like(zed_columns)

    pixels = pixels_ref[...]
    pixels_wide = pixels.astype(f32)
    same = same_ref[...]
    same_low = same.astype(bf16)
    grad_t = grad_ref[...].astype(f32).T.astype(bf16)
    line = lax.broadcasted_iota(jnp.int32, zed_columns.shape, 1)
    pixel_grad = None
    for i in range(2):
        probs = pair_probs(pixels, same, keys_ref[0, i : i + 1, :])
        weighted = (probs * pixels_wide).astype(bf16)
        grad_i = grad_t[i * HEAD_DIM : (i + 1) * HEAD_DIM, :]
        spread = dot(table_ref[:, i * HEAD_DIM : (i + 1) * HEAD_DIM], grad_i)
        high, low = split_two(spread * pixels_wide)
        prob_grad = dot(same_low, high) + dot(same_low, low)
        lifted = probs * prob_grad
        centre = jnp.sum(lifted[PATCH_COLS : PATCH_COLS + VARS], axis=0, keepdims=True)
        score_grad = lifted - probs * centre
        x_ref[:, i * COLS : (i + 1) * COLS] = dot_nt(grad_i, weighted).astype(bf16)
        sums = jnp.sum(score_grad * pixels_wide, axis=1, keepdims=True)
        zed_columns[...] += jnp.where(line == 2 * step + i, sums, 0.0)
        term = probs * spread + score_grad * keys_col_ref[0, :, i : i + 1]
        pixel_grad = term if pixel_grad is None else pixel_grad + term

    @pl.when(step == 0)
    def _():
        pixel_ref[...] = pixel_grad

    @pl.when(step > 0)
    def _():
        pixel_ref[...] += pixel_grad

    @pl.when(step == PAIRS - 1)
    def _():
        zed_ref[...] = zed_columns[...].T[:HEADS]


def variable_back(pixels, same, keys_rows, keys_cols, table, grad):
    rows = pixels.shape[1]
    return pl.pallas_call(
        variable_back_kernel,
        out_shape=[
            jax.ShapeDtypeStruct((D // 2, 2 * COLS), bf16),
            jax.ShapeDtypeStruct((HEADS, COLS), f32),
            jax.ShapeDtypeStruct((COLS, rows), f32),
        ],
        grid=(PAIRS,),
        in_specs=[
            pl.BlockSpec((COLS, rows), lambda h: (0, 0)),
            pl.BlockSpec((COLS, COLS), lambda h: (0, 0)),
            pl.BlockSpec((1, 2, COLS), lambda h: (h, 0, 0)),
            pl.BlockSpec((1, COLS, 2), lambda h: (h, 0, 0)),
            pl.BlockSpec((COLS, 128), lambda h: (0, h)),
            pl.BlockSpec((rows, 128), lambda h: (0, h)),
        ],
        out_specs=[
            pl.BlockSpec((HEAD_DIM, 2 * COLS), lambda h: (h, 0)),
            pl.BlockSpec((HEADS, COLS), lambda h: (0, 0)),
            pl.BlockSpec((COLS, rows), lambda h: (0, 0)),
        ],
        scratch_shapes=[pltpu.VMEM((COLS, 128), f32)],
        compiler_params=pltpu.CompilerParams(vmem_limit_bytes=10 * MB),
        cost_estimate=takes(1),
        name="variable_back",
    )(pixels, same, keys_rows, keys_cols, table, grad)


def mask_rows(segment_col, segment_row, padding_col, rows):
    key_at = lax.broadcasted_iota(jnp.int32, (rows, rows), 0)
    query_at = lax.broadcasted_iota(jnp.int32, (rows, rows), 1)
    allowed = (segment_col == segment_row) & ((padding_col == 1) | (key_at == query_at))
    return jnp.where(allowed, 0.0, masked_out).astype(f32)


def attention_kernel(q_ref, k_ref, v_ref, seg_row, seg_col, pad_col, out_ref, log_ref, mask_ref):
    rows = q_ref.shape[0]

    @pl.when(pl.program_id(0) == 0)
    def _():
        mask_ref[...] = mask_rows(seg_col[...], seg_row[...], pad_col[...], rows)

    q_t = (q_ref[...].astype(f32) * scale_by).T.astype(bf16)
    v_t = v_ref[...].astype(f32).T.astype(bf16)
    outs, logs = [], []
    for i in range(2):
        span = slice(i * HEAD_DIM, (i + 1) * HEAD_DIM)
        scores = dot(k_ref[:, span], q_t[span, :]) + mask_ref[...]
        biggest = jnp.max(scores, axis=0, keepdims=True)
        raised = jnp.exp(scores - biggest)
        total = jnp.sum(raised, axis=0, keepdims=True)
        outs.append(dot(v_t[span, :], raised.astype(bf16)) * (1.0 / total))
        logs.append(biggest + jnp.log(total))
    out_ref[...] = jnp.concatenate(outs, axis=0).T.astype(bf16)
    log_ref[0] = jnp.concatenate(logs, axis=0)


def attention(project, seg_row, seg_col, pad_col):
    rows = project.shape[0]
    column = lambda first: pl.BlockSpec((rows, 128), lambda h: (0, first * PAIRS + h))
    return pl.pallas_call(
        attention_kernel,
        out_shape=[
            jax.ShapeDtypeStruct((rows, D), bf16),
            jax.ShapeDtypeStruct((PAIRS, 2, rows), f32),
        ],
        grid=(PAIRS,),
        in_specs=[
            column(0),
            column(1),
            column(2),
            pl.BlockSpec((1, rows), lambda h: (0, 0)),
            pl.BlockSpec((rows, 1), lambda h: (0, 0)),
            pl.BlockSpec((rows, 1), lambda h: (0, 0)),
        ],
        out_specs=[column(0), pl.BlockSpec((1, 2, rows), lambda h: (h, 0, 0))],
        scratch_shapes=[pltpu.VMEM((rows, rows), f32)],
        compiler_params=pltpu.CompilerParams(vmem_limit_bytes=8 * MB),
        cost_estimate=takes(12.5),
        name="attention",
    )(project, project, project, seg_row, seg_col, pad_col)


def attention_back_kernel(
    q_ref, k_ref, v_ref, grad_ref, log_ref, seg_row, seg_col, pad_col, out_ref, mask_ref
):
    rows = q_ref.shape[0]
    step = pl.program_id(0)

    @pl.when(step == 0)
    def _():
        mask_ref[...] = mask_rows(seg_col[...], seg_row[...], pad_col[...], rows)

    q_scaled = q_ref[...].astype(f32) * scale_by
    q_low = q_scaled.astype(bf16)
    q_t = q_scaled.T.astype(bf16)
    k_t = (k_ref[...].astype(f32) * scale_by).T.astype(bf16)
    grad_t = grad_ref[...].astype(f32).T.astype(bf16)
    q_grads, k_grads, v_grads = [], [], []
    for i in range(2):
        span = slice(i * HEAD_DIM, (i + 1) * HEAD_DIM)
        scores = dot(k_ref[:, span], q_t[span, :]) + mask_ref[...]
        probs = jnp.exp(scores - log_ref[0, i : i + 1, :])
        prob_grad = dot(v_ref[:, span], grad_t[span, :])
        lifted = probs * prob_grad
        centre = jnp.sum(lifted, axis=0, keepdims=True)
        score_grad = (lifted - probs * centre).astype(bf16)
        v_grads.append(dot(probs.astype(bf16), grad_ref[:, span]))
        k_grads.append(dot(score_grad, q_low[:, span]))
        q_grads.append(dot(k_t[span, :], score_grad))
    at = lambda first: pl.ds(pl.multiple_of(first * D + step * 128, 128), 128)
    out_ref[:, at(0)] = jnp.concatenate(q_grads, axis=0).T.astype(bf16)
    out_ref[:, at(1)] = jnp.concatenate(k_grads, axis=1).astype(bf16)
    out_ref[:, at(2)] = jnp.concatenate(v_grads, axis=1).astype(bf16)


def attention_back(project, grad, logs, seg_row, seg_col, pad_col):
    rows = project.shape[0]
    column = lambda first: pl.BlockSpec((rows, 128), lambda h: (0, first * PAIRS + h))
    return pl.pallas_call(
        attention_back_kernel,
        out_shape=jax.ShapeDtypeStruct((rows, 3 * D), bf16),
        grid=(PAIRS,),
        in_specs=[
            column(0),
            column(1),
            column(2),
            column(0),
            pl.BlockSpec((1, 2, rows), lambda h: (h, 0, 0)),
            pl.BlockSpec((1, rows), lambda h: (0, 0)),
            pl.BlockSpec((rows, 1), lambda h: (0, 0)),
            pl.BlockSpec((rows, 1), lambda h: (0, 0)),
        ],
        out_specs=pl.BlockSpec((rows, 3 * D), lambda h: (0, 0)),
        scratch_shapes=[pltpu.VMEM((rows, rows), f32)],
        compiler_params=pltpu.CompilerParams(vmem_limit_bytes=14 * MB),
        cost_estimate=takes(16.5),
        name="attention_back",
    )(project, project, project, grad, logs, seg_row, seg_col, pad_col)


def mlp_in_kernel(rows_ref, weight, bias, hidden, slope):
    value, change = gelu_pair(dot(rows_ref[...], weight[...]) + bias[...])
    hidden[...] = value.astype(bf16)
    slope[...] = change.astype(bf16)


def mlp_in(rows_in, weight, bias):
    rows, hidden = rows_in.shape[0], weight.shape[1]
    block = 512
    columns = lambda count: pl.BlockSpec((count, block), lambda i: (0, i))
    return pl.pallas_call(
        mlp_in_kernel,
        out_shape=[jax.ShapeDtypeStruct((rows, hidden), bf16)] * 2,
        grid=(hidden // block,),
        in_specs=[pl.BlockSpec((rows, D), lambda i: (0, 0)), columns(D), columns(1)],
        out_specs=[columns(rows)] * 2,
        compiler_params=pltpu.CompilerParams(vmem_limit_bytes=14 * MB),
        cost_estimate=takes(11),
        name="mlp_in",
    )(rows_in, weight, bias[None])


def mlp_back_kernel(core, cot, w_out, w_in, slope, own, other, grad, sums):
    step = pl.program_id(0)
    pre = (dot_nt(cot[...], w_out[...]) * slope[...].astype(f32)).astype(bf16)
    sums[0] = jnp.sum(pre.astype(f32), axis=0, keepdims=True)
    part = dot_nt(pre, w_in[...])

    @pl.when(step < 2)
    def _():
        other[...] = pre

    @pl.when(step >= 2)
    def _():
        own[...] = pre

    @pl.when(step == 0)
    def _():
        grad[...] = part

    @pl.when(step > 0)
    def _():
        grad[...] += part


def mlp_back(core, cot, w_out, w_in, slope):
    rows, hidden = cot.shape[0], w_out.shape[0]
    block = hidden // 4
    at = lambda i, c: lax.rem(i + 2 - 2 * c[0], 4)
    return pl.pallas_call(
        mlp_back_kernel,
        out_shape=[
            jax.ShapeDtypeStruct((rows, hidden // 2), bf16),
            jax.ShapeDtypeStruct((rows, hidden // 2), bf16),
            jax.ShapeDtypeStruct((rows, D), f32),
            jax.ShapeDtypeStruct((4, 1, block), f32),
        ],
        grid_spec=pltpu.PrefetchScalarGridSpec(
            num_scalar_prefetch=1,
            grid=(4,),
            in_specs=[
                pl.BlockSpec((rows, D), lambda i, c: (0, 0)),
                pl.BlockSpec((block, D), lambda i, c: (at(i, c), 0)),
                pl.BlockSpec((D, block), lambda i, c: (0, at(i, c))),
                pl.BlockSpec((rows, block), lambda i, c: (0, at(i, c))),
            ],
            out_specs=[
                pl.BlockSpec((rows, block), lambda i, c: (0, jnp.maximum(i - 2, 0))),
                pl.BlockSpec((rows, block), lambda i, c: (0, jnp.minimum(i, 1))),
                pl.BlockSpec((rows, D), lambda i, c: (0, 0)),
                pl.BlockSpec((1, 1, block), lambda i, c: (at(i, c), 0, 0)),
            ],
        ),
        compiler_params=pltpu.CompilerParams(vmem_limit_bytes=24 * MB),
        cost_estimate=takes(15.5),
        name="mlp_back",
    )(core, cot, w_out, w_in, slope)


def finish_kernel(
    spot, cross, rest, value, embed_t, key_query, query, ke, embed_out, value_out, key_out, query_out, bias_out, *sums_out
):
    z = spot[0]
    summed = cross[...]
    zed = rest[0, :, :COLS] + rest[0, :, COLS:]
    zed_both = split_two(zed)
    embed_grad = dot(value[...], summed)
    query_grad = 0.0
    per_head = 0.0
    for part in zed_both:
        embed_grad += dot(key_query[...], part) * scale_by
        query_grad += dot_nt(embed_t[...], part) * scale_by
        per_head += dot_nt(part, ke[...]) * scale_by
    embed_out[...] = embed_grad.T
    value_out[...] = dot_nt(embed_t[...], summed)
    head = lax.broadcasted_iota(jnp.int32, (HEADS, D), 0)
    line = lax.broadcasted_iota(jnp.int32, (HEADS, D), 1)
    eye = (head == line // HEAD_DIM).astype(bf16)
    high, low = split_two(query_grad)
    key_out[...] = (dot(high, eye) + dot(low, eye)) * query[...]
    head = lax.broadcasted_iota(jnp.int32, per_head.shape, 0)
    line = lax.broadcasted_iota(jnp.int32, per_head.shape, 1)
    mine = head == z * 4 + line // HEAD_DIM
    query_out[...] = jnp.sum(jnp.where(mine, per_head, 0.0), axis=0, keepdims=True)
    column = pl.multiple_of((z & 1) * COLS, COLS)
    for i, out in enumerate(sums_out):
        at = 16 + 2 * i + (z >> 1)
        out[...] = rest[at // 16, pl.ds(lax.rem(at, 16), 1), pl.ds(column, COLS)]
    for i in range(2):
        at = 16 + 14 + 2 * z + i
        bias_out[pl.ds(i, 1), :] = rest[at // 16, pl.ds(lax.rem(at, 16), 1), :]


def finish(spot, cross, rest, value, embed_t, key_query, query, ke):
    shard = value.shape[0]
    row = jax.ShapeDtypeStruct((1, shard), f32)
    out_shape = [
        jax.ShapeDtypeStruct((COLS, shard), f32),
        jax.ShapeDtypeStruct((shard, D), f32),
        jax.ShapeDtypeStruct((shard, D), f32),
        row,
        jax.ShapeDtypeStruct((2, 2 * COLS), f32),
    ] + [row] * 7
    return pl.pallas_call(
        finish_kernel,
        out_shape=out_shape,
        in_specs=[pl.BlockSpec(memory_space=pltpu.SMEM)]
        + [pl.BlockSpec(memory_space=pltpu.VMEM)] * 7,
        out_specs=[pl.BlockSpec(memory_space=pltpu.VMEM)] * len(out_shape),
        compiler_params=pltpu.CompilerParams(vmem_limit_bytes=12 * MB),
        cost_estimate=takes(3),
        name="finish",
    )(spot, cross, rest, value, embed_t, key_query, query[None], ke)


def normalise(values):
    average = jnp.mean(values, axis=-1, keepdims=True)
    centered = values - average
    variance = jnp.mean(centered * centered, axis=-1, keepdims=True)
    inverse = lax.rsqrt(variance + norm_eps)
    return centered * inverse, inverse


def normalise_back(grad, gain, unit, inverse):
    scaled = grad * gain
    first = jnp.mean(scaled, axis=-1, keepdims=True)
    second = jnp.mean(scaled * unit, axis=-1, keepdims=True)
    return inverse * (scaled - first - unit * second)


def gelu_pair(values):
    below = 0.5 * (1.0 + lax.erf(values * (0.5**0.5)))
    density = jnp.exp(-0.5 * values * values) * ((0.5 / np.pi) ** 0.5)
    return values * below, below + values * density


def per_device(
    patches,
    var_ids,
    segment_ids,
    pad_mask,
    embed_weight,
    var_embed,
    agg_query,
    key_weight,
    value_weight,
    agg_out_weight,
    agg_out_bias,
    norm_one_gain,
    norm_one_bias,
    qkv_weight,
    attn_out_weight,
    attn_out_bias,
    norm_two_gain,
    norm_two_bias,
    mlp_in_weight,
    mlp_in_bias,
    mlp_out_weight,
    mlp_out_bias,
    cotangent,
):
    rows = patches.shape[0]
    shard = D // 4
    order = Order()
    where = Where(order)
    spot = where.spot

    def half(a):
        span = a.shape[1] // 2
        return rows_from(a, where.half_column if span == D // 2 else where.wide_half_column, span, 1)

    def other_half(a):
        span = a.shape[1] // 2
        start = where.other_half_column if span == D // 2 else where.other_wide_half_column
        return rows_from(a, start, span, 1)

    singles = (
        agg_query,
        agg_out_bias,
        norm_one_gain,
        norm_one_bias,
        attn_out_bias,
        norm_two_gain,
        norm_two_bias,
        mlp_out_bias,
    )
    at_row = lax.broadcasted_iota(jnp.int32, (8, shard), 0)
    vectors = jnp.zeros((8, shard), bf16)
    for i, single in enumerate(singles):
        vectors = jnp.where(at_row == i, single[None, :], vectors)
    vectors = jnp.concatenate([vectors, mlp_in_bias.reshape(4, shard)])
    narrow_v = Narrow(vectors, order)
    narrow_a = Narrow(pieces_of([agg_out_weight], where.piece_row), order)
    narrow_b = Narrow(pieces_of([qkv_weight, attn_out_weight], where.piece_row), order)
    narrow_v.second_step()
    narrow_a.second_step()
    narrow_b.second_step()

    line = jnp.arange(COLS, dtype=jnp.int32)
    variable = jnp.where(line < PATCH_COLS, line // PIX, (line - PATCH_COLS) % VARS)
    used = line < PATCH_COLS + VARS
    same = ((variable[:, None] == variable[None, :]) & used[None, :]).astype(f32)
    picks = variable[:, None] == jnp.arange(VARS, dtype=jnp.int32)[None, :]
    chosen = jnp.sum(jnp.where(picks, var_ids[None, :], 0), axis=1)
    source = jnp.where(line < PATCH_COLS, chosen * PIX + line % PIX, chosen + PATCH_COLS)
    source = jnp.where(used, source, -1)
    chooser = (source[:, None] == line[None, :]).astype(bf16)
    embed_rows = jnp.concatenate(
        [embed_weight, var_embed, jnp.zeros((COLS - PATCH_COLS - VARS, shard), bf16)]
    )
    value_part = rows_from(value_weight, where.long_piece_row, 128, 1)
    table_part = lax.dot_general(
        value_part, embed_rows, (((0,), (1,)), ((), ())), preferred_element_type=f32
    )
    table_part = beside(table_part.astype(bf16))

    around = order_narrow(vectors, narrow_v.bundle(), spot)
    whole = [around[:, i].reshape(D) for i in range(8)]
    query_full = whole[0].astype(f32)
    agg_out_b, gain_one, bias_one, attn_out_b, gain_two, bias_two, mlp_out_b = [
        v.astype(f32) for v in whole[1:]
    ]
    mlp_in_b = around[:, 8:].reshape(4 * D).astype(f32)
    head_of = jnp.arange(D, dtype=jnp.int32) // HEAD_DIM
    heads_eye = (jnp.arange(HEADS, dtype=jnp.int32)[:, None] == head_of[None, :]).astype(f32)
    query_rows = (heads_eye * query_full[None, :]).astype(bf16)
    key_query_t = dot_nt(query_rows, key_weight).astype(bf16)
    keys_part = dot_nt(key_query_t, embed_rows) * scale_by
    packed = jnp.concatenate([table_part, beside(jnp.concatenate(split_two(keys_part)))])
    order.mark(packed)
    got_packed = [turn_narrow(packed, turn) for turn in (1, 2, 3)]

    same, chooser = order.hold(same, chooser)
    agg_out_b, gain_one, bias_one, attn_out_b, gain_two, bias_two, mlp_out_b, mlp_in_b = order.hold(
        agg_out_b, gain_one, bias_one, attn_out_b, gain_two, bias_two, mlp_out_b, mlp_in_b
    )
    piece_c = pieces_of([mlp_in_weight], where.piece_row)
    piece_d = pieces_of([mlp_out_weight], where.long_piece_row)
    order.mark(piece_c)
    order.mark(piece_d)

    full_patches = jnp.concatenate(
        [
            patches,
            jnp.ones((rows, VARS), bf16),
            jnp.zeros((rows, COLS - PATCH_COLS - VARS), bf16),
        ],
        axis=1,
    )
    pixels = lax.dot_general(
        chooser, full_patches, (((0,), (1,)), ((), ())), preferred_element_type=f32
    ).astype(bf16)
    seg_row, seg_col, pad_col = order.hold(segment_ids, segment_ids.T, pad_mask.T)
    pixels = order.hold(pixels)
    cot_half, cot_other = order.hold(half(cotangent), other_half(cotangent))
    cot_got = over_core(cot_other)

    got_packed = order.hold(*got_packed)
    total = packed.astype(f32)
    for part in got_packed:
        total = total + part.astype(f32)
    table_own = total[:32].astype(bf16)
    order.mark(table_own)
    keys_two = jnp.concatenate([total[32:, i * COLS : (i + 1) * COLS] for i in range(4)])
    keys_rows = (keys_two[:HEADS] + keys_two[HEADS:]).reshape(PAIRS, 2, COLS)
    keys_cols = keys_rows.transpose(0, 2, 1)
    spread_a = Spread(narrow_a.bundle(table_own[None]), order)
    spread_b = Spread(narrow_b.bundle(), order)
    narrow_c = Narrow(order.hold(piece_c), order)
    spread_a.near_step()
    spread_a.corner_step()
    spread_b.near_step()
    spread_a.last_step()
    parts_a = spread_a.parts()
    table, table_t = arrange(parts_a, spot)
    narrow_c.second_step()
    spread_b.corner_step()
    merged = variable_forward(pixels, same, keys_rows, order.hold(table_t))
    order.mark(merged)
    merged_there = over_core(merged)
    (agg_out_w,) = assemble([agg_out_weight], parts_a, spot)
    patch_state = dot(merged, agg_out_w) + agg_out_b
    unit_one, inverse_one = normalise(patch_state)
    normed = (unit_one * gain_one + bias_one).astype(bf16)
    order.mark(normed)
    merged_there = order.hold(merged_there)
    spread_c = Spread(narrow_c.bundle(), order)
    narrow_d = Narrow(order.hold(piece_d), order)
    spread_b.last_step()
    spread_c.near_step()
    normed_there = over_core(normed)
    qkv_w, attn_out_w = assemble([qkv_weight, attn_out_weight], spread_b.parts(), spot)
    project = dot(order.hold(normed), qkv_w).astype(bf16)
    order.mark(project)
    narrow_d.second_step()
    normed_there = order.hold(normed_there)
    attended, logs = attention(order.hold(project), seg_row, seg_col, pad_col)
    order.mark(attended)
    spread_c.corner_step()
    spread_d = Spread(narrow_d.bundle(), order)
    attended_there = over_core(attended)
    residual = patch_state + dot(order.hold(attended), attn_out_w) + attn_out_b
    unit_two, inverse_two = normalise(residual)
    normed_two = (unit_two * gain_two + bias_two).astype(bf16)
    order.mark(normed_two)
    spread_d.near_step()
    spread_c.last_step()
    normed_two_there = over_core(normed_two)
    (mlp_in_w,) = assemble([mlp_in_weight], spread_c.parts(), spot)
    attended_there, normed_two_there = order.hold(attended_there, normed_two_there)
    hidden, slope = mlp_in(order.hold(normed_two), mlp_in_w, mlp_in_b)
    order.mark(hidden)
    hidden_there = over_core(hidden)
    spread_d.corner_step()

    def grad_of(own, there, own_half, got):
        return (dot_tn(own, own_half) + dot_tn(there, got)).astype(bf16)

    def blocks(a):
        return a.reshape(4, 2, 2, a.shape[0] // 16, a.shape[1])

    cot_float = cotangent.astype(f32)
    spread_d.last_step()
    (mlp_out_w,) = assemble([mlp_out_weight], spread_d.parts(), spot)
    pre_half, pre_other, normed_two_grad, pre_sums = mlp_back(
        where.core_alone, order.hold(cotangent), mlp_out_w, mlp_in_w, slope
    )
    order.mark(pre_other)
    grad_d = blocks(grad_of(*order.hold(hidden, hidden_there), cot_half, cot_got))
    order.mark(grad_d)
    reduce_d = Reduce(grad_d, where, order)
    pre_got = over_core(pre_other)
    ke_part = lax.dot_general(
        key_weight, embed_rows, (((0,), (1,)), ((), ())), preferred_element_type=f32
    ).astype(bf16)
    ke_part = order.hold(ke_part).reshape(2, 2, shard, COLS)
    ke_kept, ke_got = take(ke_part, where.low, 1), swap_narrow(take(ke_part, where.other_low, 1), 1)
    residual_grad = cot_float + normalise_back(
        order.hold(normed_two_grad), gain_two, unit_two, inverse_two
    )
    branch_grad = residual_grad.astype(bf16)
    order.mark(branch_grad)
    branch_got = over_core(other_half(branch_grad))
    grad_c = grad_of(normed_two, normed_two_there, *order.hold(pre_half, pre_got))
    order.mark(grad_c)
    grad_c = jnp.concatenate(
        [grad_c, grad_of(attended, attended_there, *order.hold(half(branch_grad), branch_got))],
        axis=1,
    )
    order.mark(grad_c)
    reduce_c = Reduce(blocks(grad_c), where, order)
    attended_grad = dot_nt(order.hold(branch_grad), attn_out_w).astype(bf16)
    order.mark(attended_grad)
    reduce_d.step()
    ke_two = add_two(ke_kept, order.hold(ke_got))
    order.mark(ke_two)
    ke_got = swap_narrow(take(ke_two, where.other_high, 0), 2)
    attended_grad = order.hold(attended_grad)
    project_grad = attention_back(project, attended_grad, logs, seg_row, seg_col, pad_col)
    order.mark(project_grad)
    reduce_d.step()
    project_other = other_half(order.hold(project_grad))
    order.mark(project_other)
    project_got = over_core(project_other)
    reduce_c.step()
    ke_own = add_two(take(ke_two, where.high, 0), order.hold(ke_got))
    order.mark(ke_own)
    grad_b = grad_of(normed, normed_there, *order.hold(half(project_grad), project_got))
    order.mark(grad_b)
    reduce_b = Reduce(blocks(grad_b), where, order)
    normed_grad = dot_nt(order.hold(project_grad), qkv_w)
    state_grad = residual_grad + normalise_back(normed_grad, gain_one, unit_one, inverse_one)
    state_grad = state_grad.astype(bf16)
    order.mark(state_grad)
    state_got = over_core(other_half(state_grad))
    reduce_d.step()
    merged_grad = dot_nt(order.hold(state_grad), agg_out_w).astype(bf16)
    order.mark(merged_grad)
    merged_grad = order.hold(merged_grad)
    cross, zed, pixel_grad = variable_back(pixels, same, keys_rows, keys_cols, table, merged_grad)
    order.mark(cross)
    reduce_c.step()
    reduce_d.step()
    spread_d = Spread(reduce_d.total, order)
    reduce_b.step()
    grad_a = grad_of(merged, merged_there, *order.hold(half(state_grad), state_got))
    order.mark(grad_a)
    zed_parts = split_two(zed)
    column_sums = [
        jnp.sum(state_grad.astype(f32), axis=0),
        jnp.sum(normed_grad * unit_one, axis=0),
        jnp.sum(normed_grad, axis=0),
        jnp.sum(branch_grad.astype(f32), axis=0),
        jnp.sum(normed_two_grad * unit_two, axis=0),
        jnp.sum(normed_two_grad, axis=0),
        jnp.sum(cot_float, axis=0),
        pre_sums.reshape(-1),
    ]
    sums = jnp.concatenate([v.astype(bf16) for v in column_sums]).reshape(-1, 2 * COLS)
    filler = jnp.zeros((16 * (SUB - 1) - sums.shape[0], 2 * COLS), bf16)
    small = jnp.concatenate([jnp.concatenate(zed_parts, axis=1), sums, filler])
    shared = jnp.concatenate(
        [cross.reshape(SUB, HEAD_DIM, 2 * COLS), small.reshape(SUB, 16, 2 * COLS)], axis=1
    )
    shared = shared.reshape(2, 2, 2, 80, 2 * COLS)
    order.mark(shared)
    shared_got = over_core(take(shared, where.other_core, 0))
    grad_a = grad_a.reshape(4, 2, 2, shard // 4, D // 2).transpose(1, 2, 0, 3, 4)
    grad_a = grad_a.reshape(2, 2, shard, D // 2)
    shared = add_two(take(shared, where.core, 0), order.hold(shared_got))
    grad_a = jnp.concatenate([grad_a, shared], axis=2)
    order.mark(grad_a)
    reduce_a = ReduceShared(grad_a[None], where, order)
    spread_d.near_step()
    reduce_c.step()
    reduce_a.step()
    reduce_b.step()
    reduce_c.step()
    spread_c = Spread(reduce_c.total, order)
    spread_d.corner_step()
    reduce_a.step()
    spread_c.near_step()
    reduce_a.step()
    reduce_b.step()
    spread_d.last_step()
    result = (residual + dot(order.hold(hidden), mlp_out_w) + mlp_out_b).astype(bf16)
    order.mark(result)
    patches_grad = lax.dot_general(
        order.hold(pixel_grad),
        chooser.astype(f32),
        (((0,), (1,)), ((), ())),
        precision=lax.Precision.HIGHEST,
        preferred_element_type=f32,
    )[:, :PATCH_COLS]
    order.mark(patches_grad)
    reduce_a.step()
    spread_a = Spread(reduce_a.total, order)
    reduce_b.step()
    spread_b = Spread(reduce_b.total, order)
    spread_a.near_step()
    spread_b.near_step()
    spread_c.corner_step()
    (grad_mlp_out_w,) = place(spread_d.parts(), [(D, D)], spot)
    order.mark(grad_mlp_out_w)
    spread_a.corner_step()
    spread_b.corner_step()
    spread_c.last_step()
    spread_a.last_step()
    grad_mlp_in_w, grad_attn_out_w = place(spread_c.parts(), [(shard, 4 * D), (shard, D)], spot)
    order.mark(grad_mlp_in_w)
    spread_b.last_step()
    grad_agg_out_w, cross, rest = place(spread_a.parts(), [(shard, D)], spot, shared=True)
    order.mark(cross)
    (grad_qkv_w,) = place(spread_b.parts(), [(shard, 3 * D)], spot)

    finished = finish(
        spot, cross, rest, value_weight, embed_rows.T, key_query_t.T, query_full, ke_own
    )
    grad_embed, grad_value_w, grad_key_w, grad_agg_query, grad_mlp_in_b = finished[:5]
    grad_agg_query, grad_mlp_in_b = grad_agg_query.reshape(shard), grad_mlp_in_b.reshape(D)
    own = lambda i: finished[5 + i].reshape(shard)

    return (
        result,
        patches_grad,
        grad_embed[:PATCH_COLS],
        grad_embed[PATCH_COLS : PATCH_COLS + VARS],
        grad_agg_query,
        grad_key_w,
        grad_value_w,
        grad_agg_out_w,
        own(0),
        own(1),
        own(2),
        grad_qkv_w,
        grad_attn_out_w,
        own(3),
        own(4),
        own(5),
        grad_mlp_in_w,
        grad_mlp_in_b,
        grad_mlp_out_w,
        own(6),
    )


def solution(mesh):
    rows, shard = P(("wide", "narrow"), None), P("narrow", None)
    wide_shard, vector = P(None, "narrow"), P("narrow")
    return jax.shard_map(
        per_device,
        mesh=mesh,
        in_specs=(
            rows,
            P(),
            rows,
            rows,
            wide_shard,
            wide_shard,
            vector,
            shard,
            shard,
            shard,
            vector,
            vector,
            vector,
            shard,
            shard,
            vector,
            vector,
            vector,
            shard,
            vector,
            shard,
            vector,
            rows,
        ),
        out_specs=(
            rows,
            rows,
            wide_shard,
            wide_shard,
            vector,
            shard,
            shard,
            shard,
            vector,
            vector,
            vector,
            shard,
            shard,
            vector,
            vector,
            vector,
            shard,
            vector,
            shard,
            vector,
        ),
        check_vma=False,
    )
```

```python
import functools

import jax
import jax.numpy as jnp
import numpy as np
from jax import lax
from jax.experimental import pallas as pl
from jax.experimental.pallas import tpu as pltpu
from jax.sharding import PartitionSpec as P

D = 1024
HEADS = 16
HEAD_DIM = 64
VARS = 48
PIX = 4
PATCH_COLS = VARS * PIX
COLS = 256
PAIRS = HEADS // 2
SUB = 8

norm_eps = 1e-06
masked_out = -1e30
scale_by = HEAD_DIM ** (-0.5)
f32 = jnp.float32
bf16 = jnp.bfloat16
MB = 1 << 20


def takes(microseconds):
    flops = int(microseconds * 1.8 * 1e9)
    return pl.CostEstimate(flops=flops, transcendentals=0, bytes_accessed=1)


def dot(a, b):
    return jnp.dot(a, b, preferred_element_type=f32)


def dot_nt(a, b):
    return lax.dot_general(a, b, (((1,), (1,)), ((), ())), preferred_element_type=f32)


def dot_tn(a, b):
    return lax.dot_general(a, b, (((0,), (0,)), ((), ())), preferred_element_type=f32)


def split_two(a):
    high = a.astype(bf16)
    return high, (a - high.astype(f32)).astype(bf16)


def wide_pairs(bits_of):
    return [(i, i ^ bits_of(i)) for i in range(lax.axis_size("wide"))]


def over_core(a):
    return lax.ppermute(a, "wide", wide_pairs(lambda i: 1))


def over_first(a):
    return lax.ppermute(a, "wide", wide_pairs(lambda i: 4 if i & 1 else 2))


def over_second(a):
    return lax.ppermute(a, "wide", wide_pairs(lambda i: 2 if i & 1 else 4))


def turn_narrow(a, by):
    size = lax.axis_size("narrow")
    return lax.ppermute(a, "narrow", [(i, (i + by) % size) for i in range(size)])


def swap_narrow(a, bits):
    size = lax.axis_size("narrow")
    return lax.ppermute(a, "narrow", [(i, i ^ bits) for i in range(size)])


def take(a, at, axis):
    return lax.dynamic_index_in_dim(a, at, axis, keepdims=False, allow_negative_indices=False)


def rows_from(a, start, count, axis):
    return lax.dynamic_slice_in_dim(a, start, count, axis, allow_negative_indices=False)


class Order:
    def __init__(self):
        self.pending = []

    def hold(self, *arrays):
        arrays = lax.optimization_barrier((*arrays, *self.pending))[: len(arrays)]
        self.pending = [arrays[0]]
        return arrays[0] if len(arrays) == 1 else arrays

    def mark(self, array):
        self.pending.append(array)


class Where:
    def __init__(self, order):
        z, p = lax.axis_index("narrow"), lax.axis_index("wide") % SUB
        core, x, y = p & 1, (p >> 1) & 1, p >> 2
        first, second = jnp.where(core == 0, x, y), jnp.where(core == 0, y, x)
        low, high = z & 1, z >> 1
        zero = jnp.zeros_like(z)
        plain = {
            "core": core,
            "other_core": 1 - core,
            "low": low,
            "other_low": 1 - low,
            "high": high,
            "other_high": 1 - high,
            "piece_row": p * (D // 4 // SUB),
            "long_piece_row": p * (D // SUB),
            "half_column": core * (D // 2),
            "other_half_column": (1 - core) * (D // 2),
            "wide_half_column": core * (3 * D // 2),
            "other_wide_half_column": (1 - core) * (3 * D // 2),
            "spot": jnp.stack([z, p]),
            "core_alone": core[None],
            "unsent": (1 - first)[None],
            "second_step": jnp.stack([first, second]),
            "third_step": jnp.stack([zero, low]),
            "fourth_step": jnp.stack([zero, high]),
        }
        for name, value in zip(plain, order.hold(*plain.values())):
            setattr(self, name, value)


class Narrow:
    def __init__(self, own, order):
        self.order = order
        self.own = own
        self.two = swap_narrow(own, 2)

    def second_step(self):
        self.two = self.order.hold(self.two)
        both = jnp.stack([self.own, self.two])
        self.order.mark(both)
        self.others = swap_narrow(both, 1)

    def bundle(self, *more):
        others = self.order.hold(self.others)
        bundle = jnp.concatenate([self.two[None], others, *more])
        self.order.mark(bundle)
        return bundle


class Spread:
    def __init__(self, own, order):
        self.order = order
        self.own = own
        self.other = over_core(own)

    def near_step(self):
        other = self.order.hold(self.other)
        self.other = other
        both = jnp.stack([self.own, other])
        self.order.mark(both)
        self.near = over_first(both)

    def corner_step(self):
        self.near = self.order.hold(self.near)
        corner = self.near[0]
        self.order.mark(corner)
        self.corner = over_second(corner)
        self.far = over_core(self.near)

    def last_step(self):
        self.corner = self.order.hold(self.corner)
        self.order.mark(self.corner)
        self.corner_other = over_core(self.corner)

    def parts(self):
        parts = [self.own, self.other, self.near, self.far, self.corner, self.corner_other]
        return list(self.order.hold(*parts))


def origins(p, parts):
    own, other, near, far, corner, corner_other = parts
    first = 2 + 2 * (p & 1)
    second = 6 - first
    return [
        (p, own),
        (p ^ 1, other),
        (p ^ first, near.at[0]),
        (p ^ first ^ 1, near.at[1]),
        (p ^ second ^ 1, far.at[0]),
        (p ^ second, far.at[1]),
        (p ^ 6, corner),
        (p ^ 7, corner_other),
    ]


def core_and_quarter(place):
    core, x, y = place & 1, (place >> 1) & 1, place >> 2
    return core, jnp.where(core == 0, 2 * x + y, 2 * y + x)


def assemble_kernel(n_shards, spot, *refs):
    shards, parts = refs[:n_shards], refs[n_shards : n_shards + 6]
    fulls, sems = refs[n_shards + 6 : -1], refs[-1]
    z, p = spot[0], spot[1]
    copies = []

    def start(src, dst):
        copy = pltpu.make_async_copy(src, dst, sems.at[len(copies)])
        copy.start()
        copies.append(copy)

    for shard, full in zip(shards, fulls):
        rows = shard.shape[0]
        start(shard, full.at[pl.ds(pl.multiple_of(z * rows, rows), rows), :])
    for place, part in origins(p, parts):
        for i, bits in enumerate((2, 1, 3)):
            origin = z ^ bits
            left = 0
            for full in fulls:
                rows, width = full.shape[0] // 4, full.shape[1]
                count = rows // SUB
                at = pl.multiple_of(origin * rows + place * count, count)
                start(part.at[i, :, left : left + width], full.at[pl.ds(at, count), :])
                left += width
    for copy in copies:
        copy.wait()


def assemble(shards, parts, spot):
    n_copies = 25 * len(shards)
    return pl.pallas_call(
        functools.partial(assemble_kernel, len(shards)),
        out_shape=[jax.ShapeDtypeStruct((4 * s.shape[0], s.shape[1]), s.dtype) for s in shards],
        in_specs=[pl.BlockSpec(memory_space=pltpu.SMEM)]
        + [pl.BlockSpec(memory_space=pl.ANY)] * (len(shards) + 6),
        out_specs=[pl.BlockSpec(memory_space=pltpu.VMEM)] * len(shards),
        scratch_shapes=[pltpu.SemaphoreType.DMA((n_copies,))],
        compiler_params=pltpu.CompilerParams(vmem_limit_bytes=12 * MB),
        cost_estimate=takes(3.5),
        name="assemble",
    )(spot, *shards, *parts)


def pieces_of(shards, start):
    rows = shards[0].shape[0] // SUB
    return jnp.concatenate([rows_from(shard, start, rows, 0) for shard in shards], axis=1)


def beside(a):
    rows = a.shape[0] // 4
    return jnp.concatenate([a[i * rows : (i + 1) * rows] for i in range(4)], axis=1)


def add_two(a, b):
    return (a.astype(f32) + b.astype(f32)).astype(bf16)


def pick_kernel(bits, grad, sent):
    sent[...] = grad[...].reshape(sent.shape)


def pick_first(grad, bits):
    n, _, _, rows, width = grad.shape
    return pl.pallas_call(
        pick_kernel,
        out_shape=jax.ShapeDtypeStruct((n, 2, rows, width), bf16),
        grid_spec=pltpu.PrefetchScalarGridSpec(
            num_scalar_prefetch=1,
            grid=(n,),
            in_specs=[pl.BlockSpec((1, 1, 2, rows, width), lambda i, b: (i, b[0], 0, 0, 0))],
            out_specs=pl.BlockSpec((1, 2, rows, width), lambda i, b: (i, 0, 0, 0)),
        ),
        compiler_params=pltpu.CompilerParams(vmem_limit_bytes=5 * MB),
        cost_estimate=takes(2.5),
        name="pick_first",
    )(bits, grad)


def add_split_kernel(bits, kept_sent, got_sent, kept_kept, got_kept, sent, kept):
    def total(a, b):
        return (a[...].astype(f32).reshape(sent.shape) + b[...].astype(f32).reshape(sent.shape)).astype(bf16)

    sent[...] = total(kept_sent, got_sent)
    kept[...] = total(kept_kept, got_kept)


def add_split(grad, got, bits):
    n, _, _, rows, width = grad.shape
    block = (1, 1, 1, rows, width)
    got_block = (1, 1, rows, width)
    out = jax.ShapeDtypeStruct((n, rows, width), bf16)
    return pl.pallas_call(
        add_split_kernel,
        out_shape=[out, out],
        grid_spec=pltpu.PrefetchScalarGridSpec(
            num_scalar_prefetch=1,
            grid=(n,),
            in_specs=[
                pl.BlockSpec(block, lambda i, b: (i, b[0], 1 - b[1], 0, 0)),
                pl.BlockSpec(got_block, lambda i, b: (i, 1 - b[1], 0, 0)),
                pl.BlockSpec(block, lambda i, b: (i, b[0], b[1], 0, 0)),
                pl.BlockSpec(got_block, lambda i, b: (i, b[1], 0, 0)),
            ],
            out_specs=[pl.BlockSpec((1, rows, width), lambda i, b: (i, 0, 0))] * 2,
        ),
        compiler_params=pltpu.CompilerParams(vmem_limit_bytes=8 * MB),
        cost_estimate=takes(2.5),
        name="add_split",
    )(bits, grad, got, grad, got)


class Reduce:
    def __init__(self, grad, where, order):
        self.where, self.order, self.stage, self.kept = where, order, 0, grad
        sent = pick_first(grad, where.unsent)
        order.mark(sent)
        self.got = over_first(sent)

    def step(self):
        kept, got = self.kept, self.order.hold(self.got)
        self.stage += 1
        if self.stage == 4:
            self.total = across_groups(add_two(kept[0], got[0]))
            self.order.mark(self.total)
            return
        if self.stage > 1:
            rows, width = kept.shape[1:]
            kept = kept.reshape(-1, 1, 2, rows, width)
            got = got.reshape(-1, 2, rows, width)
        where = self.where
        bits = (where.second_step, where.third_step, where.fourth_step)[self.stage - 1]
        sent, self.kept = add_split(kept, got, bits)
        self.order.mark(sent)
        self.got = over_second(sent) if self.stage == 1 else swap_narrow(sent, self.stage - 1)


class ReduceShared(Reduce):
    def step(self):
        if self.stage == 0:
            return super().step()
        total = add_two(self.kept, self.order.hold(self.got))
        self.order.mark(total)
        self.stage += 1
        if self.stage == 4:
            self.total = across_groups(total)
            return
        total = total.reshape(-1, total.shape[-1])
        shape, axis = ((2, 2, 64, -1), 1) if self.stage == 2 else ((2, 64, -1), 0)
        blocks, shared = total[:-80].reshape(shape), total[-80:]

        def pick(bit):
            return jnp.concatenate([take(blocks, bit, axis).reshape(-1, total.shape[-1]), shared])

        where = self.where
        own, other = (where.low, where.other_low) if self.stage == 2 else (where.high, where.other_high)
        sent = pick(other)
        self.order.mark(sent)
        self.kept = pick(own)
        self.got = swap_narrow(sent, self.stage - 1)


def across_groups(a):
    groups = lax.axis_size("wide") // SUB
    if groups == 1:
        return a
    members = [[g * SUB + i for g in range(groups)] for i in range(SUB)]
    return lax.psum(a.astype(f32), "wide", axis_index_groups=members).astype(bf16)


def place_kernel(spans, shared, spot, *refs):
    parts, outs = refs[:6], refs[6:]
    for place, part in origins(spot[1], parts):
        core, quarter = core_and_quarter(place)
        left = 0
        for out, span in zip(outs, spans):
            count = out.shape[0] // 4
            row = pl.multiple_of(quarter * count, 16)
            column = pl.multiple_of(core * span, 128)
            out[pl.ds(row, count), pl.ds(column, span)] = part[
                :count, left : left + span
            ].astype(f32)
            left += span
        if shared:
            pair = core * 4 + quarter
            cross, rest = outs[-2:]
            row = pl.multiple_of(pair * 128, 128)
            cross[pl.ds(row, HEAD_DIM), :] = part[64:128, :COLS]
            cross[pl.ds(row + HEAD_DIM, HEAD_DIM), :] = part[64:128, COLS:]
            rest[pair] = part[128:, :].astype(f32)


def place(parts, shapes, spot, shared=False):
    spans = tuple(s[1] // 2 for s in shapes)
    out_shape = [jax.ShapeDtypeStruct(s, f32) for s in shapes]
    if shared:
        out_shape.append(jax.ShapeDtypeStruct((D, COLS), bf16))
        out_shape.append(jax.ShapeDtypeStruct((SUB, 16, 2 * COLS), f32))
    return pl.pallas_call(
        functools.partial(place_kernel, spans, shared),
        out_shape=out_shape,
        in_specs=[pl.BlockSpec(memory_space=pltpu.SMEM)]
        + [pl.BlockSpec(memory_space=pltpu.VMEM)] * 6,
        out_specs=[pl.BlockSpec(memory_space=pltpu.VMEM)] * len(out_shape),
        compiler_params=pltpu.CompilerParams(vmem_limit_bytes=10 * MB),
        cost_estimate=takes(3),
        name="place",
    )(spot, *parts)


def arrange_kernel(spot, *refs):
    parts, table, table_t = refs[:6], refs[6], refs[7]
    for place, part in origins(spot[1], parts):
        at = pl.ds(pl.multiple_of(place * 128, 128), 128)
        rows = jnp.concatenate([part[3, :, i * COLS : (i + 1) * COLS] for i in range(4)], axis=0)
        table_t[at, :] = rows
        table[:, at] = rows.astype(f32).T.astype(bf16)


def arrange(parts, spot):
    return pl.pallas_call(
        arrange_kernel,
        out_shape=[
            jax.ShapeDtypeStruct((COLS, D), bf16),
            jax.ShapeDtypeStruct((D, COLS), bf16),
        ],
        in_specs=[pl.BlockSpec(memory_space=pltpu.SMEM)]
        + [pl.BlockSpec(memory_space=pltpu.VMEM)] * 6,
        out_specs=[pl.BlockSpec(memory_space=pltpu.VMEM)] * 2,
        name="arrange",
    )(spot, *parts)


def order_kernel(spot, own, others, out):
    out[spot[0]] = own[...]
    for i, bits in enumerate((2, 1, 3)):
        out[spot[0] ^ bits] = others[i]


def order_narrow(own, others, spot):
    return pl.pallas_call(
        order_kernel,
        out_shape=jax.ShapeDtypeStruct((4, *own.shape), own.dtype),
        in_specs=[pl.BlockSpec(memory_space=pltpu.SMEM)]
        + [pl.BlockSpec(memory_space=pltpu.VMEM)] * 2,
        out_specs=pl.BlockSpec(memory_space=pltpu.VMEM),
        name="order",
    )(spot, own, others)


def pair_probs(pixels, same, keys_row):
    high, low = split_two(same * keys_row)
    scores = dot(high, pixels) + dot(low, pixels)
    biggest = jnp.max(scores[PATCH_COLS : PATCH_COLS + VARS], axis=0, keepdims=True)
    raised = jnp.exp(scores - biggest)
    total = jnp.sum(raised[PATCH_COLS : PATCH_COLS + VARS], axis=0, keepdims=True)
    return raised * (1.0 / total)


def variable_kernel(pixels_ref, same_ref, keys_ref, table_ref, merged_ref):
    pixels = pixels_ref[...]
    pixels_wide = pixels.astype(f32)
    same = same_ref[...]
    parts = []
    for i in range(2):
        probs = pair_probs(pixels, same, keys_ref[0, i : i + 1, :])
        weighted = (probs * pixels_wide).astype(bf16)
        parts.append(dot(table_ref[i * HEAD_DIM : (i + 1) * HEAD_DIM, :], weighted))
    merged_ref[...] = jnp.concatenate(parts, axis=0).T.astype(bf16)


def variable_forward(pixels, same, keys_rows, table_t):
    rows = pixels.shape[1]
    return pl.pallas_call(
        variable_kernel,
        out_shape=jax.ShapeDtypeStruct((rows, D), bf16),
        grid=(PAIRS,),
        in_specs=[
            pl.BlockSpec((COLS, rows), lambda h: (0, 0)),
            pl.BlockSpec((COLS, COLS), lambda h: (0, 0)),
            pl.BlockSpec((1, 2, COLS), lambda h: (h, 0, 0)),
            pl.BlockSpec((128, COLS), lambda h: (h, 0)),
        ],
        out_specs=pl.BlockSpec((rows, 128), lambda h: (0, h)),
        compiler_params=pltpu.CompilerParams(vmem_limit_bytes=8 * MB),
        cost_estimate=takes(4),
        name="variable_forward",
    )(pixels, same, keys_rows, table_t)


def variable_back_kernel(
    pixels_ref, same_ref, keys_ref, keys_col_ref, table_ref, grad_ref, x_ref, zed_ref, pixel_ref, zed_columns
):
    step = pl.program_id(0)

    @pl.when(step == 0)
    def _():
        zed_columns[...] = jnp.zeros_like(zed_columns)

    pixels = pixels_ref[...]
    pixels_wide = pixels.astype(f32)
    same = same_ref[...]
    same_low = same.astype(bf16)
    grad_t = grad_ref[...].astype(f32).T.astype(bf16)
    line = lax.broadcasted_iota(jnp.int32, zed_columns.shape, 1)
    pixel_grad = None
    for i in range(2):
        probs = pair_probs(pixels, same, keys_ref[0, i : i + 1, :])
        weighted = (probs * pixels_wide).astype(bf16)
        grad_i = grad_t[i * HEAD_DIM : (i + 1) * HEAD_DIM, :]
        spread = dot(table_ref[:, i * HEAD_DIM : (i + 1) * HEAD_DIM], grad_i)
        high, low = split_two(spread * pixels_wide)
        prob_grad = dot(same_low, high) + dot(same_low, low)
        lifted = probs * prob_grad
        centre = jnp.sum(lifted[PATCH_COLS : PATCH_COLS + VARS], axis=0, keepdims=True)
        score_grad = lifted - probs * centre
        x_ref[:, i * COLS : (i + 1) * COLS] = dot_nt(grad_i, weighted).astype(bf16)
        sums = jnp.sum(score_grad * pixels_wide, axis=1, keepdims=True)
        zed_columns[...] += jnp.where(line == 2 * step + i, sums, 0.0)
        term = probs * spread + score_grad * keys_col_ref[0, :, i : i + 1]
        pixel_grad = term if pixel_grad is None else pixel_grad + term

    @pl.when(step == 0)
    def _():
        pixel_ref[...] = pixel_grad

    @pl.when(step > 0)
    def _():
        pixel_ref[...] += pixel_grad

    @pl.when(step == PAIRS - 1)
    def _():
        zed_ref[...] = zed_columns[...].T[:HEADS]


def variable_back(pixels, same, keys_rows, keys_cols, table, grad):
    rows = pixels.shape[1]
    return pl.pallas_call(
        variable_back_kernel,
        out_shape=[
            jax.ShapeDtypeStruct((D // 2, 2 * COLS), bf16),
            jax.ShapeDtypeStruct((HEADS, COLS), f32),
            jax.ShapeDtypeStruct((COLS, rows), f32),
        ],
        grid=(PAIRS,),
        in_specs=[
            pl.BlockSpec((COLS, rows), lambda h: (0, 0)),
            pl.BlockSpec((COLS, COLS), lambda h: (0, 0)),
            pl.BlockSpec((1, 2, COLS), lambda h: (h, 0, 0)),
            pl.BlockSpec((1, COLS, 2), lambda h: (h, 0, 0)),
            pl.BlockSpec((COLS, 128), lambda h: (0, h)),
            pl.BlockSpec((rows, 128), lambda h: (0, h)),
        ],
        out_specs=[
            pl.BlockSpec((HEAD_DIM, 2 * COLS), lambda h: (h, 0)),
            pl.BlockSpec((HEADS, COLS), lambda h: (0, 0)),
            pl.BlockSpec((COLS, rows), lambda h: (0, 0)),
        ],
        scratch_shapes=[pltpu.VMEM((COLS, 128), f32)],
        compiler_params=pltpu.CompilerParams(vmem_limit_bytes=10 * MB),
        cost_estimate=takes(1),
        name="variable_back",
    )(pixels, same, keys_rows, keys_cols, table, grad)


def mask_rows(segment_col, segment_row, padding_col, rows):
    key_at = lax.broadcasted_iota(jnp.int32, (rows, rows), 0)
    query_at = lax.broadcasted_iota(jnp.int32, (rows, rows), 1)
    allowed = (segment_col == segment_row) & ((padding_col == 1) | (key_at == query_at))
    return jnp.where(allowed, 0.0, masked_out).astype(f32)


def attention_kernel(q_ref, k_ref, v_ref, seg_row, seg_col, pad_col, out_ref, log_ref, mask_ref):
    rows = q_ref.shape[0]

    @pl.when(pl.program_id(0) == 0)
    def _():
        mask_ref[...] = mask_rows(seg_col[...], seg_row[...], pad_col[...], rows)

    q_t = (q_ref[...].astype(f32) * scale_by).T.astype(bf16)
    v_t = v_ref[...].astype(f32).T.astype(bf16)
    outs, logs = [], []
    for i in range(2):
        span = slice(i * HEAD_DIM, (i + 1) * HEAD_DIM)
        scores = dot(k_ref[:, span], q_t[span, :]) + mask_ref[...]
        biggest = jnp.max(scores, axis=0, keepdims=True)
        raised = jnp.exp(scores - biggest)
        total = jnp.sum(raised, axis=0, keepdims=True)
        outs.append(dot(v_t[span, :], raised.astype(bf16)) * (1.0 / total))
        logs.append(biggest + jnp.log(total))
    out_ref[...] = jnp.concatenate(outs, axis=0).T.astype(bf16)
    log_ref[0] = jnp.concatenate(logs, axis=0)


def attention(project, seg_row, seg_col, pad_col):
    rows = project.shape[0]
    column = lambda first: pl.BlockSpec((rows, 128), lambda h: (0, first * PAIRS + h))
    return pl.pallas_call(
        attention_kernel,
        out_shape=[
            jax.ShapeDtypeStruct((rows, D), bf16),
            jax.ShapeDtypeStruct((PAIRS, 2, rows), f32),
        ],
        grid=(PAIRS,),
        in_specs=[
            column(0),
            column(1),
            column(2),
            pl.BlockSpec((1, rows), lambda h: (0, 0)),
            pl.BlockSpec((rows, 1), lambda h: (0, 0)),
            pl.BlockSpec((rows, 1), lambda h: (0, 0)),
        ],
        out_specs=[column(0), pl.BlockSpec((1, 2, rows), lambda h: (h, 0, 0))],
        scratch_shapes=[pltpu.VMEM((rows, rows), f32)],
        compiler_params=pltpu.CompilerParams(vmem_limit_bytes=8 * MB),
        cost_estimate=takes(12.5),
        name="attention",
    )(project, project, project, seg_row, seg_col, pad_col)


def attention_back_kernel(
    q_ref, k_ref, v_ref, grad_ref, log_ref, seg_row, seg_col, pad_col, out_ref, mask_ref
):
    rows = q_ref.shape[0]
    step = pl.program_id(0)

    @pl.when(step == 0)
    def _():
        mask_ref[...] = mask_rows(seg_col[...], seg_row[...], pad_col[...], rows)

    q_scaled = q_ref[...].astype(f32) * scale_by
    q_low = q_scaled.astype(bf16)
    q_t = q_scaled.T.astype(bf16)
    k_t = (k_ref[...].astype(f32) * scale_by).T.astype(bf16)
    grad_t = grad_ref[...].astype(f32).T.astype(bf16)
    q_grads, k_grads, v_grads = [], [], []
    for i in range(2):
        span = slice(i * HEAD_DIM, (i + 1) * HEAD_DIM)
        scores = dot(k_ref[:, span], q_t[span, :]) + mask_ref[...]
        probs = jnp.exp(scores - log_ref[0, i : i + 1, :])
        prob_grad = dot(v_ref[:, span], grad_t[span, :])
        lifted = probs * prob_grad
        centre = jnp.sum(lifted, axis=0, keepdims=True)
        score_grad = (lifted - probs * centre).astype(bf16)
        v_grads.append(dot(probs.astype(bf16), grad_ref[:, span]))
        k_grads.append(dot(score_grad, q_low[:, span]))
        q_grads.append(dot(k_t[span, :], score_grad))
    at = lambda first: pl.ds(pl.multiple_of(first * D + step * 128, 128), 128)
    out_ref[:, at(0)] = jnp.concatenate(q_grads, axis=0).T.astype(bf16)
    out_ref[:, at(1)] = jnp.concatenate(k_grads, axis=1).astype(bf16)
    out_ref[:, at(2)] = jnp.concatenate(v_grads, axis=1).astype(bf16)


def attention_back(project, grad, logs, seg_row, seg_col, pad_col):
    rows = project.shape[0]
    column = lambda first: pl.BlockSpec((rows, 128), lambda h: (0, first * PAIRS + h))
    return pl.pallas_call(
        attention_back_kernel,
        out_shape=jax.ShapeDtypeStruct((rows, 3 * D), bf16),
        grid=(PAIRS,),
        in_specs=[
            column(0),
            column(1),
            column(2),
            column(0),
            pl.BlockSpec((1, 2, rows), lambda h: (h, 0, 0)),
            pl.BlockSpec((1, rows), lambda h: (0, 0)),
            pl.BlockSpec((rows, 1), lambda h: (0, 0)),
            pl.BlockSpec((rows, 1), lambda h: (0, 0)),
        ],
        out_specs=pl.BlockSpec((rows, 3 * D), lambda h: (0, 0)),
        scratch_shapes=[pltpu.VMEM((rows, rows), f32)],
        compiler_params=pltpu.CompilerParams(vmem_limit_bytes=14 * MB),
        cost_estimate=takes(16.5),
        name="attention_back",
    )(project, project, project, grad, logs, seg_row, seg_col, pad_col)


def mlp_in_kernel(rows_ref, weight, bias, hidden, slope):
    value, change = gelu_pair(dot(rows_ref[...], weight[...]) + bias[...])
    hidden[...] = value.astype(bf16)
    slope[...] = change.astype(bf16)


def mlp_in(rows_in, weight, bias):
    rows, hidden = rows_in.shape[0], weight.shape[1]
    block = 512
    columns = lambda count: pl.BlockSpec((count, block), lambda i: (0, i))
    return pl.pallas_call(
        mlp_in_kernel,
        out_shape=[jax.ShapeDtypeStruct((rows, hidden), bf16)] * 2,
        grid=(hidden // block,),
        in_specs=[pl.BlockSpec((rows, D), lambda i: (0, 0)), columns(D), columns(1)],
        out_specs=[columns(rows)] * 2,
        compiler_params=pltpu.CompilerParams(vmem_limit_bytes=14 * MB),
        cost_estimate=takes(11),
        name="mlp_in",
    )(rows_in, weight, bias[None])


def mlp_back_kernel(core, cot, w_out, w_in, slope, own, other, grad, sums):
    step = pl.program_id(0)
    pre = (dot_nt(cot[...], w_out[...]) * slope[...].astype(f32)).astype(bf16)
    sums[0] = jnp.sum(pre.astype(f32), axis=0, keepdims=True)
    part = dot_nt(pre, w_in[...])

    @pl.when(step < 2)
    def _():
        other[...] = pre

    @pl.when(step >= 2)
    def _():
        own[...] = pre

    @pl.when(step == 0)
    def _():
        grad[...] = part

    @pl.when(step > 0)
    def _():
        grad[...] += part


def mlp_back(core, cot, w_out, w_in, slope):
    rows, hidden = cot.shape[0], w_out.shape[0]
    block = hidden // 4
    at = lambda i, c: lax.rem(i + 2 - 2 * c[0], 4)
    return pl.pallas_call(
        mlp_back_kernel,
        out_shape=[
            jax.ShapeDtypeStruct((rows, hidden // 2), bf16),
            jax.ShapeDtypeStruct((rows, hidden // 2), bf16),
            jax.ShapeDtypeStruct((rows, D), f32),
            jax.ShapeDtypeStruct((4, 1, block), f32),
        ],
        grid_spec=pltpu.PrefetchScalarGridSpec(
            num_scalar_prefetch=1,
            grid=(4,),
            in_specs=[
                pl.BlockSpec((rows, D), lambda i, c: (0, 0)),
                pl.BlockSpec((block, D), lambda i, c: (at(i, c), 0)),
                pl.BlockSpec((D, block), lambda i, c: (0, at(i, c))),
                pl.BlockSpec((rows, block), lambda i, c: (0, at(i, c))),
            ],
            out_specs=[
                pl.BlockSpec((rows, block), lambda i, c: (0, jnp.maximum(i - 2, 0))),
                pl.BlockSpec((rows, block), lambda i, c: (0, jnp.minimum(i, 1))),
                pl.BlockSpec((rows, D), lambda i, c: (0, 0)),
                pl.BlockSpec((1, 1, block), lambda i, c: (at(i, c), 0, 0)),
            ],
        ),
        compiler_params=pltpu.CompilerParams(vmem_limit_bytes=24 * MB),
        cost_estimate=takes(15.5),
        name="mlp_back",
    )(core, cot, w_out, w_in, slope)


def finish_kernel(
    spot, cross, rest, value, embed_t, key_query, query, ke, embed_out, value_out, key_out, query_out, bias_out, *sums_out
):
    z = spot[0]
    summed = cross[...]
    zed = rest[0, :, :COLS] + rest[0, :, COLS:]
    zed_both = split_two(zed)
    embed_grad = dot(value[...], summed)
    query_grad = 0.0
    per_head = 0.0
    for part in zed_both:
        embed_grad += dot(key_query[...], part) * scale_by
        query_grad += dot_nt(embed_t[...], part) * scale_by
        per_head += dot_nt(part, ke[...]) * scale_by
    embed_out[...] = embed_grad.T
    value_out[...] = dot_nt(embed_t[...], summed)
    head = lax.broadcasted_iota(jnp.int32, (HEADS, D), 0)
    line = lax.broadcasted_iota(jnp.int32, (HEADS, D), 1)
    eye = (head == line // HEAD_DIM).astype(bf16)
    high, low = split_two(query_grad)
    key_out[...] = (dot(high, eye) + dot(low, eye)) * query[...]
    head = lax.broadcasted_iota(jnp.int32, per_head.shape, 0)
    line = lax.broadcasted_iota(jnp.int32, per_head.shape, 1)
    mine = head == z * 4 + line // HEAD_DIM
    query_out[...] = jnp.sum(jnp.where(mine, per_head, 0.0), axis=0, keepdims=True)
    column = pl.multiple_of((z & 1) * COLS, COLS)
    for i, out in enumerate(sums_out):
        at = 16 + 2 * i + (z >> 1)
        out[...] = rest[at // 16, pl.ds(lax.rem(at, 16), 1), pl.ds(column, COLS)]
    for i in range(2):
        at = 16 + 14 + 2 * z + i
        bias_out[pl.ds(i, 1), :] = rest[at // 16, pl.ds(lax.rem(at, 16), 1), :]


def finish(spot, cross, rest, value, embed_t, key_query, query, ke):
    shard = value.shape[0]
    row = jax.ShapeDtypeStruct((1, shard), f32)
    out_shape = [
        jax.ShapeDtypeStruct((COLS, shard), f32),
        jax.ShapeDtypeStruct((shard, D), f32),
        jax.ShapeDtypeStruct((shard, D), f32),
        row,
        jax.ShapeDtypeStruct((2, 2 * COLS), f32),
    ] + [row] * 7
    return pl.pallas_call(
        finish_kernel,
        out_shape=out_shape,
        in_specs=[pl.BlockSpec(memory_space=pltpu.SMEM)]
        + [pl.BlockSpec(memory_space=pltpu.VMEM)] * 7,
        out_specs=[pl.BlockSpec(memory_space=pltpu.VMEM)] * len(out_shape),
        compiler_params=pltpu.CompilerParams(vmem_limit_bytes=12 * MB),
        cost_estimate=takes(3),
        name="finish",
    )(spot, cross, rest, value, embed_t, key_query, query[None], ke)


def normalise(values):
    average = jnp.mean(values, axis=-1, keepdims=True)
    centered = values - average
    variance = jnp.mean(centered * centered, axis=-1, keepdims=True)
    inverse = lax.rsqrt(variance + norm_eps)
    return centered * inverse, inverse


def normalise_back(grad, gain, unit, inverse):
    scaled = grad * gain
    first = jnp.mean(scaled, axis=-1, keepdims=True)
    second = jnp.mean(scaled * unit, axis=-1, keepdims=True)
    return inverse * (scaled - first - unit * second)


def gelu_pair(values):
    below = 0.5 * (1.0 + lax.erf(values * (0.5**0.5)))
    density = jnp.exp(-0.5 * values * values) * ((0.5 / np.pi) ** 0.5)
    return values * below, below + values * density


def per_device(
    patches,
    var_ids,
    segment_ids,
    pad_mask,
    embed_weight,
    var_embed,
    agg_query,
    key_weight,
    value_weight,
    agg_out_weight,
    agg_out_bias,
    norm_one_gain,
    norm_one_bias,
    qkv_weight,
    attn_out_weight,
    attn_out_bias,
    norm_two_gain,
    norm_two_bias,
    mlp_in_weight,
    mlp_in_bias,
    mlp_out_weight,
    mlp_out_bias,
    cotangent,
):
    rows = patches.shape[0]
    shard = D // 4
    order = Order()
    where = Where(order)
    spot = where.spot

    def half(a):
        span = a.shape[1] // 2
        return rows_from(a, where.half_column if span == D // 2 else where.wide_half_column, span, 1)

    def other_half(a):
        span = a.shape[1] // 2
        start = where.other_half_column if span == D // 2 else where.other_wide_half_column
        return rows_from(a, start, span, 1)

    singles = (
        agg_query,
        agg_out_bias,
        norm_one_gain,
        norm_one_bias,
        attn_out_bias,
        norm_two_gain,
        norm_two_bias,
        mlp_out_bias,
    )
    at_row = lax.broadcasted_iota(jnp.int32, (8, shard), 0)
    vectors = jnp.zeros((8, shard), bf16)
    for i, single in enumerate(singles):
        vectors = jnp.where(at_row == i, single[None, :], vectors)
    vectors = jnp.concatenate([vectors, mlp_in_bias.reshape(4, shard)])
    narrow_v = Narrow(vectors, order)
    narrow_a = Narrow(pieces_of([agg_out_weight], where.piece_row), order)
    narrow_b = Narrow(pieces_of([qkv_weight, attn_out_weight], where.piece_row), order)
    narrow_v.second_step()
    narrow_a.second_step()
    narrow_b.second_step()

    line = jnp.arange(COLS, dtype=jnp.int32)
    variable = jnp.where(line < PATCH_COLS, line // PIX, (line - PATCH_COLS) % VARS)
    used = line < PATCH_COLS + VARS
    same = ((variable[:, None] == variable[None, :]) & used[None, :]).astype(f32)
    picks = variable[:, None] == jnp.arange(VARS, dtype=jnp.int32)[None, :]
    chosen = jnp.sum(jnp.where(picks, var_ids[None, :], 0), axis=1)
    source = jnp.where(line < PATCH_COLS, chosen * PIX + line % PIX, chosen + PATCH_COLS)
    source = jnp.where(used, source, -1)
    chooser = (source[:, None] == line[None, :]).astype(bf16)
    embed_rows = jnp.concatenate(
        [embed_weight, var_embed, jnp.zeros((COLS - PATCH_COLS - VARS, shard), bf16)]
    )
    value_part = rows_from(value_weight, where.long_piece_row, 128, 1)
    table_part = lax.dot_general(
        value_part, embed_rows, (((0,), (1,)), ((), ())), preferred_element_type=f32
    )
    table_part = beside(table_part.astype(bf16))

    around = order_narrow(vectors, narrow_v.bundle(), spot)
    whole = [around[:, i].reshape(D) for i in range(8)]
    query_full = whole[0].astype(f32)
    agg_out_b, gain_one, bias_one, attn_out_b, gain_two, bias_two, mlp_out_b = [
        v.astype(f32) for v in whole[1:]
    ]
    mlp_in_b = around[:, 8:].reshape(4 * D).astype(f32)
    head_of = jnp.arange(D, dtype=jnp.int32) // HEAD_DIM
    heads_eye = (jnp.arange(HEADS, dtype=jnp.int32)[:, None] == head_of[None, :]).astype(f32)
    query_rows = (heads_eye * query_full[None, :]).astype(bf16)
    key_query_t = dot_nt(query_rows, key_weight).astype(bf16)
    keys_part = dot_nt(key_query_t, embed_rows) * scale_by
    packed = jnp.concatenate([table_part, beside(jnp.concatenate(split_two(keys_part)))])
    order.mark(packed)
    got_packed = [turn_narrow(packed, turn) for turn in (1, 2, 3)]

    same, chooser = order.hold(same, chooser)
    agg_out_b, gain_one, bias_one, attn_out_b, gain_two, bias_two, mlp_out_b, mlp_in_b = order.hold(
        agg_out_b, gain_one, bias_one, attn_out_b, gain_two, bias_two, mlp_out_b, mlp_in_b
    )
    piece_c = pieces_of([mlp_in_weight], where.piece_row)
    piece_d = pieces_of([mlp_out_weight], where.long_piece_row)
    order.mark(piece_c)
    order.mark(piece_d)

    full_patches = jnp.concatenate(
        [
            patches,
            jnp.ones((rows, VARS), bf16),
            jnp.zeros((rows, COLS - PATCH_COLS - VARS), bf16),
        ],
        axis=1,
    )
    pixels = lax.dot_general(
        chooser, full_patches, (((0,), (1,)), ((), ())), preferred_element_type=f32
    ).astype(bf16)
    seg_row, seg_col, pad_col = order.hold(segment_ids, segment_ids.T, pad_mask.T)
    pixels = order.hold(pixels)
    cot_half, cot_other = order.hold(half(cotangent), other_half(cotangent))
    cot_got = over_core(cot_other)

    got_packed = order.hold(*got_packed)
    total = packed.astype(f32)
    for part in got_packed:
        total = total + part.astype(f32)
    table_own = total[:32].astype(bf16)
    order.mark(table_own)
    keys_two = jnp.concatenate([total[32:, i * COLS : (i + 1) * COLS] for i in range(4)])
    keys_rows = (keys_two[:HEADS] + keys_two[HEADS:]).reshape(PAIRS, 2, COLS)
    keys_cols = keys_rows.transpose(0, 2, 1)
    spread_a = Spread(narrow_a.bundle(table_own[None]), order)
    spread_b = Spread(narrow_b.bundle(), order)
    narrow_c = Narrow(order.hold(piece_c), order)
    spread_a.near_step()
    spread_a.corner_step()
    spread_b.near_step()
    spread_a.last_step()
    parts_a = spread_a.parts()
    table, table_t = arrange(parts_a, spot)
    (agg_out_w,) = assemble([agg_out_weight], parts_a, spot)
    order.mark(table_t)
    order.mark(agg_out_w)
    narrow_c.second_step()
    spread_b.corner_step()
    merged = variable_forward(pixels, same, keys_rows, order.hold(table_t))
    order.mark(merged)
    merged_there = over_core(merged)
    spread_b.last_step()
    patch_state = dot(merged, agg_out_w) + agg_out_b
    unit_one, inverse_one = normalise(patch_state)
    normed = (unit_one * gain_one + bias_one).astype(bf16)
    order.mark(normed)
    merged_there = order.hold(merged_there)
    spread_c = Spread(narrow_c.bundle(), order)
    narrow_d = Narrow(order.hold(piece_d), order)
    spread_c.near_step()
    normed_there = over_core(normed)
    qkv_w, attn_out_w = assemble([qkv_weight, attn_out_weight], spread_b.parts(), spot)
    project = dot(order.hold(normed), qkv_w).astype(bf16)
    order.mark(project)
    narrow_d.second_step()
    normed_there = order.hold(normed_there)
    attended, logs = attention(order.hold(project), seg_row, seg_col, pad_col)
    order.mark(attended)
    spread_c.corner_step()
    spread_d = Spread(narrow_d.bundle(), order)
    attended_there = over_core(attended)
    residual = patch_state + dot(order.hold(attended), attn_out_w) + attn_out_b
    unit_two, inverse_two = normalise(residual)
    normed_two = (unit_two * gain_two + bias_two).astype(bf16)
    order.mark(normed_two)
    spread_d.near_step()
    spread_c.last_step()
    normed_two_there = over_core(normed_two)
    (mlp_in_w,) = assemble([mlp_in_weight], spread_c.parts(), spot)
    attended_there, normed_two_there = order.hold(attended_there, normed_two_there)
    hidden, slope = mlp_in(order.hold(normed_two), mlp_in_w, mlp_in_b)
    order.mark(hidden)
    hidden_there = over_core(hidden)
    spread_d.corner_step()

    def grad_of(own, there, own_half, got):
        return (dot_tn(own, own_half) + dot_tn(there, got)).astype(bf16)

    def blocks(a):
        return a.reshape(4, 2, 2, a.shape[0] // 16, a.shape[1])

    cot_float = cotangent.astype(f32)
    spread_d.last_step()
    (mlp_out_w,) = assemble([mlp_out_weight], spread_d.parts(), spot)
    pre_half, pre_other, normed_two_grad, pre_sums = mlp_back(
        where.core_alone, order.hold(cotangent), mlp_out_w, mlp_in_w, slope
    )
    order.mark(pre_other)
    grad_d = blocks(grad_of(*order.hold(hidden, hidden_there), cot_half, cot_got))
    order.mark(grad_d)
    reduce_d = Reduce(grad_d, where, order)
    pre_got = over_core(pre_other)
    ke_part = lax.dot_general(
        key_weight, embed_rows, (((0,), (1,)), ((), ())), preferred_element_type=f32
    ).astype(bf16)
    ke_part = order.hold(ke_part).reshape(2, 2, shard, COLS)
    ke_kept, ke_got = take(ke_part, where.low, 1), swap_narrow(take(ke_part, where.other_low, 1), 1)
    residual_grad = cot_float + normalise_back(
        order.hold(normed_two_grad), gain_two, unit_two, inverse_two
    )
    branch_grad = residual_grad.astype(bf16)
    order.mark(branch_grad)
    branch_got = over_core(other_half(branch_grad))
    grad_c = grad_of(normed_two, normed_two_there, *order.hold(pre_half, pre_got))
    order.mark(grad_c)
    grad_c = jnp.concatenate(
        [grad_c, grad_of(attended, attended_there, *order.hold(half(branch_grad), branch_got))],
        axis=1,
    )
    order.mark(grad_c)
    reduce_c = Reduce(blocks(grad_c), where, order)
    attended_grad = dot_nt(order.hold(branch_grad), attn_out_w).astype(bf16)
    order.mark(attended_grad)
    reduce_d.step()
    ke_two = add_two(ke_kept, order.hold(ke_got))
    order.mark(ke_two)
    ke_got = swap_narrow(take(ke_two, where.other_high, 0), 2)
    attended_grad = order.hold(attended_grad)
    project_grad = attention_back(project, attended_grad, logs, seg_row, seg_col, pad_col)
    project_other = other_half(project_grad)
    order.mark(project_other)
    project_got = over_core(project_other)
    reduce_d.step()
    reduce_c.step()
    ke_own = add_two(take(ke_two, where.high, 0), order.hold(ke_got))
    order.mark(ke_own)
    grad_b = grad_of(normed, normed_there, *order.hold(half(project_grad), project_got))
    order.mark(grad_b)
    reduce_b = Reduce(blocks(grad_b), where, order)
    normed_grad = dot_nt(order.hold(project_grad), qkv_w)
    state_grad = residual_grad + normalise_back(normed_grad, gain_one, unit_one, inverse_one)
    state_grad = state_grad.astype(bf16)
    order.mark(state_grad)
    state_got = over_core(other_half(state_grad))
    reduce_d.step()
    merged_grad = dot_nt(order.hold(state_grad), agg_out_w).astype(bf16)
    order.mark(merged_grad)
    reduce_c.step()
    merged_grad = order.hold(merged_grad)
    cross, zed, pixel_grad = variable_back(pixels, same, keys_rows, keys_cols, table, merged_grad)
    order.mark(cross)
    reduce_d.step()
    spread_d = Spread(reduce_d.total, order)
    reduce_c.step()
    reduce_b.step()
    grad_a = grad_of(merged, merged_there, *order.hold(half(state_grad), state_got))
    order.mark(grad_a)
    zed_parts = split_two(zed)
    column_sums = [
        jnp.sum(state_grad.astype(f32), axis=0),
        jnp.sum(normed_grad * unit_one, axis=0),
        jnp.sum(normed_grad, axis=0),
        jnp.sum(branch_grad.astype(f32), axis=0),
        jnp.sum(normed_two_grad * unit_two, axis=0),
        jnp.sum(normed_two_grad, axis=0),
        jnp.sum(cot_float, axis=0),
        pre_sums.reshape(-1),
    ]
    sums = jnp.concatenate([v.astype(bf16) for v in column_sums]).reshape(-1, 2 * COLS)
    filler = jnp.zeros((16 * (SUB - 1) - sums.shape[0], 2 * COLS), bf16)
    small = jnp.concatenate([jnp.concatenate(zed_parts, axis=1), sums, filler])
    shared = jnp.concatenate(
        [cross.reshape(SUB, HEAD_DIM, 2 * COLS), small.reshape(SUB, 16, 2 * COLS)], axis=1
    )
    shared = shared.reshape(2, 2, 2, 80, 2 * COLS)
    order.mark(shared)
    shared_got = over_core(take(shared, where.other_core, 0))
    grad_a = grad_a.reshape(4, 2, 2, shard // 4, D // 2).transpose(1, 2, 0, 3, 4)
    grad_a = grad_a.reshape(2, 2, shard, D // 2)
    shared = add_two(take(shared, where.core, 0), order.hold(shared_got))
    grad_a = jnp.concatenate([grad_a, shared], axis=2)
    order.mark(grad_a)
    reduce_a = ReduceShared(grad_a[None], where, order)
    spread_d.near_step()
    reduce_b.step()
    reduce_c.step()
    spread_c = Spread(reduce_c.total, order)
    reduce_a.step()
    spread_d.corner_step()
    reduce_b.step()
    reduce_a.step()
    result = (residual + dot(order.hold(hidden), mlp_out_w) + mlp_out_b).astype(bf16)
    order.mark(result)
    reduce_b.step()
    spread_b = Spread(reduce_b.total, order)
    spread_c.near_step()
    reduce_a.step()
    spread_d.last_step()
    spread_b.near_step()
    patches_grad = lax.dot_general(
        order.hold(pixel_grad),
        chooser.astype(f32),
        (((0,), (1,)), ((), ())),
        precision=lax.Precision.HIGHEST,
        preferred_element_type=f32,
    )[:, :PATCH_COLS]
    order.mark(patches_grad)
    reduce_a.step()
    spread_a = Spread(reduce_a.total, order)
    spread_c.corner_step()
    spread_a.near_step()
    spread_b.corner_step()
    (grad_mlp_out_w,) = place(spread_d.parts(), [(D, D)], spot)
    order.mark(grad_mlp_out_w)
    spread_c.last_step()
    spread_a.corner_step()
    spread_b.last_step()
    grad_mlp_in_w, grad_attn_out_w = place(spread_c.parts(), [(shard, 4 * D), (shard, D)], spot)
    order.mark(grad_mlp_in_w)
    spread_a.last_step()
    (grad_qkv_w,) = place(spread_b.parts(), [(shard, 3 * D)], spot)
    order.mark(grad_qkv_w)
    grad_agg_out_w, cross, rest = place(spread_a.parts(), [(shard, D)], spot, shared=True)
    finished = finish(
        spot, cross, rest, value_weight, embed_rows.T, key_query_t.T, query_full, ke_own
    )
    grad_embed, grad_value_w, grad_key_w, grad_agg_query, grad_mlp_in_b = finished[:5]
    grad_agg_query, grad_mlp_in_b = grad_agg_query.reshape(shard), grad_mlp_in_b.reshape(D)
    own = lambda i: finished[5 + i].reshape(shard)

    return (
        result,
        patches_grad,
        grad_embed[:PATCH_COLS],
        grad_embed[PATCH_COLS : PATCH_COLS + VARS],
        grad_agg_query,
        grad_key_w,
        grad_value_w,
        grad_agg_out_w,
        own(0),
        own(1),
        own(2),
        grad_qkv_w,
        grad_attn_out_w,
        own(3),
        own(4),
        own(5),
        grad_mlp_in_w,
        grad_mlp_in_b,
        grad_mlp_out_w,
        own(6),
    )


def solution(mesh):
    rows, shard = P(("wide", "narrow"), None), P("narrow", None)
    wide_shard, vector = P(None, "narrow"), P("narrow")
    return jax.shard_map(
        per_device,
        mesh=mesh,
        in_specs=(
            rows,
            P(),
            rows,
            rows,
            wide_shard,
            wide_shard,
            vector,
            shard,
            shard,
            shard,
            vector,
            vector,
            vector,
            shard,
            shard,
            vector,
            vector,
            vector,
            shard,
            vector,
            shard,
            vector,
            rows,
        ),
        out_specs=(
            rows,
            rows,
            wide_shard,
            wide_shard,
            vector,
            shard,
            shard,
            shard,
            vector,
            vector,
            vector,
            shard,
            shard,
            vector,
            vector,
            vector,
            shard,
            vector,
            shard,
            vector,
        ),
        check_vma=False,
    )
```

```python
import functools

import jax
import jax.numpy as jnp
import numpy as np
from jax import lax
from jax.experimental import pallas as pl
from jax.experimental.pallas import tpu as pltpu
from jax.sharding import PartitionSpec as P

D = 1024
HEADS = 16
HEAD_DIM = 64
VARS = 48
PIX = 4
PATCH_COLS = VARS * PIX
COLS = 256
PAIRS = HEADS // 2
SUB = 8

norm_eps = 1e-06
masked_out = -1e30
scale_by = HEAD_DIM ** (-0.5)
f32 = jnp.float32
bf16 = jnp.bfloat16
MB = 1 << 20


def takes(microseconds):
    flops = int(microseconds * 1.8 * 1e9)
    return pl.CostEstimate(flops=flops, transcendentals=0, bytes_accessed=1)


def dot(a, b):
    return jnp.dot(a, b, preferred_element_type=f32)


def dot_nt(a, b):
    return lax.dot_general(a, b, (((1,), (1,)), ((), ())), preferred_element_type=f32)


def dot_tn(a, b):
    return lax.dot_general(a, b, (((0,), (0,)), ((), ())), preferred_element_type=f32)


def split_two(a):
    high = a.astype(bf16)
    return high, (a - high.astype(f32)).astype(bf16)


def wide_pairs(bits_of):
    return [(i, i ^ bits_of(i)) for i in range(lax.axis_size("wide"))]


def over_core(a):
    return lax.ppermute(a, "wide", wide_pairs(lambda i: 1))


def over_first(a):
    return lax.ppermute(a, "wide", wide_pairs(lambda i: 4 if i & 1 else 2))


def over_second(a):
    return lax.ppermute(a, "wide", wide_pairs(lambda i: 2 if i & 1 else 4))


def turn_narrow(a, by):
    size = lax.axis_size("narrow")
    return lax.ppermute(a, "narrow", [(i, (i + by) % size) for i in range(size)])


def swap_narrow(a, bits):
    size = lax.axis_size("narrow")
    return lax.ppermute(a, "narrow", [(i, i ^ bits) for i in range(size)])


def take(a, at, axis):
    return lax.dynamic_index_in_dim(a, at, axis, keepdims=False, allow_negative_indices=False)


def rows_from(a, start, count, axis):
    return lax.dynamic_slice_in_dim(a, start, count, axis, allow_negative_indices=False)


class Order:
    def __init__(self):
        self.pending = []

    def hold(self, *arrays):
        arrays = lax.optimization_barrier((*arrays, *self.pending))[: len(arrays)]
        self.pending = [arrays[0]]
        return arrays[0] if len(arrays) == 1 else arrays

    def mark(self, array):
        self.pending.append(array)


class Where:
    def __init__(self, order):
        z, p = lax.axis_index("narrow"), lax.axis_index("wide") % SUB
        core, x, y = p & 1, (p >> 1) & 1, p >> 2
        first, second = jnp.where(core == 0, x, y), jnp.where(core == 0, y, x)
        low, high = z & 1, z >> 1
        zero = jnp.zeros_like(z)
        plain = {
            "core": core,
            "other_core": 1 - core,
            "low": low,
            "other_low": 1 - low,
            "high": high,
            "other_high": 1 - high,
            "piece_row": p * (D // 4 // SUB),
            "long_piece_row": p * (D // SUB),
            "half_column": core * (D // 2),
            "other_half_column": (1 - core) * (D // 2),
            "wide_half_column": core * (3 * D // 2),
            "other_wide_half_column": (1 - core) * (3 * D // 2),
            "spot": jnp.stack([z, p]),
            "core_alone": core[None],
            "unsent": (1 - first)[None],
            "second_step": jnp.stack([first, second]),
            "third_step": jnp.stack([zero, low]),
            "fourth_step": jnp.stack([zero, high]),
        }
        for name, value in zip(plain, order.hold(*plain.values())):
            setattr(self, name, value)


class Narrow:
    def __init__(self, own, order):
        self.order = order
        self.own = own
        self.two = swap_narrow(own, 2)

    def second_step(self):
        self.two = self.order.hold(self.two)
        both = jnp.stack([self.own, self.two])
        self.order.mark(both)
        self.others = swap_narrow(both, 1)

    def bundle(self, *more):
        others = self.order.hold(self.others)
        bundle = jnp.concatenate([self.two[None], others, *more])
        self.order.mark(bundle)
        return bundle


class Spread:
    def __init__(self, own, order):
        self.order = order
        self.own = own
        self.other = over_core(own)

    def near_step(self):
        other = self.order.hold(self.other)
        self.other = other
        both = jnp.stack([self.own, other])
        self.order.mark(both)
        self.near = over_first(both)

    def corner_step(self):
        self.near = self.order.hold(self.near)
        corner = self.near[0]
        self.order.mark(corner)
        self.corner = over_second(corner)
        self.far = over_core(self.near)

    def last_step(self):
        self.corner = self.order.hold(self.corner)
        self.order.mark(self.corner)
        self.corner_other = over_core(self.corner)

    def parts(self):
        parts = [self.own, self.other, self.near, self.far, self.corner, self.corner_other]
        return list(self.order.hold(*parts))


def origins(p, parts):
    own, other, near, far, corner, corner_other = parts
    first = 2 + 2 * (p & 1)
    second = 6 - first
    return [
        (p, own),
        (p ^ 1, other),
        (p ^ first, near.at[0]),
        (p ^ first ^ 1, near.at[1]),
        (p ^ second ^ 1, far.at[0]),
        (p ^ second, far.at[1]),
        (p ^ 6, corner),
        (p ^ 7, corner_other),
    ]


def core_and_quarter(place):
    core, x, y = place & 1, (place >> 1) & 1, place >> 2
    return core, jnp.where(core == 0, 2 * x + y, 2 * y + x)


def assemble_kernel(n_shards, spot, *refs):
    shards, parts = refs[:n_shards], refs[n_shards : n_shards + 6]
    fulls, sems = refs[n_shards + 6 : -1], refs[-1]
    z, p = spot[0], spot[1]
    copies = []

    def start(src, dst):
        copy = pltpu.make_async_copy(src, dst, sems.at[len(copies)])
        copy.start()
        copies.append(copy)

    for shard, full in zip(shards, fulls):
        rows = shard.shape[0]
        start(shard, full.at[pl.ds(pl.multiple_of(z * rows, rows), rows), :])
    for place, part in origins(p, parts):
        for i, bits in enumerate((2, 1, 3)):
            origin = z ^ bits
            left = 0
            for full in fulls:
                rows, width = full.shape[0] // 4, full.shape[1]
                count = rows // SUB
                at = pl.multiple_of(origin * rows + place * count, count)
                start(part.at[i, :, left : left + width], full.at[pl.ds(at, count), :])
                left += width
    for copy in copies:
        copy.wait()


def assemble(shards, parts, spot):
    n_copies = 25 * len(shards)
    return pl.pallas_call(
        functools.partial(assemble_kernel, len(shards)),
        out_shape=[jax.ShapeDtypeStruct((4 * s.shape[0], s.shape[1]), s.dtype) for s in shards],
        in_specs=[pl.BlockSpec(memory_space=pltpu.SMEM)]
        + [pl.BlockSpec(memory_space=pl.ANY)] * (len(shards) + 6),
        out_specs=[pl.BlockSpec(memory_space=pltpu.VMEM)] * len(shards),
        scratch_shapes=[pltpu.SemaphoreType.DMA((n_copies,))],
        compiler_params=pltpu.CompilerParams(vmem_limit_bytes=12 * MB),
        cost_estimate=takes(3.5),
        name="assemble",
    )(spot, *shards, *parts)


def pieces_of(shards, start):
    rows = shards[0].shape[0] // SUB
    return jnp.concatenate([rows_from(shard, start, rows, 0) for shard in shards], axis=1)


def beside(a):
    rows = a.shape[0] // 4
    return jnp.concatenate([a[i * rows : (i + 1) * rows] for i in range(4)], axis=1)


def add_two(a, b):
    return (a.astype(f32) + b.astype(f32)).astype(bf16)


def pick_kernel(bits, grad, sent):
    sent[...] = grad[...].reshape(sent.shape)


def pick_first(grad, bits):
    n, _, _, rows, width = grad.shape
    return pl.pallas_call(
        pick_kernel,
        out_shape=jax.ShapeDtypeStruct((n, 2, rows, width), bf16),
        grid_spec=pltpu.PrefetchScalarGridSpec(
            num_scalar_prefetch=1,
            grid=(n,),
            in_specs=[pl.BlockSpec((1, 1, 2, rows, width), lambda i, b: (i, b[0], 0, 0, 0))],
            out_specs=pl.BlockSpec((1, 2, rows, width), lambda i, b: (i, 0, 0, 0)),
        ),
        compiler_params=pltpu.CompilerParams(vmem_limit_bytes=5 * MB),
        cost_estimate=takes(2.5),
        name="pick_first",
    )(bits, grad)


def add_split_kernel(bits, kept_sent, got_sent, kept_kept, got_kept, sent, kept):
    def total(a, b):
        return (a[...].astype(f32).reshape(sent.shape) + b[...].astype(f32).reshape(sent.shape)).astype(bf16)

    sent[...] = total(kept_sent, got_sent)
    kept[...] = total(kept_kept, got_kept)


def add_split(grad, got, bits):
    n, _, _, rows, width = grad.shape
    block = (1, 1, 1, rows, width)
    got_block = (1, 1, rows, width)
    out = jax.ShapeDtypeStruct((n, rows, width), bf16)
    return pl.pallas_call(
        add_split_kernel,
        out_shape=[out, out],
        grid_spec=pltpu.PrefetchScalarGridSpec(
            num_scalar_prefetch=1,
            grid=(n,),
            in_specs=[
                pl.BlockSpec(block, lambda i, b: (i, b[0], 1 - b[1], 0, 0)),
                pl.BlockSpec(got_block, lambda i, b: (i, 1 - b[1], 0, 0)),
                pl.BlockSpec(block, lambda i, b: (i, b[0], b[1], 0, 0)),
                pl.BlockSpec(got_block, lambda i, b: (i, b[1], 0, 0)),
            ],
            out_specs=[pl.BlockSpec((1, rows, width), lambda i, b: (i, 0, 0))] * 2,
        ),
        compiler_params=pltpu.CompilerParams(vmem_limit_bytes=8 * MB),
        cost_estimate=takes(2.5),
        name="add_split",
    )(bits, grad, got, grad, got)


class Reduce:
    def __init__(self, grad, where, order):
        self.where, self.order, self.stage, self.kept = where, order, 0, grad
        sent = pick_first(grad, where.unsent)
        order.mark(sent)
        self.got = over_first(sent)

    def step(self):
        kept, got = self.kept, self.order.hold(self.got)
        self.stage += 1
        if self.stage == 4:
            self.total = across_groups(add_two(kept[0], got[0]))
            self.order.mark(self.total)
            return
        if self.stage > 1:
            rows, width = kept.shape[1:]
            kept = kept.reshape(-1, 1, 2, rows, width)
            got = got.reshape(-1, 2, rows, width)
        where = self.where
        bits = (where.second_step, where.third_step, where.fourth_step)[self.stage - 1]
        sent, self.kept = add_split(kept, got, bits)
        self.order.mark(sent)
        self.got = over_second(sent) if self.stage == 1 else swap_narrow(sent, self.stage - 1)


class ReduceShared(Reduce):
    def step(self):
        if self.stage == 0:
            return super().step()
        total = add_two(self.kept, self.order.hold(self.got))
        self.order.mark(total)
        self.stage += 1
        if self.stage == 4:
            self.total = across_groups(total)
            return
        total = total.reshape(-1, total.shape[-1])
        shape, axis = ((2, 2, 64, -1), 1) if self.stage == 2 else ((2, 64, -1), 0)
        blocks, shared = total[:-80].reshape(shape), total[-80:]

        def pick(bit):
            return jnp.concatenate([take(blocks, bit, axis).reshape(-1, total.shape[-1]), shared])

        where = self.where
        own, other = (where.low, where.other_low) if self.stage == 2 else (where.high, where.other_high)
        sent = pick(other)
        self.order.mark(sent)
        self.kept = pick(own)
        self.got = swap_narrow(sent, self.stage - 1)


def across_groups(a):
    groups = lax.axis_size("wide") // SUB
    if groups == 1:
        return a
    members = [[g * SUB + i for g in range(groups)] for i in range(SUB)]
    return lax.psum(a.astype(f32), "wide", axis_index_groups=members).astype(bf16)


def place_kernel(spans, shared, spot, *refs):
    parts, outs = refs[:6], refs[6:]
    for place, part in origins(spot[1], parts):
        core, quarter = core_and_quarter(place)
        left = 0
        for out, span in zip(outs, spans):
            count = out.shape[0] // 4
            row = pl.multiple_of(quarter * count, 16)
            column = pl.multiple_of(core * span, 128)
            out[pl.ds(row, count), pl.ds(column, span)] = part[
                :count, left : left + span
            ].astype(f32)
            left += span
        if shared:
            pair = core * 4 + quarter
            cross, rest = outs[-2:]
            row = pl.multiple_of(pair * 128, 128)
            cross[pl.ds(row, HEAD_DIM), :] = part[64:128, :COLS]
            cross[pl.ds(row + HEAD_DIM, HEAD_DIM), :] = part[64:128, COLS:]
            rest[pair] = part[128:, :].astype(f32)


def place(parts, shapes, spot, shared=False):
    spans = tuple(s[1] // 2 for s in shapes)
    out_shape = [jax.ShapeDtypeStruct(s, f32) for s in shapes]
    if shared:
        out_shape.append(jax.ShapeDtypeStruct((D, COLS), bf16))
        out_shape.append(jax.ShapeDtypeStruct((SUB, 16, 2 * COLS), f32))
    return pl.pallas_call(
        functools.partial(place_kernel, spans, shared),
        out_shape=out_shape,
        in_specs=[pl.BlockSpec(memory_space=pltpu.SMEM)]
        + [pl.BlockSpec(memory_space=pltpu.VMEM)] * 6,
        out_specs=[pl.BlockSpec(memory_space=pltpu.VMEM)] * len(out_shape),
        compiler_params=pltpu.CompilerParams(vmem_limit_bytes=10 * MB),
        cost_estimate=takes(3),
        name="place",
    )(spot, *parts)


def arrange_kernel(spot, *refs):
    parts, table, table_t = refs[:6], refs[6], refs[7]
    for place, part in origins(spot[1], parts):
        at = pl.ds(pl.multiple_of(place * 128, 128), 128)
        rows = jnp.concatenate([part[3, :, i * COLS : (i + 1) * COLS] for i in range(4)], axis=0)
        table_t[at, :] = rows
        table[:, at] = rows.astype(f32).T.astype(bf16)


def arrange(parts, spot):
    return pl.pallas_call(
        arrange_kernel,
        out_shape=[
            jax.ShapeDtypeStruct((COLS, D), bf16),
            jax.ShapeDtypeStruct((D, COLS), bf16),
        ],
        in_specs=[pl.BlockSpec(memory_space=pltpu.SMEM)]
        + [pl.BlockSpec(memory_space=pltpu.VMEM)] * 6,
        out_specs=[pl.BlockSpec(memory_space=pltpu.VMEM)] * 2,
        name="arrange",
    )(spot, *parts)


def order_kernel(spot, own, others, out):
    out[spot[0]] = own[...]
    for i, bits in enumerate((2, 1, 3)):
        out[spot[0] ^ bits] = others[i]


def order_narrow(own, others, spot):
    return pl.pallas_call(
        order_kernel,
        out_shape=jax.ShapeDtypeStruct((4, *own.shape), own.dtype),
        in_specs=[pl.BlockSpec(memory_space=pltpu.SMEM)]
        + [pl.BlockSpec(memory_space=pltpu.VMEM)] * 2,
        out_specs=pl.BlockSpec(memory_space=pltpu.VMEM),
        name="order",
    )(spot, own, others)


def pair_probs(pixels, same, keys_row):
    high, low = split_two(same * keys_row)
    scores = dot(high, pixels) + dot(low, pixels)
    biggest = jnp.max(scores[PATCH_COLS : PATCH_COLS + VARS], axis=0, keepdims=True)
    raised = jnp.exp(scores - biggest)
    total = jnp.sum(raised[PATCH_COLS : PATCH_COLS + VARS], axis=0, keepdims=True)
    return raised * (1.0 / total)


def variable_kernel(pixels_ref, same_ref, keys_ref, table_ref, merged_ref):
    pixels = pixels_ref[...]
    pixels_wide = pixels.astype(f32)
    same = same_ref[...]
    parts = []
    for i in range(2):
        probs = pair_probs(pixels, same, keys_ref[0, i : i + 1, :])
        weighted = (probs * pixels_wide).astype(bf16)
        parts.append(dot(table_ref[i * HEAD_DIM : (i + 1) * HEAD_DIM, :], weighted))
    merged_ref[...] = jnp.concatenate(parts, axis=0).T.astype(bf16)


def variable_forward(pixels, same, keys_rows, table_t):
    rows = pixels.shape[1]
    return pl.pallas_call(
        variable_kernel,
        out_shape=jax.ShapeDtypeStruct((rows, D), bf16),
        grid=(PAIRS,),
        in_specs=[
            pl.BlockSpec((COLS, rows), lambda h: (0, 0)),
            pl.BlockSpec((COLS, COLS), lambda h: (0, 0)),
            pl.BlockSpec((1, 2, COLS), lambda h: (h, 0, 0)),
            pl.BlockSpec((128, COLS), lambda h: (h, 0)),
        ],
        out_specs=pl.BlockSpec((rows, 128), lambda h: (0, h)),
        compiler_params=pltpu.CompilerParams(vmem_limit_bytes=8 * MB),
        cost_estimate=takes(4),
        name="variable_forward",
    )(pixels, same, keys_rows, table_t)


def variable_back_kernel(
    pixels_ref, same_ref, keys_ref, keys_col_ref, table_ref, grad_ref, x_ref, zed_ref, pixel_ref, zed_columns
):
    step = pl.program_id(0)

    @pl.when(step == 0)
    def _():
        zed_columns[...] = jnp.zeros_like(zed_columns)

    pixels = pixels_ref[...]
    pixels_wide = pixels.astype(f32)
    same = same_ref[...]
    same_low = same.astype(bf16)
    grad_t = grad_ref[...].astype(f32).T.astype(bf16)
    line = lax.broadcasted_iota(jnp.int32, zed_columns.shape, 1)
    pixel_grad = None
    for i in range(2):
        probs = pair_probs(pixels, same, keys_ref[0, i : i + 1, :])
        weighted = (probs * pixels_wide).astype(bf16)
        grad_i = grad_t[i * HEAD_DIM : (i + 1) * HEAD_DIM, :]
        spread = dot(table_ref[:, i * HEAD_DIM : (i + 1) * HEAD_DIM], grad_i)
        high, low = split_two(spread * pixels_wide)
        prob_grad = dot(same_low, high) + dot(same_low, low)
        lifted = probs * prob_grad
        centre = jnp.sum(lifted[PATCH_COLS : PATCH_COLS + VARS], axis=0, keepdims=True)
        score_grad = lifted - probs * centre
        x_ref[:, i * COLS : (i + 1) * COLS] = dot_nt(grad_i, weighted).astype(bf16)
        sums = jnp.sum(score_grad * pixels_wide, axis=1, keepdims=True)
        zed_columns[...] += jnp.where(line == 2 * step + i, sums, 0.0)
        term = probs * spread + score_grad * keys_col_ref[0, :, i : i + 1]
        pixel_grad = term if pixel_grad is None else pixel_grad + term

    @pl.when(step == 0)
    def _():
        pixel_ref[...] = pixel_grad

    @pl.when(step > 0)
    def _():
        pixel_ref[...] += pixel_grad

    @pl.when(step == PAIRS - 1)
    def _():
        zed_ref[...] = zed_columns[...].T[:HEADS]


def variable_back(pixels, same, keys_rows, keys_cols, table, grad):
    rows = pixels.shape[1]
    return pl.pallas_call(
        variable_back_kernel,
        out_shape=[
            jax.ShapeDtypeStruct((D // 2, 2 * COLS), bf16),
            jax.ShapeDtypeStruct((HEADS, COLS), f32),
            jax.ShapeDtypeStruct((COLS, rows), f32),
        ],
        grid=(PAIRS,),
        in_specs=[
            pl.BlockSpec((COLS, rows), lambda h: (0, 0)),
            pl.BlockSpec((COLS, COLS), lambda h: (0, 0)),
            pl.BlockSpec((1, 2, COLS), lambda h: (h, 0, 0)),
            pl.BlockSpec((1, COLS, 2), lambda h: (h, 0, 0)),
            pl.BlockSpec((COLS, 128), lambda h: (0, h)),
            pl.BlockSpec((rows, 128), lambda h: (0, h)),
        ],
        out_specs=[
            pl.BlockSpec((HEAD_DIM, 2 * COLS), lambda h: (h, 0)),
            pl.BlockSpec((HEADS, COLS), lambda h: (0, 0)),
            pl.BlockSpec((COLS, rows), lambda h: (0, 0)),
        ],
        scratch_shapes=[pltpu.VMEM((COLS, 128), f32)],
        compiler_params=pltpu.CompilerParams(vmem_limit_bytes=10 * MB),
        cost_estimate=takes(1),
        name="variable_back",
    )(pixels, same, keys_rows, keys_cols, table, grad)


def mask_rows(segment_col, segment_row, padding_col, rows):
    key_at = lax.broadcasted_iota(jnp.int32, (rows, rows), 0)
    query_at = lax.broadcasted_iota(jnp.int32, (rows, rows), 1)
    allowed = (segment_col == segment_row) & ((padding_col == 1) | (key_at == query_at))
    return jnp.where(allowed, 0.0, masked_out).astype(f32)


def attention_kernel(q_ref, k_ref, v_ref, seg_row, seg_col, pad_col, out_ref, log_ref, mask_ref):
    rows = q_ref.shape[0]

    @pl.when(pl.program_id(0) == 0)
    def _():
        mask_ref[...] = mask_rows(seg_col[...], seg_row[...], pad_col[...], rows)

    q_t = (q_ref[...].astype(f32) * scale_by).T.astype(bf16)
    v_t = v_ref[...].astype(f32).T.astype(bf16)
    outs, logs = [], []
    for i in range(2):
        span = slice(i * HEAD_DIM, (i + 1) * HEAD_DIM)
        scores = dot(k_ref[:, span], q_t[span, :]) + mask_ref[...]
        biggest = jnp.max(scores, axis=0, keepdims=True)
        raised = jnp.exp(scores - biggest)
        total = jnp.sum(raised, axis=0, keepdims=True)
        outs.append(dot(v_t[span, :], raised.astype(bf16)) * (1.0 / total))
        logs.append(biggest + jnp.log(total))
    out_ref[...] = jnp.concatenate(outs, axis=0).T.astype(bf16)
    log_ref[0] = jnp.concatenate(logs, axis=0)


def attention(project, seg_row, seg_col, pad_col):
    rows = project.shape[0]
    column = lambda first: pl.BlockSpec((rows, 128), lambda h: (0, first * PAIRS + h))
    return pl.pallas_call(
        attention_kernel,
        out_shape=[
            jax.ShapeDtypeStruct((rows, D), bf16),
            jax.ShapeDtypeStruct((PAIRS, 2, rows), f32),
        ],
        grid=(PAIRS,),
        in_specs=[
            column(0),
            column(1),
            column(2),
            pl.BlockSpec((1, rows), lambda h: (0, 0)),
            pl.BlockSpec((rows, 1), lambda h: (0, 0)),
            pl.BlockSpec((rows, 1), lambda h: (0, 0)),
        ],
        out_specs=[column(0), pl.BlockSpec((1, 2, rows), lambda h: (h, 0, 0))],
        scratch_shapes=[pltpu.VMEM((rows, rows), f32)],
        compiler_params=pltpu.CompilerParams(vmem_limit_bytes=8 * MB),
        cost_estimate=takes(12.5),
        name="attention",
    )(project, project, project, seg_row, seg_col, pad_col)


def attention_back_kernel(
    q_ref, k_ref, v_ref, grad_ref, log_ref, seg_row, seg_col, pad_col, out_ref, mask_ref
):
    rows = q_ref.shape[0]
    step = pl.program_id(0)

    @pl.when(step == 0)
    def _():
        mask_ref[...] = mask_rows(seg_col[...], seg_row[...], pad_col[...], rows)

    q_scaled = q_ref[...].astype(f32) * scale_by
    q_low = q_scaled.astype(bf16)
    q_t = q_scaled.T.astype(bf16)
    k_t = (k_ref[...].astype(f32) * scale_by).T.astype(bf16)
    grad_t = grad_ref[...].astype(f32).T.astype(bf16)
    q_grads, k_grads, v_grads = [], [], []
    for i in range(2):
        span = slice(i * HEAD_DIM, (i + 1) * HEAD_DIM)
        scores = dot(k_ref[:, span], q_t[span, :]) + mask_ref[...]
        probs = jnp.exp(scores - log_ref[0, i : i + 1, :])
        prob_grad = dot(v_ref[:, span], grad_t[span, :])
        lifted = probs * prob_grad
        centre = jnp.sum(lifted, axis=0, keepdims=True)
        score_grad = (lifted - probs * centre).astype(bf16)
        v_grads.append(dot(probs.astype(bf16), grad_ref[:, span]))
        k_grads.append(dot(score_grad, q_low[:, span]))
        q_grads.append(dot(k_t[span, :], score_grad))
    at = lambda first: pl.ds(pl.multiple_of(first * D + step * 128, 128), 128)
    out_ref[:, at(0)] = jnp.concatenate(q_grads, axis=0).T.astype(bf16)
    out_ref[:, at(1)] = jnp.concatenate(k_grads, axis=1).astype(bf16)
    out_ref[:, at(2)] = jnp.concatenate(v_grads, axis=1).astype(bf16)


def attention_back(project, grad, logs, seg_row, seg_col, pad_col):
    rows = project.shape[0]
    column = lambda first: pl.BlockSpec((rows, 128), lambda h: (0, first * PAIRS + h))
    return pl.pallas_call(
        attention_back_kernel,
        out_shape=jax.ShapeDtypeStruct((rows, 3 * D), bf16),
        grid=(PAIRS,),
        in_specs=[
            column(0),
            column(1),
            column(2),
            column(0),
            pl.BlockSpec((1, 2, rows), lambda h: (h, 0, 0)),
            pl.BlockSpec((1, rows), lambda h: (0, 0)),
            pl.BlockSpec((rows, 1), lambda h: (0, 0)),
            pl.BlockSpec((rows, 1), lambda h: (0, 0)),
        ],
        out_specs=pl.BlockSpec((rows, 3 * D), lambda h: (0, 0)),
        scratch_shapes=[pltpu.VMEM((rows, rows), f32)],
        compiler_params=pltpu.CompilerParams(vmem_limit_bytes=14 * MB),
        cost_estimate=takes(16.5),
        name="attention_back",
    )(project, project, project, grad, logs, seg_row, seg_col, pad_col)


def mlp_in_kernel(rows_ref, weight, bias, hidden, slope):
    value, change = gelu_pair(dot(rows_ref[...], weight[...]) + bias[...])
    hidden[...] = value.astype(bf16)
    slope[...] = change.astype(bf16)


def mlp_in(rows_in, weight, bias):
    rows, hidden = rows_in.shape[0], weight.shape[1]
    block = 512
    columns = lambda count: pl.BlockSpec((count, block), lambda i: (0, i))
    return pl.pallas_call(
        mlp_in_kernel,
        out_shape=[jax.ShapeDtypeStruct((rows, hidden), bf16)] * 2,
        grid=(hidden // block,),
        in_specs=[pl.BlockSpec((rows, D), lambda i: (0, 0)), columns(D), columns(1)],
        out_specs=[columns(rows)] * 2,
        compiler_params=pltpu.CompilerParams(vmem_limit_bytes=14 * MB),
        cost_estimate=takes(11),
        name="mlp_in",
    )(rows_in, weight, bias[None])


def mlp_back_kernel(core, cot, w_out, w_in, slope, own, other, grad, sums):
    step = pl.program_id(0)
    pre = (dot_nt(cot[...], w_out[...]) * slope[...].astype(f32)).astype(bf16)
    sums[0] = jnp.sum(pre.astype(f32), axis=0, keepdims=True)
    part = dot_nt(pre, w_in[...])

    @pl.when(step < 2)
    def _():
        other[...] = pre

    @pl.when(step >= 2)
    def _():
        own[...] = pre

    @pl.when(step == 0)
    def _():
        grad[...] = part

    @pl.when(step > 0)
    def _():
        grad[...] += part


def mlp_back(core, cot, w_out, w_in, slope):
    rows, hidden = cot.shape[0], w_out.shape[0]
    block = hidden // 4
    at = lambda i, c: lax.rem(i + 2 - 2 * c[0], 4)
    return pl.pallas_call(
        mlp_back_kernel,
        out_shape=[
            jax.ShapeDtypeStruct((rows, hidden // 2), bf16),
            jax.ShapeDtypeStruct((rows, hidden // 2), bf16),
            jax.ShapeDtypeStruct((rows, D), f32),
            jax.ShapeDtypeStruct((4, 1, block), f32),
        ],
        grid_spec=pltpu.PrefetchScalarGridSpec(
            num_scalar_prefetch=1,
            grid=(4,),
            in_specs=[
                pl.BlockSpec((rows, D), lambda i, c: (0, 0)),
                pl.BlockSpec((block, D), lambda i, c: (at(i, c), 0)),
                pl.BlockSpec((D, block), lambda i, c: (0, at(i, c))),
                pl.BlockSpec((rows, block), lambda i, c: (0, at(i, c))),
            ],
            out_specs=[
                pl.BlockSpec((rows, block), lambda i, c: (0, jnp.maximum(i - 2, 0))),
                pl.BlockSpec((rows, block), lambda i, c: (0, jnp.minimum(i, 1))),
                pl.BlockSpec((rows, D), lambda i, c: (0, 0)),
                pl.BlockSpec((1, 1, block), lambda i, c: (at(i, c), 0, 0)),
            ],
        ),
        compiler_params=pltpu.CompilerParams(vmem_limit_bytes=24 * MB),
        cost_estimate=takes(15.5),
        name="mlp_back",
    )(core, cot, w_out, w_in, slope)


def finish_kernel(
    spot, cross, rest, value, embed_t, key_query, query, ke, embed_out, value_out, key_out, query_out, bias_out, *sums_out
):
    z = spot[0]
    summed = cross[...]
    zed = rest[0, :, :COLS] + rest[0, :, COLS:]
    zed_both = split_two(zed)
    embed_grad = dot(value[...], summed)
    query_grad = 0.0
    per_head = 0.0
    for part in zed_both:
        embed_grad += dot(key_query[...], part) * scale_by
        query_grad += dot_nt(embed_t[...], part) * scale_by
        per_head += dot_nt(part, ke[...]) * scale_by
    embed_out[...] = embed_grad.T
    value_out[...] = dot_nt(embed_t[...], summed)
    head = lax.broadcasted_iota(jnp.int32, (HEADS, D), 0)
    line = lax.broadcasted_iota(jnp.int32, (HEADS, D), 1)
    eye = (head == line // HEAD_DIM).astype(bf16)
    high, low = split_two(query_grad)
    key_out[...] = (dot(high, eye) + dot(low, eye)) * query[...]
    head = lax.broadcasted_iota(jnp.int32, per_head.shape, 0)
    line = lax.broadcasted_iota(jnp.int32, per_head.shape, 1)
    mine = head == z * 4 + line // HEAD_DIM
    query_out[...] = jnp.sum(jnp.where(mine, per_head, 0.0), axis=0, keepdims=True)
    column = pl.multiple_of((z & 1) * COLS, COLS)
    for i, out in enumerate(sums_out):
        at = 16 + 2 * i + (z >> 1)
        out[...] = rest[at // 16, pl.ds(lax.rem(at, 16), 1), pl.ds(column, COLS)]
    for i in range(2):
        at = 16 + 14 + 2 * z + i
        bias_out[pl.ds(i, 1), :] = rest[at // 16, pl.ds(lax.rem(at, 16), 1), :]


def finish(spot, cross, rest, value, embed_t, key_query, query, ke):
    shard = value.shape[0]
    row = jax.ShapeDtypeStruct((1, shard), f32)
    out_shape = [
        jax.ShapeDtypeStruct((COLS, shard), f32),
        jax.ShapeDtypeStruct((shard, D), f32),
        jax.ShapeDtypeStruct((shard, D), f32),
        row,
        jax.ShapeDtypeStruct((2, 2 * COLS), f32),
    ] + [row] * 7
    return pl.pallas_call(
        finish_kernel,
        out_shape=out_shape,
        in_specs=[pl.BlockSpec(memory_space=pltpu.SMEM)]
        + [pl.BlockSpec(memory_space=pltpu.VMEM)] * 7,
        out_specs=[pl.BlockSpec(memory_space=pltpu.VMEM)] * len(out_shape),
        compiler_params=pltpu.CompilerParams(vmem_limit_bytes=12 * MB),
        cost_estimate=takes(3),
        name="finish",
    )(spot, cross, rest, value, embed_t, key_query, query[None], ke)


def normalise(values):
    average = jnp.mean(values, axis=-1, keepdims=True)
    centered = values - average
    variance = jnp.mean(centered * centered, axis=-1, keepdims=True)
    inverse = lax.rsqrt(variance + norm_eps)
    return centered * inverse, inverse


def normalise_back(grad, gain, unit, inverse):
    scaled = grad * gain
    first = jnp.mean(scaled, axis=-1, keepdims=True)
    second = jnp.mean(scaled * unit, axis=-1, keepdims=True)
    return inverse * (scaled - first - unit * second)


def gelu_pair(values):
    below = 0.5 * (1.0 + lax.erf(values * (0.5**0.5)))
    density = jnp.exp(-0.5 * values * values) * ((0.5 / np.pi) ** 0.5)
    return values * below, below + values * density


def per_device(
    patches,
    var_ids,
    segment_ids,
    pad_mask,
    embed_weight,
    var_embed,
    agg_query,
    key_weight,
    value_weight,
    agg_out_weight,
    agg_out_bias,
    norm_one_gain,
    norm_one_bias,
    qkv_weight,
    attn_out_weight,
    attn_out_bias,
    norm_two_gain,
    norm_two_bias,
    mlp_in_weight,
    mlp_in_bias,
    mlp_out_weight,
    mlp_out_bias,
    cotangent,
):
    rows = patches.shape[0]
    shard = D // 4
    order = Order()
    where = Where(order)
    spot = where.spot

    def half(a):
        span = a.shape[1] // 2
        return rows_from(a, where.half_column if span == D // 2 else where.wide_half_column, span, 1)

    def other_half(a):
        span = a.shape[1] // 2
        start = where.other_half_column if span == D // 2 else where.other_wide_half_column
        return rows_from(a, start, span, 1)

    singles = (
        agg_query,
        agg_out_bias,
        norm_one_gain,
        norm_one_bias,
        attn_out_bias,
        norm_two_gain,
        norm_two_bias,
        mlp_out_bias,
    )
    at_row = lax.broadcasted_iota(jnp.int32, (8, shard), 0)
    vectors = jnp.zeros((8, shard), bf16)
    for i, single in enumerate(singles):
        vectors = jnp.where(at_row == i, single[None, :], vectors)
    vectors = jnp.concatenate([vectors, mlp_in_bias.reshape(4, shard)])
    narrow_v = Narrow(vectors, order)
    narrow_a = Narrow(pieces_of([agg_out_weight], where.piece_row), order)
    narrow_b = Narrow(pieces_of([qkv_weight, attn_out_weight], where.piece_row), order)
    narrow_v.second_step()
    narrow_a.second_step()
    narrow_b.second_step()

    line = jnp.arange(COLS, dtype=jnp.int32)
    variable = jnp.where(line < PATCH_COLS, line // PIX, (line - PATCH_COLS) % VARS)
    used = line < PATCH_COLS + VARS
    same = ((variable[:, None] == variable[None, :]) & used[None, :]).astype(f32)
    picks = variable[:, None] == jnp.arange(VARS, dtype=jnp.int32)[None, :]
    chosen = jnp.sum(jnp.where(picks, var_ids[None, :], 0), axis=1)
    source = jnp.where(line < PATCH_COLS, chosen * PIX + line % PIX, chosen + PATCH_COLS)
    source = jnp.where(used, source, -1)
    chooser = (source[:, None] == line[None, :]).astype(bf16)
    embed_rows = jnp.concatenate(
        [embed_weight, var_embed, jnp.zeros((COLS - PATCH_COLS - VARS, shard), bf16)]
    )
    value_part = rows_from(value_weight, where.long_piece_row, 128, 1)
    table_part = lax.dot_general(
        value_part, embed_rows, (((0,), (1,)), ((), ())), preferred_element_type=f32
    )
    table_part = beside(table_part.astype(bf16))

    around = order_narrow(vectors, narrow_v.bundle(), spot)
    whole = [around[:, i].reshape(D) for i in range(8)]
    query_full = whole[0].astype(f32)
    agg_out_b, gain_one, bias_one, attn_out_b, gain_two, bias_two, mlp_out_b = [
        v.astype(f32) for v in whole[1:]
    ]
    mlp_in_b = around[:, 8:].reshape(4 * D).astype(f32)
    head_of = jnp.arange(D, dtype=jnp.int32) // HEAD_DIM
    heads_eye = (jnp.arange(HEADS, dtype=jnp.int32)[:, None] == head_of[None, :]).astype(f32)
    query_rows = (heads_eye * query_full[None, :]).astype(bf16)
    key_query_t = dot_nt(query_rows, key_weight).astype(bf16)
    keys_part = dot_nt(key_query_t, embed_rows) * scale_by
    packed = jnp.concatenate([table_part, beside(jnp.concatenate(split_two(keys_part)))])
    order.mark(packed)
    got_packed = [turn_narrow(packed, turn) for turn in (1, 2, 3)]

    same, chooser = order.hold(same, chooser)
    agg_out_b, gain_one, bias_one, attn_out_b, gain_two, bias_two, mlp_out_b, mlp_in_b = order.hold(
        agg_out_b, gain_one, bias_one, attn_out_b, gain_two, bias_two, mlp_out_b, mlp_in_b
    )
    piece_c = pieces_of([mlp_in_weight], where.piece_row)
    piece_d = pieces_of([mlp_out_weight], where.long_piece_row)
    order.mark(piece_c)
    order.mark(piece_d)

    full_patches = jnp.concatenate(
        [
            patches,
            jnp.ones((rows, VARS), bf16),
            jnp.zeros((rows, COLS - PATCH_COLS - VARS), bf16),
        ],
        axis=1,
    )
    pixels = lax.dot_general(
        chooser, full_patches, (((0,), (1,)), ((), ())), preferred_element_type=f32
    ).astype(bf16)
    seg_row, seg_col, pad_col = order.hold(segment_ids, segment_ids.T, pad_mask.T)
    pixels = order.hold(pixels)
    cot_half, cot_other = order.hold(half(cotangent), other_half(cotangent))
    cot_got = over_core(cot_other)

    got_packed = order.hold(*got_packed)
    total = packed.astype(f32)
    for part in got_packed:
        total = total + part.astype(f32)
    table_own = total[:32].astype(bf16)
    order.mark(table_own)
    keys_two = jnp.concatenate([total[32:, i * COLS : (i + 1) * COLS] for i in range(4)])
    keys_rows = (keys_two[:HEADS] + keys_two[HEADS:]).reshape(PAIRS, 2, COLS)
    keys_cols = keys_rows.transpose(0, 2, 1)
    spread_a = Spread(narrow_a.bundle(table_own[None]), order)
    spread_b = Spread(narrow_b.bundle(), order)
    narrow_c = Narrow(order.hold(piece_c), order)
    spread_a.near_step()
    spread_a.corner_step()
    spread_b.near_step()
    spread_a.last_step()
    parts_a = spread_a.parts()
    table, table_t = arrange(parts_a, spot)
    (agg_out_w,) = assemble([agg_out_weight], parts_a, spot)
    order.mark(table_t)
    order.mark(agg_out_w)
    narrow_c.second_step()
    spread_b.corner_step()
    merged = variable_forward(pixels, same, keys_rows, order.hold(table_t))
    order.mark(merged)
    merged_there = over_core(merged)
    spread_b.last_step()
    patch_state = dot(merged, agg_out_w) + agg_out_b
    unit_one, inverse_one = normalise(patch_state)
    normed = (unit_one * gain_one + bias_one).astype(bf16)
    order.mark(normed)
    merged_there = order.hold(merged_there)
    spread_c = Spread(narrow_c.bundle(), order)
    narrow_d = Narrow(order.hold(piece_d), order)
    spread_c.near_step()
    normed_there = over_core(normed)
    qkv_w, attn_out_w = assemble([qkv_weight, attn_out_weight], spread_b.parts(), spot)
    project = dot(order.hold(normed), qkv_w).astype(bf16)
    order.mark(project)
    narrow_d.second_step()
    normed_there = order.hold(normed_there)
    attended, logs = attention(order.hold(project), seg_row, seg_col, pad_col)
    order.mark(attended)
    spread_c.corner_step()
    spread_d = Spread(narrow_d.bundle(), order)
    attended_there = over_core(attended)
    residual = patch_state + dot(order.hold(attended), attn_out_w) + attn_out_b
    unit_two, inverse_two = normalise(residual)
    normed_two = (unit_two * gain_two + bias_two).astype(bf16)
    order.mark(normed_two)
    ke_part = lax.dot_general(
        key_weight, embed_rows, (((0,), (1,)), ((), ())), preferred_element_type=f32
    ).astype(bf16)
    order.mark(ke_part)
    order.mark(keys_cols)
    spread_d.near_step()
    spread_c.last_step()
    normed_two_there = over_core(normed_two)
    (mlp_in_w,) = assemble([mlp_in_weight], spread_c.parts(), spot)
    attended_there, normed_two_there = order.hold(attended_there, normed_two_there)
    hidden, slope = mlp_in(order.hold(normed_two), mlp_in_w, mlp_in_b)
    order.mark(hidden)
    hidden_there = over_core(hidden)
    spread_d.corner_step()

    def grad_of(own, there, own_half, got):
        return (dot_tn(own, own_half) + dot_tn(there, got)).astype(bf16)

    def blocks(a):
        return a.reshape(4, 2, 2, a.shape[0] // 16, a.shape[1])

    cot_float = cotangent.astype(f32)
    spread_d.last_step()
    (mlp_out_w,) = assemble([mlp_out_weight], spread_d.parts(), spot)
    pre_half, pre_other, normed_two_grad, pre_sums = mlp_back(
        where.core_alone, order.hold(cotangent), mlp_out_w, mlp_in_w, slope
    )
    order.mark(pre_other)
    grad_d = blocks(grad_of(*order.hold(hidden, hidden_there), cot_half, cot_got))
    order.mark(grad_d)
    reduce_d = Reduce(grad_d, where, order)
    pre_got = over_core(pre_other)
    ke_part = order.hold(ke_part).reshape(2, 2, shard, COLS)
    ke_kept, ke_got = take(ke_part, where.low, 1), swap_narrow(take(ke_part, where.other_low, 1), 1)
    residual_grad = cot_float + normalise_back(
        order.hold(normed_two_grad), gain_two, unit_two, inverse_two
    )
    branch_grad = residual_grad.astype(bf16)
    order.mark(branch_grad)
    branch_got = over_core(other_half(branch_grad))
    grad_c = grad_of(normed_two, normed_two_there, *order.hold(pre_half, pre_got))
    order.mark(grad_c)
    grad_c = jnp.concatenate(
        [grad_c, grad_of(attended, attended_there, *order.hold(half(branch_grad), branch_got))],
        axis=1,
    )
    order.mark(grad_c)
    reduce_c = Reduce(blocks(grad_c), where, order)
    attended_grad = dot_nt(order.hold(branch_grad), attn_out_w).astype(bf16)
    order.mark(attended_grad)
    reduce_d.step()
    ke_two = add_two(ke_kept, order.hold(ke_got))
    order.mark(ke_two)
    ke_got = swap_narrow(take(ke_two, where.other_high, 0), 2)
    attended_grad = order.hold(attended_grad)
    project_grad = attention_back(project, attended_grad, logs, seg_row, seg_col, pad_col)
    project_other = other_half(project_grad)
    order.mark(project_other)
    project_got = over_core(project_other)
    reduce_d.step()
    late = order.hold(normed_two_grad)
    sums_two = [jnp.sum(late * unit_two, axis=0), jnp.sum(late, axis=0)]
    order.mark(sums_two[0])
    order.mark(sums_two[1])
    reduce_c.step()
    ke_own = add_two(take(ke_two, where.high, 0), order.hold(ke_got))
    order.mark(ke_own)
    grad_b = grad_of(normed, normed_there, *order.hold(half(project_grad), project_got))
    order.mark(grad_b)
    reduce_b = Reduce(blocks(grad_b), where, order)
    normed_grad = dot_nt(order.hold(project_grad), qkv_w)
    state_grad = residual_grad + normalise_back(normed_grad, gain_one, unit_one, inverse_one)
    state_grad = state_grad.astype(bf16)
    order.mark(state_grad)
    state_got = over_core(other_half(state_grad))
    reduce_d.step()
    merged_grad = dot_nt(order.hold(state_grad), agg_out_w).astype(bf16)
    order.mark(merged_grad)
    reduce_c.step()
    merged_grad = order.hold(merged_grad)
    cross, zed, pixel_grad = variable_back(pixels, same, keys_rows, keys_cols, table, merged_grad)
    order.mark(cross)
    reduce_d.step()
    spread_d = Spread(reduce_d.total, order)
    reduce_c.step()
    reduce_b.step()
    grad_a = grad_of(merged, merged_there, *order.hold(half(state_grad), state_got))
    order.mark(grad_a)
    zed_parts = split_two(zed)
    column_sums = [
        jnp.sum(state_grad.astype(f32), axis=0),
        jnp.sum(normed_grad * unit_one, axis=0),
        jnp.sum(normed_grad, axis=0),
        jnp.sum(branch_grad.astype(f32), axis=0),
        *sums_two,
        jnp.sum(cot_float, axis=0),
        pre_sums.reshape(-1),
    ]
    sums = jnp.concatenate([v.astype(bf16) for v in column_sums]).reshape(-1, 2 * COLS)
    filler = jnp.zeros((16 * (SUB - 1) - sums.shape[0], 2 * COLS), bf16)
    small = jnp.concatenate([jnp.concatenate(zed_parts, axis=1), sums, filler])
    shared = jnp.concatenate(
        [cross.reshape(SUB, HEAD_DIM, 2 * COLS), small.reshape(SUB, 16, 2 * COLS)], axis=1
    )
    shared = shared.reshape(2, 2, 2, 80, 2 * COLS)
    order.mark(shared)
    shared_got = over_core(take(shared, where.other_core, 0))
    grad_a = grad_a.reshape(4, 2, 2, shard // 4, D // 2).transpose(1, 2, 0, 3, 4)
    grad_a = grad_a.reshape(2, 2, shard, D // 2)
    shared = add_two(take(shared, where.core, 0), order.hold(shared_got))
    grad_a = jnp.concatenate([grad_a, shared], axis=2)
    order.mark(grad_a)
    reduce_a = ReduceShared(grad_a[None], where, order)
    reduce_b.step()
    reduce_c.step()
    spread_c = Spread(reduce_c.total, order)
    reduce_a.step()
    spread_d.near_step()
    reduce_b.step()
    reduce_a.step()
    spread_d.corner_step()
    result = (residual + dot(order.hold(hidden), mlp_out_w) + mlp_out_b).astype(bf16)
    order.mark(result)
    reduce_b.step()
    spread_b = Spread(reduce_b.total, order)
    spread_c.near_step()
    reduce_a.step()
    spread_d.last_step()
    spread_b.near_step()
    patches_grad = lax.dot_general(
        order.hold(pixel_grad),
        chooser.astype(f32),
        (((0,), (1,)), ((), ())),
        precision=lax.Precision.HIGHEST,
        preferred_element_type=f32,
    )[:, :PATCH_COLS]
    order.mark(patches_grad)
    reduce_a.step()
    spread_a = Spread(reduce_a.total, order)
    spread_c.corner_step()
    spread_a.near_step()
    spread_b.corner_step()
    (grad_mlp_out_w,) = place(spread_d.parts(), [(D, D)], spot)
    order.mark(grad_mlp_out_w)
    spread_c.last_step()
    spread_a.corner_step()
    spread_b.last_step()
    grad_mlp_in_w, grad_attn_out_w = place(spread_c.parts(), [(shard, 4 * D), (shard, D)], spot)
    order.mark(grad_mlp_in_w)
    spread_a.last_step()
    (grad_qkv_w,) = place(spread_b.parts(), [(shard, 3 * D)], spot)
    order.mark(grad_qkv_w)
    grad_agg_out_w, cross, rest = place(spread_a.parts(), [(shard, D)], spot, shared=True)
    finished = finish(
        spot, cross, rest, value_weight, embed_rows.T, key_query_t.T, query_full, ke_own
    )
    grad_embed, grad_value_w, grad_key_w, grad_agg_query, grad_mlp_in_b = finished[:5]
    grad_agg_query, grad_mlp_in_b = grad_agg_query.reshape(shard), grad_mlp_in_b.reshape(D)
    own = lambda i: finished[5 + i].reshape(shard)

    return (
        result,
        patches_grad,
        grad_embed[:PATCH_COLS],
        grad_embed[PATCH_COLS : PATCH_COLS + VARS],
        grad_agg_query,
        grad_key_w,
        grad_value_w,
        grad_agg_out_w,
        own(0),
        own(1),
        own(2),
        grad_qkv_w,
        grad_attn_out_w,
        own(3),
        own(4),
        own(5),
        grad_mlp_in_w,
        grad_mlp_in_b,
        grad_mlp_out_w,
        own(6),
    )


def solution(mesh):
    rows, shard = P(("wide", "narrow"), None), P("narrow", None)
    wide_shard, vector = P(None, "narrow"), P("narrow")
    return jax.shard_map(
        per_device,
        mesh=mesh,
        in_specs=(
            rows,
            P(),
            rows,
            rows,
            wide_shard,
            wide_shard,
            vector,
            shard,
            shard,
            shard,
            vector,
            vector,
            vector,
            shard,
            shard,
            vector,
            vector,
            vector,
            shard,
            vector,
            shard,
            vector,
            rows,
        ),
        out_specs=(
            rows,
            rows,
            wide_shard,
            wide_shard,
            vector,
            shard,
            shard,
            shard,
            vector,
            vector,
            vector,
            shard,
            shard,
            vector,
            vector,
            vector,
            shard,
            vector,
            shard,
            vector,
        ),
        check_vma=False,
    )
```
